32 devices in a mesh: res: 8 (over z, x), nbr: 4 (over y, core).
Axes of the slice: x: 2, y: 2, z: 4, core: 2. Of those that a mesh axis runs over, the one named last changes fastest.
Arguments:
- nodes: bfloat16 [1536, 512], P('res'), may hold values from -6 to 6
- edges: bfloat16 [1536, 60, 192], P('res', 'nbr'), may hold values from -6 to 6
- neighbours: int32 [1536, 60], P('res', 'nbr'), may hold values from 0 to 1535, as said below
- residue_mask: int32 [1536], P('res'), may hold values from 0 to 1, as said below
- msg_w1: bfloat16 [1216, 512], replicated, may hold values from -0.15625 to 0.15625
- msg_b1: bfloat16 [512], replicated, may hold values from -1.5 to 1.5
- msg_w2: bfloat16 [512, 512], replicated, may hold values from -0.25 to 0.25
- msg_b2: bfloat16 [512], replicated, may hold values from -1.5 to 1.5
- msg_w3: bfloat16 [512, 512], replicated, may hold values from -0.5 to 0.5
- msg_b3: bfloat16 [512], replicated, may hold values from -1.5 to 1.5
- norm1_gain: bfloat16 [512], replicated, may hold values from 0.25 to 1.75
- norm1_bias: bfloat16 [512], replicated, may hold values from -1.5 to 1.5
- ffn_w1: bfloat16 [512, 2048], replicated, may hold values from -0.25 to 0.25
- ffn_b1: bfloat16 [2048], replicated, may hold values from -1.5 to 1.5
- ffn_w2: bfloat16 [2048, 512], replicated, may hold values from -0.125 to 0.125
- ffn_b2: bfloat16 [512], replicated, may hold values from -1.5 to 1.5
- norm2_gain: bfloat16 [512], replicated, may hold values from 0.25 to 1.75
- norm2_bias: bfloat16 [512], replicated, may hold values from -1.5 to 1.5
- edge_w1: bfloat16 [1216, 192], replicated, may hold values from -0.15625 to 0.15625
- edge_b1: bfloat16 [192], replicated, may hold values from -1.5 to 1.5
- edge_w2: bfloat16 [192, 192], replicated, may hold values from -0.4375 to 0.4375
- edge_b2: bfloat16 [192], replicated, may hold values from -1.5 to 1.5
- edge_w3: bfloat16 [192, 192], replicated, may hold values from -0.4375 to 0.4375
- edge_b3: bfloat16 [192], replicated, may hold values from -1.5 to 1.5
- norm3_gain: bfloat16 [192], replicated, may hold values from 0.25 to 1.75
- norm3_bias: bfloat16 [192], replicated, may hold values from -1.5 to 1.5
- node_cot: bfloat16 [1536, 512], P('res'), may hold values from -6 to 6
- edge_cot: bfloat16 [1536, 60, 192], P('res', 'nbr'), may hold values from -6 to 6
Outputs:
- nodes_out: bfloat16 [1536, 512], P('res')
- edges_out: bfloat16 [1536, 60, 192], P('res', 'nbr')
- nodes_grad: float32 [1536, 512], P('res')
- edges_grad: float32 [1536, 60, 192], P('res', 'nbr')
- msg_w1_grad: float32 [1216, 512], P('nbr')
- msg_b1_grad: float32 [512], P('nbr')
- msg_w2_grad: float32 [512, 512], P('nbr')
- msg_b2_grad: float32 [512], P('nbr')
- msg_w3_grad: float32 [512, 512], P('nbr')
- msg_b3_grad: float32 [512], P('nbr')
- norm1_gain_grad: float32 [512], P('nbr')
- norm1_bias_grad: float32 [512], P('nbr')
- ffn_w1_grad: float32 [512, 2048], P('nbr')
- ffn_b1_grad: float32 [2048], P('nbr')
- ffn_w2_grad: float32 [2048, 512], P('nbr')
- ffn_b2_grad: float32 [512], P('nbr')
- norm2_gain_grad: float32 [512], P('nbr')
- norm2_bias_grad: float32 [512], P('nbr')
- edge_w1_grad: float32 [1216, 192], P('nbr')
- edge_b1_grad: float32 [192], P('nbr')
- edge_w2_grad: float32 [192, 192], P('nbr')
- edge_b2_grad: float32 [192], P('nbr')
- edge_w3_grad: float32 [192, 192], P('nbr')
- edge_b3_grad: float32 [192], P('nbr')
- norm3_gain_grad: float32 [192], P('nbr')
- norm3_bias_grad: float32 [192], P('nbr')
The draws below stay inside these ranges and needn't reach their ends.
Inputs may be any that keep to these rules, and one draw needn't show every extreme that they name: `residue_mask`: within each block of 192 slots (one index of res) the real residues (1) come first and fill a quarter of the slots or more; some block is all real. `neighbours`: column 0 of each row names the slot itself. Every other entry names either a slot of the row's own block of 192 slots within 24 positions of it, or a real residue of any block. The rows of one block name at most 32 distinct slots of any other block, and in every draw some block names exactly 32 slots of some other block in column 1.
All inputs are finite; a program needn't handle non-finite values.
Results may differ from the reference program's by a relative error of at most 0.017.
Values may be sent and summed in bfloat16 or wider, within the bound.
No kernel may reach another device: no remote copies, remote signals or barrier semaphores. Data moves between devices by JAX's collectives and lax.ppermute only.
A program may use at most 192 MiB of HBM per device.

```python
import math
import jax
import jax.numpy as jnp
from jax import lax

D = 512
E = 192
FF = 2048
K = 60
NODE_DEV = 192
IN = 1216
NODES = 1536


def device_counts(key):
    devices = NODES // NODE_DEV
    least = max(NODE_DEV // 4, 1)
    counts = jax.random.randint(jax.random.fold_in(key, 11), (devices,), least, NODE_DEV + 1)
    fuller = jax.random.randint(jax.random.fold_in(key, 12), (), 0, devices)
    return jnp.where(jnp.arange(devices) == fuller, NODE_DEV, counts).astype(jnp.int32)


def draw_residue_mask(key, part):
    counts = device_counts(key)
    places = jnp.arange(NODE_DEV)
    return (places[None, :] < counts[:, None]).astype(jnp.int32).reshape(NODES)


def draw_neighbours(key, part):
    counts = device_counts(key)
    key = jax.random.fold_in(key, 5)
    devices = NODES // NODE_DEV
    far_most = min(32, NODE_DEV // 4)
    streams = jax.random.split(key, 6)
    rows_all = jnp.arange(NODES)
    home = rows_all // NODE_DEV
    place = rows_all % NODE_DEV
    owner = jax.random.randint(streams[0], (NODES, K), 0, devices)
    picks = jax.random.randint(streams[1], (NODES, K), 0, far_most)
    starts = jax.random.randint(streams[4], (devices, devices), 0, NODE_DEV)
    within = (starts[home[:, None], owner] + picks) % counts[owner]
    distant = owner * NODE_DEV + within
    offsets = jax.random.randint(streams[2], (NODES, K), -24, 25)
    block_start = (home * NODE_DEV)[:, None]
    nearby = jnp.clip(rows_all[:, None] + offsets, block_start, block_start + NODE_DEV - 1)
    choose = jax.random.randint(streams[3], (NODES, K), 0, 2)
    picked = jnp.where(choose == 0, nearby, distant)
    targets = (jnp.arange(devices) + 1 + jax.random.randint(streams[5], (devices,), 0, devices - 1)) % devices
    target_row = targets[home]
    forced = target_row * NODE_DEV + (starts[home, target_row] + place) % counts[target_row]
    picked = picked.at[:, 1].set(jnp.where(place < far_most, forced, picked[:, 1]))
    return picked.at[:, 0].set(rows_all).astype(jnp.int32)


def level_of(key, dims, cuts, low, largest):
    def one(position, blocks):
        draws = jax.random.uniform(jax.random.fold_in(jax.random.fold_in(key, 6), position), (blocks,), jnp.float32, low / len(cuts), largest / len(cuts))
        return jnp.repeat(jnp.exp(draws), dims[position] // blocks).reshape((-1,) + (1,) * (len(dims) - position - 1))

    loudness = one(*cuts[0])
    for cut in cuts[1:]:
        loudness = loudness * one(*cut)
    return loudness


def normal_values(rng, shape, scale, limit, cuts=(), held_as=jnp.bfloat16):
    result = scale * jax.random.normal(rng, shape, jnp.float32)
    if cuts:
        result = result * level_of(rng, shape, cuts, -0.22, 0.18)
    return jnp.clip(result, -limit, limit).astype(held_as)


def setup_inputs(seed: int = 0) -> dict:
    seeds = jax.random.split(jax.random.key(seed), 29)
    nodes = normal_values(seeds[0], (NODES, D), 1.0, 6.0, ((0, 8),))
    edges = normal_values(seeds[1], (NODES, K, E), 1.0, 6.0, ((0, 8), (1, 4)))
    neighbours = draw_neighbours(jax.random.fold_in(seeds[28], 71), 0)
    residue_mask = draw_residue_mask(jax.random.fold_in(seeds[28], 71), 0)
    msg_w1 = normal_values(seeds[4], (IN, D), IN ** -0.5, 0.15625)
    msg_b1 = normal_values(seeds[5], (D,), 0.3, 1.5)
    msg_w2 = normal_values(seeds[6], (D, D), D ** -0.5, 0.25)
    msg_b2 = normal_values(seeds[7], (D,), 0.3, 1.5)
    msg_w3 = normal_values(seeds[8], (D, D), (D // 4) ** -0.5, 0.5)
    msg_b3 = normal_values(seeds[9], (D,), 0.3, 1.5)
    norm1_gain = jnp.clip(1.0 + 0.15 * jax.random.normal(seeds[10], (D,), jnp.float32), 0.25, 1.75).astype(jnp.bfloat16)
    norm1_bias = normal_values(seeds[11], (D,), 0.3, 1.5)
    ffn_w1 = normal_values(seeds[12], (D, FF), D ** -0.5, 0.25)
    ffn_b1 = normal_values(seeds[13], (FF,), 0.3, 1.5)
    ffn_w2 = normal_values(seeds[14], (FF, D), FF ** -0.5, 0.125)
    ffn_b2 = normal_values(seeds[15], (D,), 0.3, 1.5)
    norm2_gain = jnp.clip(1.0 + 0.15 * jax.random.normal(seeds[16], (D,), jnp.float32), 0.25, 1.75).astype(jnp.bfloat16)
    norm2_bias = normal_values(seeds[17], (D,), 0.3, 1.5)
    edge_w1 = normal_values(seeds[18], (IN, E), IN ** -0.5, 0.15625)
    edge_b1 = normal_values(seeds[19], (E,), 0.3, 1.5)
    edge_w2 = normal_values(seeds[20], (E, E), E ** -0.5, 0.4375)
    edge_b2 = normal_values(seeds[21], (E,), 0.3, 1.5)
    edge_w3 = normal_values(seeds[22], (E, E), E ** -0.5, 0.4375)
    edge_b3 = normal_values(seeds[23], (E,), 0.3, 1.5)
    norm3_gain = jnp.clip(1.0 + 0.15 * jax.random.normal(seeds[24], (E,), jnp.float32), 0.25, 1.75).astype(jnp.bfloat16)
    norm3_bias = normal_values(seeds[25], (E,), 0.3, 1.5)
    node_cot = normal_values(seeds[26], (NODES, D), 1.0, 6.0, ((0, 8),))
    edge_cot = normal_values(seeds[27], (NODES, K, E), 1.0, 6.0, ((0, 8), (1, 4)))
    return dict(nodes=nodes, edges=edges, neighbours=neighbours, residue_mask=residue_mask, msg_w1=msg_w1, msg_b1=msg_b1, msg_w2=msg_w2, msg_b2=msg_b2, msg_w3=msg_w3, msg_b3=msg_b3, norm1_gain=norm1_gain, norm1_bias=norm1_bias, ffn_w1=ffn_w1, ffn_b1=ffn_b1, ffn_w2=ffn_w2, ffn_b2=ffn_b2, norm2_gain=norm2_gain, norm2_bias=norm2_bias, edge_w1=edge_w1, edge_b1=edge_b1, edge_w2=edge_w2, edge_b2=edge_b2, edge_w3=edge_w3, edge_b3=edge_b3, norm3_gain=norm3_gain, norm3_bias=norm3_bias, node_cot=node_cot, edge_cot=edge_cot)


precise = lax.Precision.HIGHEST

@jax.custom_vjp
def low(v):
    return lax.optimization_barrier(v.astype(jnp.bfloat16)).astype(jnp.float32)

@jax.custom_vjp
def low_back(v):
    return v

def low_keep(v):
    return (low(v), None)

def low_pass(kept, grad):
    return (grad,)

def back_keep(v):
    return (v, None)

def back_low(kept, grad):
    return (low(grad),)
low.defvjp(low_keep, low_pass)
low_back.defvjp(back_keep, back_low)

def product(former, latter):
    return jnp.dot(former, latter, precision=precise)

def layer_norm(values, scale_row, offset_row):
    centre = lax.optimization_barrier(jnp.mean(values, axis=-1, keepdims=True))
    centred = values - centre
    spread = lax.optimization_barrier(jnp.mean(centred * centred, axis=-1, keepdims=True))
    return centred * lax.rsqrt(spread + 1e-05) * scale_row + offset_row

def reference(nodes, edges, neighbours, residue_mask, msg_w1, msg_b1, msg_w2, msg_b2, msg_w3, msg_b3, norm1_gain, norm1_bias, ffn_w1, ffn_b1, ffn_w2, ffn_b2, norm2_gain, norm2_bias, edge_w1, edge_b1, edge_w2, edge_b2, edge_w3, edge_b3, norm3_gain, norm3_bias, node_cot, edge_cot):
    block = math.gcd(NODES, 512)
    blocks = NODES // block
    present = residue_mask.astype(jnp.float32)
    edge_mask = present[:, None] * jnp.take(present, neighbours, axis=0)
    counts = jnp.maximum(lax.optimization_barrier(jnp.sum(edge_mask, axis=1)), 1.0)
    index_blocks = neighbours.reshape(blocks, block, K)
    mask_blocks = edge_mask.reshape(blocks, block, K)
    params = tuple((weight.astype(jnp.float32) for weight in (msg_w1, msg_b1, msg_w2, msg_b2, msg_w3, msg_b3, norm1_gain, norm1_bias, ffn_w1, ffn_b1, ffn_w2, ffn_b2, norm2_gain, norm2_bias, edge_w1, edge_b1, edge_w2, edge_b2, edge_w3, edge_b3, norm3_gain, norm3_bias)))

    def forward(state, edge_state, weights):
        m_w1, m_b1, m_w2, m_b2, m_w3, m_b3, n1_gain, n1_bias, f_w1, f_b1, f_w2, f_b2, n2_gain, n2_bias, e_w1, e_b1, e_w2, e_b2, e_w3, e_b3, n3_gain, n3_bias = weights

        def message_block(pieces):
            own_rows, edge_rows, index_rows, mask_rows = pieces
            near_rows = jnp.take(state, index_rows, axis=0)
            first = low_back(product(own_rows, m_w1[:D])[:, None, :] + product(near_rows, m_w1[D:2 * D]) + product(edge_rows, m_w1[2 * D:]) + m_b1)
            second = low_back(product(low(jax.nn.gelu(first)), m_w2) + m_b2)
            third = low_back(product(low(jax.nn.gelu(second)), m_w3) + m_b3)
            return lax.optimization_barrier(jnp.sum(mask_rows[:, :, None] * third, axis=1))
        summed = lax.map(jax.checkpoint(message_block), (state.reshape(blocks, block, D), edge_state.reshape(blocks, block, K, E), index_blocks, mask_blocks)).reshape(NODES, D)
        mixed_sum = state + summed / counts[:, None]
        first_norm = layer_norm(mixed_sum, n1_gain, n1_bias)
        hidden = low_back(product(low(first_norm), f_w1) + f_b1)
        branch = low_back(product(low(jax.nn.gelu(hidden)), f_w2) + f_b2)
        updated = present[:, None] * layer_norm(first_norm + branch, n2_gain, n2_bias)
        sent_low = low(updated)

        def edge_block(pieces):
            own_rows, edge_rows, index_rows, mask_rows = pieces
            near_rows = jnp.take(sent_low, index_rows, axis=0)
            first = low_back(product(own_rows, e_w1[:D])[:, None, :] + product(near_rows, e_w1[D:2 * D]) + product(edge_rows, e_w1[2 * D:]) + e_b1)
            second = low_back(product(low(jax.nn.gelu(first)), e_w2) + e_b2)
            third = low_back(product(low(jax.nn.gelu(second)), e_w3) + e_b3)
            return mask_rows[:, :, None] * layer_norm(edge_rows + third, n3_gain, n3_bias)
        edge_out = lax.map(jax.checkpoint(edge_block), (sent_low.reshape(blocks, block, D), edge_state.reshape(blocks, block, K, E), index_blocks, mask_blocks)).reshape(NODES, K, E)
        return (updated, edge_out)
    state = nodes.astype(jnp.float32)
    edge_state = edges.astype(jnp.float32)
    outputs, pullback = jax.vjp(forward, state, edge_state, params)
    node_grad, edge_grad, grads = pullback((node_cot.astype(jnp.float32), edge_cot.astype(jnp.float32)))
    return (outputs[0].astype(jnp.bfloat16), outputs[1].astype(jnp.bfloat16), node_grad, edge_grad, grads[0], grads[1], grads[2], grads[3], grads[4], grads[5], grads[6], grads[7], grads[8], grads[9], grads[10], grads[11], grads[12], grads[13], grads[14], grads[15], grads[16], grads[17], grads[18], grads[19], grads[20], grads[21])
```

```python
import functools

import jax
import jax.numpy as jnp
from jax import lax
from jax.experimental import pallas as pl
from jax.experimental.pallas import tpu as pltpu
from jax.sharding import PartitionSpec as P

D = 512
E = 192
FF = 2048
FAR = 32
SLOT = 16
VMEM = 56 * 1024 * 1024

bf16 = jnp.bfloat16
f32 = jnp.float32


def mm(a, b):
    return jnp.dot(a, b, preferred_element_type=f32)


def mm_tn(a, b):
    return lax.dot_general(a, b, (((0,), (0,)), ((), ())), preferred_element_type=f32)


def mm_nt(a, b):
    return lax.dot_general(a, b, (((1,), (1,)), ((), ())), preferred_element_type=f32)


def gelu_pair(v):
    c0 = 0.7978845608028654
    c1 = 0.044715 * c0
    square = v * v
    t = jnp.tanh(v * (c0 + c1 * square))
    half = 0.5 + 0.5 * t
    act = v * half
    return act, half + act * (1.0 - t) * (c0 + (3.0 * c1) * square)


def norm_forward(values):
    centred = values - jnp.mean(values, axis=-1, keepdims=True)
    inverse = lax.rsqrt(jnp.mean(centred * centred, axis=-1, keepdims=True) + 1e-05)
    return centred * inverse, inverse


def norm_backward(upstream, normed, inverse, gain):
    scaled = upstream * gain
    first = jnp.mean(scaled, axis=-1, keepdims=True)
    second = jnp.mean(scaled * normed, axis=-1, keepdims=True)
    return inverse * (scaled - first - normed * second)


def column_sum(values):
    return jnp.sum(values, axis=0, keepdims=True)


def iota(shape, dim):
    return lax.broadcasted_iota(jnp.int32, shape, dim)


def present_column(mask_ref, rows):
    real = jnp.sum(mask_ref[...].astype(f32), axis=1, keepdims=True)
    return (iota((rows, 1), 0).astype(f32) < real).astype(f32)


def pick_matrix(want_ref, rows):
    want = want_ref[...][:, :1].astype(f32)
    return (want == iota((want.shape[0], rows), 1).astype(f32)).astype(bf16)


def one_hot(column, width):
    return (column == iota((column.shape[0], width), 1)).astype(bf16)


def padded(ref, pad):
    rows, kn, c = ref.shape
    pad[:, kn:, :] = jnp.zeros((rows, SLOT - kn, c), pad.dtype)
    pad[:, :kn, :] = ref[...]
    return pad[...].reshape(rows * SLOT, c)


def spread(rows, values):
    n, c = rows.shape
    return (values.reshape(n, SLOT, c) + rows[:, None, :]).reshape(n * SLOT, c)


def gathered(values):
    n, c = values.shape
    return jnp.sum(values.reshape(n // SLOT, SLOT, c), axis=1)


def index_kernel(blocks, me_ref, near_ref, mask_ref, col_ref, want_ref, count_ref):
    rows, kn = near_ref.shape
    total = rows * SLOT
    me = me_ref[0].astype(f32)
    lanes = max(128, blocks)
    wide = jnp.broadcast_to(near_ref[...].astype(f32)[:, None, :], (rows, SLOT, kn)).reshape(total, kn)
    place = iota((total, 1), 0) & (SLOT - 1)
    index = jnp.sum(jnp.where(iota((total, kn), 1) == place, wide, 0.0), axis=1, keepdims=True)
    valid = place < kn
    block = jnp.floor((index + 0.5) * (1.0 / rows))
    slot = index - block * rows
    local = block == me
    far = jnp.logical_and(valid, jnp.logical_not(local))
    hot_slot = (slot == iota((total, rows), 1).astype(f32)).astype(bf16)
    block_key = jnp.where(far, block, -1.0)
    hot_block = (block_key == iota((total, lanes), 1).astype(f32)).astype(bf16)
    flags = (mm_tn(hot_block, hot_slot) > 0.0).astype(f32)
    before = (iota((rows, rows), 0) < iota((rows, rows), 1)).astype(bf16)
    rank = mm(flags.astype(bf16), before)
    edge_rank = jnp.sum(mm(hot_block, rank.astype(bf16)) * hot_slot.astype(f32), axis=1, keepdims=True)
    real = jnp.sum(mask_ref[...].astype(f32), axis=1, keepdims=True)
    own_place = (iota((total, 1), 0) // SLOT).astype(f32)
    named = jnp.logical_or(jnp.logical_not(local), slot < real)
    kept = jnp.logical_and(jnp.logical_and(valid, named), own_place < real)
    column = jnp.where(local, blocks * FAR + slot, block * FAR + edge_rank)
    column = jnp.where(kept, column, -1.0)
    col_ref[...] = column.astype(jnp.int32)
    key = jnp.where(flags > 0.0, rank, -1.0)[:blocks]
    key = jnp.broadcast_to(key[:, None, :], (blocks, FAR, rows)).reshape(blocks * FAR, rows)
    level = (iota((blocks * FAR, 1), 0) & (FAR - 1)).astype(f32)
    hit = (key == level).astype(f32)
    place_row = iota((blocks * FAR, rows), 1).astype(f32)
    want = jnp.sum(hit * place_row, axis=1, keepdims=True)
    found = jnp.sum(hit, axis=1, keepdims=True)
    want = jnp.where(found > 0.0, want, 255.0)
    want_ref[...] = jnp.broadcast_to(want, want_ref.shape).astype(bf16)
    counts = jnp.sum(kept.astype(f32).reshape(rows, SLOT, 1), axis=1)
    count_ref[...] = jnp.broadcast_to(counts, count_ref.shape).astype(bf16)


def message_forward_kernel(
    col_ref, edges_ref, nodes_ref, far_ref, w1_ref, w2_ref, small_ref,
    act1_ref, d1_ref, d2_ref, sum_ref, table, own, pad,
):
    step = pl.program_id(0)
    rows = edges_ref.shape[0]
    n_far = far_ref.shape[0]
    width = table.shape[0]

    @pl.when(step == 0)
    def _():
        weight = w1_ref[D : 2 * D, :]
        table[:n_far] = mm(far_ref[...], weight).astype(bf16)
        table[n_far:] = mm(nodes_ref[...], weight).astype(bf16)
        own[...] = mm(nodes_ref[...], w1_ref[:D, :]) + small_ref[0:1, :]

    edge = padded(edges_ref, pad)
    column = col_ref[...]
    pre1 = mm(one_hot(column, width), table[...]) + mm(edge, w1_ref[2 * D :, :])
    pre1 = spread(own[pl.ds(step * rows, rows), :], pre1)
    act, slope = gelu_pair(pre1)
    act1 = act.astype(bf16)
    act1_ref[...] = act1
    d1_ref[...] = slope.astype(bf16)
    act, slope = gelu_pair(mm(act1, w2_ref[...]) + small_ref[1:2, :])
    weight = (column >= 0).astype(f32)
    d2_ref[...] = (slope * weight).astype(bf16)
    sum_ref[...] = gathered(act.astype(bf16).astype(f32) * weight).astype(bf16)


def node_forward_kernel(
    sum_a, sum_b, count_a, count_b, nodes_ref, mask_ref, want_ref, w3_ref, f1_ref, f2_ref, small_ref, small_ff_ref,
    total_ref, low_ref, normed1_ref, inv1_ref, hid_ref, slope_ref, normed2_ref, inv2_ref, sent_ref, send_ref,
):
    rows = nodes_ref.shape[0]
    present = present_column(mask_ref, rows)
    count = count_a[...].astype(f32) + count_b[...].astype(f32)
    count = count[:, :1]
    total = sum_a[...].astype(f32) + sum_b[...].astype(f32)
    high = total.astype(bf16)
    total_ref[...] = high
    rest = (total - high.astype(f32)).astype(bf16)
    summed = mm(high, w3_ref[...]) + mm(rest, w3_ref[...]) + count * small_ref[2:3, :]
    mixed = nodes_ref[...].astype(f32) + summed / jnp.maximum(count, 1.0)
    normed, inverse = norm_forward(mixed)
    normed1_ref[...] = normed
    inv1_ref[...] = inverse
    first = normed * small_ref[3:4, :] + small_ref[4:5, :]
    low = first.astype(bf16)
    low_ref[...] = low
    act, slope = gelu_pair(mm(low, f1_ref[...]) + small_ff_ref[...])
    act = act.astype(bf16)
    hid_ref[...] = act
    slope_ref[...] = slope.astype(bf16)
    branch = mm(act, f2_ref[...]) + small_ref[5:6, :]
    normed, inverse = norm_forward(first + branch)
    normed2_ref[...] = normed
    inv2_ref[...] = inverse
    sent = (present * (normed * small_ref[6:7, :] + small_ref[7:8, :])).astype(bf16)
    sent_ref[...] = sent
    send_ref[...] = mm(pick_matrix(want_ref, rows), sent).astype(bf16)


def edge_kernel(
    order, col_ref, edges_ref, cot_ref, sent_ref, far_ref, w1_ref, w2_ref, w3_ref, small_ref,
    out_ref, base_ref, own_ref, far_grad_ref, local_grad_ref, packed_ref,
    table, own, pad, pad2, sums, w1_acc, w2_acc, w3_acc, bias_acc, own_acc,
):
    step = pl.program_id(0)
    last = pl.num_programs(0) - 1
    rows, kn, _ = edges_ref.shape
    n_far = far_ref.shape[0]
    width = table.shape[0]

    @pl.when(step == 0)
    def _():
        weight = w1_ref[D : 2 * D, :]
        table[:n_far] = mm(far_ref[...], weight).astype(bf16)
        table[n_far:] = mm(sent_ref[...], weight).astype(bf16)
        own[...] = mm(sent_ref[...], w1_ref[:D, :]) + small_ref[0:1, :]
        for acc in (sums, w1_acc, w2_acc, w3_acc, bias_acc):
            acc[...] = jnp.zeros_like(acc)

    edge = padded(edges_ref, pad)
    cot = padded(cot_ref, pad2)
    column = col_ref[...]
    hot = one_hot(column, width)
    pre1 = mm(hot, table[...]) + mm(edge, w1_ref[2 * D :, :])
    pre1 = spread(own[pl.ds(step * rows, rows), :], pre1)
    act, slope1 = gelu_pair(pre1)
    act1 = act.astype(bf16)
    act, slope2 = gelu_pair(mm(act1, w2_ref[...]) + small_ref[1:2, :])
    act2 = act.astype(bf16)
    branch = mm(act2, w3_ref[...]) + small_ref[2:3, :]
    weight = (column >= 0).astype(f32)
    normed, inverse = norm_forward(edge.astype(f32) + branch)
    gain = small_ref[3:4, :]
    out = weight * (normed * gain + small_ref[4:5, :])
    out_ref[...] = out.astype(bf16).reshape(rows, SLOT, E)[:, :kn, :]
    up = weight * cot.astype(f32)
    grad = norm_backward(up, normed, inverse, gain)
    low3 = grad.astype(bf16)
    w3_acc[...] += mm_tn(act2, low3)
    low2 = (slope2 * mm_nt(low3, w3_ref[...])).astype(bf16)
    w2_acc[...] += mm_tn(act1, low2)
    low1 = (slope1 * mm_nt(low2, w2_ref[...])).astype(bf16)
    w1_acc[...] += mm_tn(edge, low1)
    sums[...] += mm_tn(hot, low1)
    base_ref[...] = grad + mm_nt(low1, w1_ref[2 * D :, :])
    own_sum = gathered(low1.astype(f32))
    own_ref[...] = own_sum.astype(bf16)
    own_acc[pl.ds(step * rows, rows), :] = own_sum
    row = iota((16, 1), 0)
    bias_acc[...] += (
        jnp.where(row == 0, column_sum(own_sum), 0.0)
        + jnp.where(row == 1, column_sum(low2.astype(f32)), 0.0)
        + jnp.where(row == 2, column_sum(low3.astype(f32)), 0.0)
        + jnp.where(row == 3, column_sum(up * normed), 0.0)
        + jnp.where(row == 4, column_sum(up), 0.0)
    )

    @pl.when(step == last)
    def _():
        total = sums[...]
        far_grad_ref[...] = total[:n_far].astype(bf16)
        local_grad_ref[...] = total[n_far:].astype(bf16)
        sent = sent_ref[...]
        parts = len(order)
        first = (2 * D + E) // parts
        second = E // parts
        whole = jnp.concatenate(
            [
                mm_tn(sent, own_acc[...].astype(bf16)),
                mm_tn(far_ref[...], total[:n_far].astype(bf16)) + mm_tn(sent, total[n_far:].astype(bf16)),
                w1_acc[...],
            ],
            axis=0,
        ).astype(bf16)
        second_w = w2_acc[...].astype(bf16)
        third_w = w3_acc[...].astype(bf16)
        bias = bias_acc[...].astype(bf16)
        for q, n in enumerate(order):
            packed_ref[q, :first, :] = whole[n * first : (n + 1) * first]
            packed_ref[q, first : first + second, :] = second_w[n * second : (n + 1) * second]
            packed_ref[q, first + second : first + 2 * second, :] = third_w[n * second : (n + 1) * second]
            packed_ref[q, first + 2 * second :, :] = bias


def returned_kernel(own_ref, local_ref, back_ref, want_ref, out_ref):
    rows = local_ref.shape[0]
    near = local_ref[...].astype(f32) + mm_tn(pick_matrix(want_ref, rows), back_ref[...])
    out_ref[...] = jnp.concatenate([own_ref[...], near.astype(bf16)], axis=1)


def returned_last_kernel(own_ref, local_ref, back_ref, want_ref, w1_ref, out_ref):
    rows = local_ref.shape[0]
    near = local_ref[...].astype(f32) + mm_tn(pick_matrix(want_ref, rows), back_ref[...])
    grad = mm_nt(own_ref[...], w1_ref[:D, :]) + mm_nt(near.astype(bf16), w1_ref[D : 2 * D, :])
    out_ref[...] = grad.astype(bf16)


def node_backward_kernel(
    parts, place_ref, back_a, back_b, count_a, count_b, cot_ref, mask_ref, total_ref, low_ref, normed1_ref, inv1_ref,
    hid_ref, slope_ref, normed2_ref, inv2_ref, ew1_ref, w3_ref, f1_ref, f2_ref, small_ref, edge_part_ref,
    mixed_ref, up_ref, bias_ref, packed_ref, hid_grad,
):
    rows = cot_ref.shape[0]
    place = place_ref[0]
    present = present_column(mask_ref, rows)
    count = (count_a[...].astype(f32) + count_b[...].astype(f32))[:, :1]
    back = (back_a[...].astype(f32) + back_b[...].astype(f32)).astype(bf16)
    node_back = mm_nt(back[:, :E], ew1_ref[:D, :]) + mm_nt(back[:, E:], ew1_ref[D : 2 * D, :])
    up = present * (cot_ref[...].astype(f32) + node_back)
    normed2 = normed2_ref[...]
    sum_grad = norm_backward(up, normed2, inv2_ref[...], small_ref[6:7, :])
    branch_grad = sum_grad.astype(bf16)
    hidden_grad = (slope_ref[...].astype(f32) * mm_nt(branch_grad, f2_ref[...])).astype(bf16)
    first_grad = sum_grad + mm_nt(hidden_grad, f1_ref[...])
    normed1 = normed1_ref[...]
    mixed_grad = norm_backward(first_grad, normed1, inv1_ref[...], small_ref[3:4, :])
    mixed_ref[...] = mixed_grad
    message_grad = (mixed_grad / jnp.maximum(count, 1.0)).astype(bf16)
    up_ref[...] = mm_nt(message_grad, w3_ref[...])
    row = iota((16, 1), 0)
    hidden_sum = column_sum(hidden_grad.astype(f32))
    bias = (
        jnp.where(row == 2, column_sum(count * message_grad.astype(f32)), 0.0)
        + jnp.where(row == 3, column_sum(first_grad * normed1), 0.0)
        + jnp.where(row == 4, column_sum(first_grad), 0.0)
        + jnp.where(row == 5, column_sum(branch_grad.astype(f32)), 0.0)
        + jnp.where(row == 6, column_sum(up * normed2), 0.0)
        + jnp.where(row == 7, column_sum(up), 0.0)
    )
    for j in range(FF // D):
        bias = bias + jnp.where(row == 8 + j, hidden_sum[:, j * D : (j + 1) * D], 0.0)
    bias_ref[...] = bias * (1.0 / parts)
    wide, narrow = FF // parts, D // parts
    low = low_ref[:, pl.ds(pl.multiple_of(place * narrow, narrow), narrow)]
    for j in range(FF // D):
        packed_ref[j * narrow : (j + 1) * narrow, :] = mm_tn(low, hidden_grad[:, j * D : (j + 1) * D]).astype(bf16)
    hid = hid_ref[:, pl.ds(pl.multiple_of(place * wide, wide), wide)]
    packed_ref[D : D + wide, :] = mm_tn(hid, branch_grad).astype(bf16)
    total = total_ref[:, pl.ds(pl.multiple_of(place * narrow, narrow), narrow)]
    packed_ref[D + wide : D + wide + narrow, :] = mm_tn(total, message_grad).astype(bf16)
    at = D + wide + narrow
    half = edge_part_ref.shape[0] // 2
    packed_ref[at:, :] = jnp.zeros((packed_ref.shape[0] - at, D), bf16)
    packed_ref[at : at + half, :E] = edge_part_ref[:half, :]
    packed_ref[at : at + half, 256 : 256 + E] = edge_part_ref[half:, :]


def message_backward_kernel(
    order, col_ref, edges_ref, act1_ref, d1_ref, d2_ref, up_ref, base_ref, nodes_ref, far_ref, w1_ref, w2_ref, node_bias_ref,
    out_ref, own_ref, far_grad_ref, local_grad_ref, packed_ref,
    pad, sums, w1_acc, w2_acc, bias_acc, own_acc,
):
    step = pl.program_id(0)
    last = pl.num_programs(0) - 1
    rows, kn, _ = edges_ref.shape
    n_far = far_ref.shape[0]
    width = sums.shape[0]

    @pl.when(step == 0)
    def _():
        for acc in (sums, w1_acc, w2_acc):
            acc[...] = jnp.zeros_like(acc)
        bias_acc[...] = node_bias_ref[...]

    edge = padded(edges_ref, pad)
    hot = one_hot(col_ref[...], width)
    up = jnp.broadcast_to(up_ref[...][:, None, :], (rows, SLOT, D)).reshape(rows * SLOT, D)
    low2 = (d2_ref[...].astype(f32) * up).astype(bf16)
    w2_acc[...] += mm_tn(act1_ref[...], low2)
    low1 = (d1_ref[...].astype(f32) * mm_nt(low2, w2_ref[...])).astype(bf16)
    w1_acc[...] += mm_tn(edge, low1)
    sums[...] += mm_tn(hot, low1)
    grad = base_ref[...] + mm_nt(low1, w1_ref[2 * D :, :])
    out_ref[...] = grad.reshape(rows, SLOT, E)[:, :kn, :]
    own_sum = gathered(low1.astype(f32))
    own_ref[...] = own_sum.astype(bf16)
    own_acc[pl.ds(step * rows, rows), :] = own_sum
    row = iota((16, 1), 0)
    bias_acc[...] += jnp.where(row == 0, column_sum(own_sum), 0.0) + jnp.where(
        row == 1, column_sum(low2.astype(f32)), 0.0
    )

    @pl.when(step == last)
    def _():
        total = sums[...]
        far_grad_ref[...] = total[:n_far].astype(bf16)
        local_grad_ref[...] = total[n_far:].astype(bf16)
        nodes = nodes_ref[...]
        parts = len(order)
        first = (2 * D + E) // parts
        second = D // parts
        whole = jnp.concatenate(
            [
                mm_tn(nodes, own_acc[...].astype(bf16)),
                mm_tn(far_ref[...], total[:n_far].astype(bf16)) + mm_tn(nodes, total[n_far:].astype(bf16)),
                w1_acc[...],
            ],
            axis=0,
        ).astype(bf16)
        second_w = w2_acc[...].astype(bf16)
        bias = bias_acc[...].astype(bf16)
        for q, n in enumerate(order):
            packed_ref[q, :first, :] = whole[n * first : (n + 1) * first]
            packed_ref[q, first : first + second, :] = second_w[n * second : (n + 1) * second]
            packed_ref[q, first + second : first + second + 16, :] = bias
            if packed_ref.shape[1] > first + second + 16:
                packed_ref[q, first + second + 16 :, :] = jnp.zeros(
                    (packed_ref.shape[1] - first - second - 16, D), bf16
                )


def swap(values, axis, bit):
    return lax.ppermute(values, axis, [(i, i ^ bit) for i in range(lax.axis_size(axis))])


def bits_of(axis):
    size, bit, out = lax.axis_size(axis), 1, []
    while bit < size:
        out.append(bit)
        bit *= 2
    return out


def add_low(a, b):
    return (a.astype(f32) + b.astype(f32)).astype(bf16)


def shared_sum(values, axis):
    bits = bits_of(axis)
    for bit in bits[:-1]:
        values = add_low(values, swap(values, axis, bit))
    return values, swap(values, axis, bits[-1])


def halves(values, axis, bit):
    half = values.shape[0] // 2
    side = (lax.axis_index(axis) // bit) & 1
    kept = lax.dynamic_slice_in_dim(values, side * half, half, 0)
    given = lax.dynamic_slice_in_dim(values, (1 - side) * half, half, 0)
    return kept, given


def scattered_sum(values, axis):
    for bit in bits_of(axis):
        kept, given = halves(values, axis, bit)
        values = add_low(kept, swap(given, axis, bit))
    return values


def assembled(values, axis):
    for bit in reversed(bits_of(axis)):
        other = swap(values, axis, bit)
        side = (lax.axis_index(axis) // bit) & 1
        rows = values.shape[0]
        whole = jnp.zeros((2 * rows,) + values.shape[1:], values.dtype)
        whole = lax.dynamic_update_slice_in_dim(whole, values, side * rows, 0)
        values = lax.dynamic_update_slice_in_dim(whole, other, (1 - side) * rows, 0)
    return values


def exchange(values, blocks):
    shaped = values.reshape((blocks, values.shape[0] // blocks) + values.shape[1:])
    return lax.all_to_all(shaped, "res", 0, 0, tiled=True).reshape(values.shape)


def call(kernel, outs, scratch=(), grid=None, in_specs=None, out_specs=None, cost=None):
    extra = {}
    if grid is not None:
        extra = dict(grid=grid, in_specs=in_specs, out_specs=out_specs)
    elif in_specs is not None:
        extra = dict(in_specs=in_specs)
    return pl.pallas_call(
        kernel,
        out_shape=outs,
        scratch_shapes=list(scratch),
        compiler_params=pltpu.CompilerParams(vmem_limit_bytes=VMEM),
        cost_estimate=cost,
        **extra,
    )


def shape(dims, dtype):
    return jax.ShapeDtypeStruct(dims, dtype)


def up_to(value, unit):
    return -(-value // unit) * unit


def on_device(
    nodes,
    edges,
    neighbours,
    residue_mask,
    msg_w1,
    msg_b1,
    msg_w2,
    msg_b2,
    msg_w3,
    msg_b3,
    norm1_gain,
    norm1_bias,
    ffn_w1,
    ffn_b1,
    ffn_w2,
    ffn_b2,
    norm2_gain,
    norm2_bias,
    edge_w1,
    edge_b1,
    edge_w2,
    edge_b2,
    edge_w3,
    edge_b3,
    norm3_gain,
    norm3_bias,
    node_cot,
    edge_cot,
):
    rows, kn = neighbours.shape
    blocks, parts = lax.axis_size("res"), lax.axis_size("nbr")
    total = rows * SLOT
    n_far = blocks * FAR
    width = n_far + rows
    tile = rows // 4
    grid = (rows // tile,)
    nbr_bits = bits_of("nbr")
    order = tuple(
        sum(bit for i, bit in enumerate(nbr_bits) if (q >> (len(nbr_bits) - 1 - i)) & 1) for q in range(parts)
    )
    mask_row = residue_mask.reshape(1, rows)
    small = jnp.stack([msg_b1, msg_b2, msg_b3, norm1_gain, norm1_bias, ffn_b2, norm2_gain, norm2_bias]).astype(f32)
    small_ff = ffn_b1.reshape(1, FF).astype(f32)
    small_edge = jnp.stack(
        [edge_b1, edge_b2, edge_b3, norm3_gain, norm3_bias, norm3_bias, norm3_bias, norm3_bias]
    ).astype(f32)
    res_place = lax.axis_index("res").astype(jnp.int32).reshape(1)
    nbr_place = lax.axis_index("nbr").astype(jnp.int32).reshape(1)

    smem = pl.BlockSpec(memory_space=pltpu.SMEM)
    vmem = pl.BlockSpec(memory_space=pltpu.VMEM)

    def fixed(*dims):
        return pl.BlockSpec(dims, lambda i: (0,) * len(dims))

    def tiled(*dims):
        return pl.BlockSpec(dims, lambda i: (i,) + (0,) * (len(dims) - 1))

    column, want, counts = call(
        functools.partial(index_kernel, blocks),
        (shape((total, 1), jnp.int32), shape((n_far, 128), bf16), shape((rows, 128), bf16)),
        in_specs=[smem, vmem, vmem],
    )(res_place, neighbours, mask_row)
    wanted = exchange(want, blocks)
    count_a, count_b = shared_sum(counts, "nbr")

    picks = (wanted[:, :1].astype(jnp.int32) == iota((n_far, rows), 1)).astype(bf16)
    far_nodes = exchange(mm(picks, nodes).astype(bf16), blocks)

    edge_tile = tiled(tile, kn, E)
    flat = tiled(tile * SLOT, D)
    act1, d1, d2, act_sum = call(
        message_forward_kernel,
        (shape((total, D), bf16), shape((total, D), bf16), shape((total, D), bf16), shape((rows, D), bf16)),
        scratch=[pltpu.VMEM((width, D), bf16), pltpu.VMEM((rows, D), f32), pltpu.VMEM((tile, SLOT, E), bf16)],
        grid=grid,
        in_specs=[
            tiled(tile * SLOT, 1),
            edge_tile,
            fixed(rows, D),
            fixed(n_far, D),
            fixed(2 * D + E, D),
            fixed(D, D),
            fixed(8, D),
        ],
        out_specs=(flat, flat, flat, tiled(tile, D)),
    )(column, edges, nodes, far_nodes, msg_w1, msg_w2, small)
    sum_a, sum_b = shared_sum(act_sum, "nbr")

    total_act, first_low, normed1, inv1, hidden, hidden_slope, normed2, inv2, sent, send = call(
        node_forward_kernel,
        (
            shape((rows, D), bf16),
            shape((rows, D), bf16),
            shape((rows, D), f32),
            shape((rows, 1), f32),
            shape((rows, FF), bf16),
            shape((rows, FF), bf16),
            shape((rows, D), f32),
            shape((rows, 1), f32),
            shape((rows, D), bf16),
            shape((n_far, D), bf16),
        ),
    )(sum_a, sum_b, count_a, count_b, nodes, mask_row, wanted, msg_w3, ffn_w1, ffn_w2, small, small_ff)
    far_sent = exchange(send, blocks)

    first_rows, second_rows = (2 * D + E) // parts, E // parts
    edge_rows = up_to(first_rows + 2 * second_rows + 16, 32)
    edges_out, base, own_sum, far_sum, local_sum, edge_packed = call(
        functools.partial(edge_kernel, order),
        (
            shape((rows, kn, E), bf16),
            shape((total, E), f32),
            shape((rows, E), bf16),
            shape((n_far, E), bf16),
            shape((rows, E), bf16),
            shape((parts, edge_rows, E), bf16),
        ),
        scratch=[
            pltpu.VMEM((width, E), bf16),
            pltpu.VMEM((rows, E), f32),
            pltpu.VMEM((tile, SLOT, E), bf16),
            pltpu.VMEM((tile, SLOT, E), bf16),
            pltpu.VMEM((width, E), f32),
            pltpu.VMEM((E, E), f32),
            pltpu.VMEM((E, E), f32),
            pltpu.VMEM((E, E), f32),
            pltpu.VMEM((16, E), f32),
            pltpu.VMEM((rows, E), f32),
        ],
        grid=grid,
        in_specs=[
            tiled(tile * SLOT, 1),
            edge_tile,
            edge_tile,
            fixed(rows, D),
            fixed(n_far, D),
            fixed(2 * D + E, E),
            fixed(E, E),
            fixed(E, E),
            fixed(8, E),
        ],
        out_specs=(
            edge_tile,
            tiled(tile * SLOT, E),
            tiled(tile, E),
            fixed(n_far, E),
            fixed(rows, E),
            fixed(parts, edge_rows, E),
        ),
    )(column, edges, edge_cot, sent, far_sent, edge_w1, edge_w2, edge_w3, small_edge)

    back = call(returned_kernel, shape((rows, 2 * E), bf16))(own_sum, local_sum, exchange(far_sum, blocks), wanted)
    back_a, back_b = shared_sum(back, "nbr")
    edge_part = scattered_sum(edge_packed, "nbr").reshape(edge_rows, E)

    wide, narrow = FF // parts, D // parts
    node_rows = up_to(D + wide + narrow + edge_rows // 2, 16 * blocks)
    mixed_grad, up, node_bias, node_packed = call(
        functools.partial(node_backward_kernel, parts),
        (
            shape((rows, D), f32),
            shape((rows, D), f32),
            shape((16, D), f32),
            shape((node_rows, D), bf16),
        ),
        scratch=[pltpu.VMEM((rows, FF), bf16)],
        in_specs=[smem] + [vmem] * 20,
    )(
        nbr_place, back_a, back_b, count_a, count_b, node_cot, mask_row, total_act, first_low, normed1, inv1,
        hidden, hidden_slope, normed2, inv2, edge_w1, msg_w3, ffn_w1, ffn_w2, small, edge_part,
    )
    node_share = assembled(scattered_sum(node_packed, "res"), "res")

    msg_rows = up_to(first_rows + narrow + 16, 8 * blocks)
    edges_grad, own_sum, far_sum, local_sum, msg_packed = call(
        functools.partial(message_backward_kernel, order),
        (
            shape((rows, kn, E), f32),
            shape((rows, D), bf16),
            shape((n_far, D), bf16),
            shape((rows, D), bf16),
            shape((parts, msg_rows, D), bf16),
        ),
        scratch=[
            pltpu.VMEM((tile, SLOT, E), bf16),
            pltpu.VMEM((width, D), f32),
            pltpu.VMEM((E, D), f32),
            pltpu.VMEM((D, D), f32),
            pltpu.VMEM((16, D), f32),
            pltpu.VMEM((rows, D), f32),
        ],
        grid=grid,
        in_specs=[
            tiled(tile * SLOT, 1),
            edge_tile,
            flat,
            flat,
            flat,
            tiled(tile, D),
            tiled(tile * SLOT, E),
            fixed(rows, D),
            fixed(n_far, D),
            fixed(2 * D + E, D),
            fixed(D, D),
            fixed(16, D),
        ],
        out_specs=(edge_tile, tiled(tile, D), fixed(n_far, D), fixed(rows, D), fixed(parts, msg_rows, D)),
    )(column, edges, act1, d1, d2, up, base, nodes, far_nodes, msg_w1, msg_w2, node_bias)

    back = call(returned_last_kernel, shape((rows, D), bf16))(
        own_sum, local_sum, exchange(far_sum, blocks), wanted, msg_w1
    )
    back_a, back_b = shared_sum(back, "nbr")
    nodes_grad = mixed_grad + (back_a.astype(f32) + back_b.astype(f32))
    msg_part = scattered_sum(msg_packed, "nbr").reshape(msg_rows, D)
    msg_share = assembled(scattered_sum(msg_part, "res"), "res").astype(f32)

    node_share = node_share.astype(f32)
    ffn_w1_grad = jnp.concatenate([node_share[j * narrow : (j + 1) * narrow] for j in range(FF // D)], axis=1)
    ffn_w2_grad = node_share[D : D + wide]
    at = D + wide + narrow
    msg_w3_grad = node_share[D + wide : at]
    half = edge_rows // 2
    edge_share = jnp.concatenate([node_share[at : at + half, :E], node_share[at : at + half, 256 : 256 + E]], axis=0)
    edge_w1_grad = edge_share[:first_rows]
    edge_w2_grad = edge_share[first_rows : first_rows + second_rows]
    edge_w3_grad = edge_share[first_rows + second_rows : first_rows + 2 * second_rows]
    place = lax.axis_index("nbr")
    edge_bias = edge_share[first_rows + 2 * second_rows : first_rows + 2 * second_rows + 8]
    edge_bias = lax.dynamic_slice_in_dim(edge_bias, place * second_rows, second_rows, 1)
    msg_w1_grad = msg_share[:first_rows]
    msg_w2_grad = msg_share[first_rows : first_rows + narrow]
    bias_all = msg_share[first_rows + narrow : first_rows + narrow + 16]
    bias = lax.dynamic_slice_in_dim(bias_all[:8], place * narrow, narrow, 1)
    ffn_b1_grad = lax.dynamic_index_in_dim(bias_all[8 : 8 + FF // D], place, 0, keepdims=False)
    return (
        sent,
        edges_out,
        nodes_grad,
        edges_grad,
        msg_w1_grad,
        bias[0],
        msg_w2_grad,
        bias[1],
        msg_w3_grad,
        bias[2],
        bias[3],
        bias[4],
        ffn_w1_grad,
        ffn_b1_grad,
        ffn_w2_grad,
        bias[5],
        bias[6],
        bias[7],
        edge_w1_grad,
        edge_bias[0],
        edge_w2_grad,
        edge_bias[1],
        edge_w3_grad,
        edge_bias[2],
        edge_bias[3],
        edge_bias[4],
    )


def solution(mesh):
    every = P()
    in_specs = (
        (P("res", None), P("res", "nbr", None), P("res", "nbr"), P("res"))
        + (every,) * 22
        + (P("res", None), P("res", "nbr", None))
    )
    matrix, vector = P("nbr", None), P("nbr")
    out_specs = (
        (P("res", None), P("res", "nbr", None), P("res", None), P("res", "nbr", None))
        + (matrix, vector) * 3
        + (vector, vector, matrix, vector, matrix, vector, vector, vector)
        + (matrix, vector) * 3
        + (vector, vector)
    )
    return jax.shard_map(on_device, mesh=mesh, in_specs=in_specs, out_specs=out_specs, check_vma=False)
```

```python
import functools

import jax
import jax.numpy as jnp
from jax import lax
from jax.experimental import pallas as pl
from jax.experimental.pallas import tpu as pltpu
from jax.sharding import PartitionSpec as P

D = 512
E = 192
FF = 2048
FAR = 32
SLOT = 16
KT = 5
VMEM = 32 * 1024 * 1024

bf16 = jnp.bfloat16
f32 = jnp.float32


def mm(a, b):
    return jnp.dot(a, b, preferred_element_type=f32)


def mm_tn(a, b):
    return lax.dot_general(a, b, (((0,), (0,)), ((), ())), preferred_element_type=f32)


def mm_nt(a, b):
    return lax.dot_general(a, b, (((1,), (1,)), ((), ())), preferred_element_type=f32)


def gelu_pair(v):
    c0 = 0.7978845608028654
    c1 = 0.044715 * c0
    square = v * v
    t = jnp.tanh(v * (c0 + c1 * square))
    half = 0.5 + 0.5 * t
    act = v * half
    return act, half + act * (1.0 - t) * (c0 + (3.0 * c1) * square)


def norm_forward(values):
    centred = values - jnp.mean(values, axis=-1, keepdims=True)
    inverse = lax.rsqrt(jnp.mean(centred * centred, axis=-1, keepdims=True) + 1e-05)
    return centred * inverse, inverse


def norm_backward(upstream, normed, inverse, gain):
    scaled = upstream * gain
    first = jnp.mean(scaled, axis=-1, keepdims=True)
    second = jnp.mean(scaled * normed, axis=-1, keepdims=True)
    return inverse * (scaled - first - normed * second)


def row_of(ref):
    return ref[...].astype(f32).reshape(1, ref.shape[0])


def column_sum(values):
    return jnp.sum(values, axis=0, keepdims=True)


def iota(shape, dim):
    return lax.broadcasted_iota(jnp.int32, shape, dim)


def present_column(mask_ref, rows):
    real = jnp.sum(mask_ref[...].astype(f32), axis=1, keepdims=True)
    return (iota((rows, 1), 0).astype(f32) < real).astype(f32)


def pick_matrix(want_ref, rows):
    want = want_ref[...][:, :1].astype(f32)
    return (want == iota((want.shape[0], rows), 1).astype(f32)).astype(bf16)


def one_hot(column, width):
    return (column == iota((column.shape[0], width), 1)).astype(bf16)


def columns_of(col_ref, first, count):
    values = col_ref[...]
    lane = iota(values.shape, 1)
    return [
        jnp.sum(jnp.where(lane == first + j, values, 0.0), axis=1, keepdims=True).astype(jnp.int32)
        for j in range(count)
    ]


def kept_weight(columns):
    return jnp.concatenate([(column >= 0).astype(f32) for column in columns], axis=0)


def spread(rows, values):
    n, c = rows.shape
    return (values.reshape(-1, n, c) + rows[None]).reshape(values.shape)


def gathered(values, n):
    return jnp.sum(values.reshape(-1, n, values.shape[1]), axis=0)


def slot_sums(row_ref, first, count, width, values, acc):
    n = row_ref.shape[1]
    for j in range(count):
        row = row_ref[pl.ds(first + j, 1), :]
        hot = (row == iota((width, n), 0)).astype(bf16)
        acc[...] += mm(hot, values[j * n : (j + 1) * n])


def index_kernel(blocks, me_ref, near_ref, mask_ref, row_ref, col_ref, want_ref, count_ref):
    kn, rows = near_ref.shape
    me = me_ref[0].astype(f32)
    lanes = max(16, blocks)
    index = near_ref[...].astype(f32)
    block = jnp.floor((index + 0.5) * (1.0 / rows))
    slot = index - block * rows
    local = block == me
    far_block = jnp.where(local, -1.0, block)
    real = jnp.sum(mask_ref[...].astype(f32), axis=1, keepdims=True)
    own_place = iota((kn, rows), 1).astype(f32)
    kept = jnp.logical_and(jnp.logical_or(jnp.logical_not(local), slot < real), own_place < real)
    slot_line = iota((rows, rows), 0).astype(f32)
    block_line = iota((lanes, rows), 0).astype(f32)
    hot_slot = [(slot[k : k + 1] == slot_line).astype(bf16) for k in range(kn)]
    hot_block = [(far_block[k : k + 1] == block_line).astype(bf16) for k in range(kn)]
    named = mm_nt(hot_block[0], hot_slot[0])
    for k in range(1, kn):
        named = named + mm_nt(hot_block[k], hot_slot[k])
    flags = (named > 0.0).astype(f32)
    before = (iota((rows, rows), 0) < iota((rows, rows), 1)).astype(bf16)
    rank = mm(flags.astype(bf16), before)
    key = jnp.where(flags > 0.0, rank, -1.0)[:blocks]
    key = jnp.broadcast_to(key[:, None, :], (blocks, FAR, rows)).reshape(blocks * FAR, rows)
    level = (iota((blocks * FAR, 1), 0) & (FAR - 1)).astype(f32)
    hit = (key == level).astype(f32)
    place_row = iota((blocks * FAR, rows), 1).astype(f32)
    want = jnp.sum(hit * place_row, axis=1, keepdims=True)
    found = jnp.sum(hit, axis=1, keepdims=True)
    want = jnp.where(found > 0.0, want, 255.0)
    want_ref[...] = jnp.broadcast_to(want, want_ref.shape).astype(bf16)
    after = (iota((rows, rows), 0) > iota((rows, rows), 1)).astype(bf16)
    rank_down = mm_nt(after, flags.astype(bf16)).astype(bf16)
    edge_rank = jnp.concatenate(
        [
            jnp.sum(mm(rank_down, hot_block[k]) * hot_slot[k].astype(f32), axis=0, keepdims=True)
            for k in range(kn)
        ],
        axis=0,
    )
    place = jnp.where(local, blocks * FAR + slot, block * FAR + edge_rank)
    place = jnp.where(kept, place, -1.0)
    place = jnp.concatenate([place, jnp.full((SLOT - kn, rows), -1.0, f32)], axis=0)
    row_ref[...] = place.astype(jnp.int32)
    col_ref[...] = place.T
    counts = jnp.sum((col_ref[...] >= 0.0).astype(f32), axis=1, keepdims=True)
    count_ref[...] = jnp.broadcast_to(counts, count_ref.shape).astype(bf16)


def message_forward_kernel(
    col_ref, edges_ref, nodes_ref, far_ref, w1_ref, w2_ref, b1_ref, b2_ref,
    act1_ref, d1_ref, d2_ref, sum_ref, table, own, acc,
):
    step = pl.program_id(0)
    last = pl.num_programs(0) - 1
    kt, rows, _ = edges_ref.shape
    n_far = far_ref.shape[0]
    width = table.shape[0]

    @pl.when(step == 0)
    def _():
        weight = w1_ref[D : 2 * D, :]
        table[:n_far] = mm(far_ref[...], weight).astype(bf16)
        table[n_far:] = mm(nodes_ref[...], weight).astype(bf16)
        own[...] = mm(nodes_ref[...], w1_ref[:D, :]) + row_of(b1_ref)
        acc[...] = jnp.zeros_like(acc)

    edge = edges_ref[...].reshape(kt * rows, E)
    columns = columns_of(col_ref, step * kt, kt)
    hot = jnp.concatenate([one_hot(column, width) for column in columns], axis=0)
    pre1 = spread(own[...], mm(hot, table[...]) + mm(edge, w1_ref[2 * D :, :]))
    act, slope = gelu_pair(pre1)
    act1 = act.astype(bf16)
    act1_ref[...] = act1
    d1_ref[...] = slope.astype(bf16)
    act, slope = gelu_pair(mm(act1, w2_ref[...]) + row_of(b2_ref))
    weight = kept_weight(columns)
    d2_ref[...] = (slope * weight).astype(bf16)
    acc[...] += gathered(act.astype(bf16).astype(f32) * weight, rows)

    @pl.when(step == last)
    def _():
        sum_ref[...] = acc[...].astype(bf16)


def node_forward_kernel(
    sum_a, sum_b, count_a, count_b, nodes_ref, mask_ref, want_ref, w3_ref, f1_ref, f2_ref,
    b3_ref, gain1_ref, bias1_ref, fb1_ref, fb2_ref, gain2_ref, bias2_ref,
    total_ref, low_ref, normed1_ref, inv1_ref, hid_ref, slope_ref, normed2_ref, inv2_ref, sent_ref, send_ref,
):
    rows = nodes_ref.shape[0]
    present = present_column(mask_ref, rows)
    count = count_a[...].astype(f32) + count_b[...].astype(f32)
    count = count[:, :1]
    total = sum_a[...].astype(f32) + sum_b[...].astype(f32)
    high = total.astype(bf16)
    total_ref[...] = high
    rest = (total - high.astype(f32)).astype(bf16)
    summed = mm(high, w3_ref[...]) + mm(rest, w3_ref[...]) + count * row_of(b3_ref)
    mixed = nodes_ref[...].astype(f32) + summed / jnp.maximum(count, 1.0)
    normed, inverse = norm_forward(mixed)
    normed1_ref[...] = normed
    inv1_ref[...] = inverse
    first = normed * row_of(gain1_ref) + row_of(bias1_ref)
    low = first.astype(bf16)
    low_ref[...] = low
    act, slope = gelu_pair(mm(low, f1_ref[...]) + row_of(fb1_ref))
    act = act.astype(bf16)
    hid_ref[...] = act
    slope_ref[...] = slope.astype(bf16)
    branch = mm(act, f2_ref[...]) + row_of(fb2_ref)
    normed, inverse = norm_forward(first + branch)
    normed2_ref[...] = normed
    inv2_ref[...] = inverse
    sent = (present * (normed * row_of(gain2_ref) + row_of(bias2_ref))).astype(bf16)
    sent_ref[...] = sent
    send_ref[...] = mm(pick_matrix(want_ref, rows), sent).astype(bf16)


def edge_kernel(
    order, row_ref, col_ref, edges_ref, cot_ref, sent_ref, far_ref, w1_ref, w2_ref, w3_ref, b1_ref, b2_ref, b3_ref, gain_ref, shift_ref,
    out_ref, base_ref, own_ref, far_grad_ref, local_grad_ref, packed_ref,
    table, own, sums, w1_acc, w2_acc, w3_acc, bias_acc, own_acc,
):
    step = pl.program_id(0)
    last = pl.num_programs(0) - 1
    kt, rows, _ = edges_ref.shape
    n_far = far_ref.shape[0]
    width = table.shape[0]

    @pl.when(step == 0)
    def _():
        weight = w1_ref[:, D : 2 * D]
        table[:n_far] = mm_nt(far_ref[...], weight).astype(bf16)
        table[n_far:] = mm_nt(sent_ref[...], weight).astype(bf16)
        own[...] = mm_nt(sent_ref[...], w1_ref[:, :D]) + row_of(b1_ref)
        for acc in (sums, w1_acc, w2_acc, w3_acc, bias_acc, own_acc):
            acc[...] = jnp.zeros_like(acc)

    edge = edges_ref[...].reshape(kt * rows, E)
    cot = cot_ref[...].reshape(kt * rows, E)
    columns = columns_of(col_ref, step * kt, kt)
    hot = jnp.concatenate([one_hot(column, width) for column in columns], axis=0)
    edge_weight = w1_ref[:, 2 * D :]
    pre1 = spread(own[...], mm(hot, table[...]) + mm_nt(edge, edge_weight))
    act, slope1 = gelu_pair(pre1)
    act1 = act.astype(bf16)
    act, slope2 = gelu_pair(mm(act1, w2_ref[...]) + row_of(b2_ref))
    act2 = act.astype(bf16)
    branch = mm(act2, w3_ref[...]) + row_of(b3_ref)
    weight = kept_weight(columns)
    normed, inverse = norm_forward(edge.astype(f32) + branch)
    gain = row_of(gain_ref)
    out = weight * (normed * gain + row_of(shift_ref))
    out_ref[...] = out.astype(bf16).reshape(kt, rows, E)
    up = weight * cot.astype(f32)
    grad = norm_backward(up, normed, inverse, gain)
    low3 = grad.astype(bf16)
    w3_acc[...] += mm_tn(act2, low3)
    low2 = (slope2 * mm_nt(low3, w3_ref[...])).astype(bf16)
    w2_acc[...] += mm_tn(act1, low2)
    low1 = (slope1 * mm_nt(low2, w2_ref[...])).astype(bf16)
    w1_acc[...] += mm_tn(edge, low1)
    slot_sums(row_ref, step * kt, kt, width, low1, sums)
    base_ref[...] = grad + mm(low1, edge_weight)
    own_sum = gathered(low1.astype(f32), rows)
    own_acc[...] += own_sum
    row = iota((16, 1), 0)
    bias_acc[...] += (
        jnp.where(row == 0, column_sum(own_sum), 0.0)
        + jnp.where(row == 1, column_sum(low2.astype(f32)), 0.0)
        + jnp.where(row == 2, column_sum(low3.astype(f32)), 0.0)
        + jnp.where(row == 3, column_sum(up * normed), 0.0)
        + jnp.where(row == 4, column_sum(up), 0.0)
    )

    @pl.when(step == last)
    def _():
        total = sums[...]
        own_low = own_acc[...].astype(bf16)
        own_ref[...] = own_low
        far_grad_ref[...] = total[:n_far].astype(bf16)
        local_grad_ref[...] = total[n_far:].astype(bf16)
        sent = sent_ref[...]
        parts = len(order)
        first = (2 * D + E) // parts
        second = E // parts
        whole = jnp.concatenate(
            [
                mm_tn(sent, own_low),
                mm_tn(far_ref[...], total[:n_far].astype(bf16)) + mm_tn(sent, total[n_far:].astype(bf16)),
                w1_acc[...],
            ],
            axis=0,
        ).astype(bf16)
        second_w = w2_acc[...].astype(bf16)
        third_w = w3_acc[...].astype(bf16)
        bias = bias_acc[...].astype(bf16)
        for q, n in enumerate(order):
            packed_ref[q, :first, :] = whole[n * first : (n + 1) * first]
            packed_ref[q, first : first + second, :] = second_w[n * second : (n + 1) * second]
            packed_ref[q, first + second : first + 2 * second, :] = third_w[n * second : (n + 1) * second]
            packed_ref[q, first + 2 * second :, :] = bias


def returned_kernel(own_ref, local_ref, back_ref, want_ref, out_ref):
    rows = local_ref.shape[0]
    near = local_ref[...].astype(f32) + mm_tn(pick_matrix(want_ref, rows), back_ref[...])
    out_ref[...] = jnp.concatenate([own_ref[...], near.astype(bf16)], axis=1)


def returned_last_kernel(own_ref, local_ref, back_ref, want_ref, w1_ref, out_ref):
    rows = local_ref.shape[0]
    near = local_ref[...].astype(f32) + mm_tn(pick_matrix(want_ref, rows), back_ref[...])
    grad = mm_nt(own_ref[...], w1_ref[:D, :]) + mm_nt(near.astype(bf16), w1_ref[D : 2 * D, :])
    out_ref[...] = grad.astype(bf16)


def node_backward_kernel(
    parts, place_ref, back_a, back_b, count_a, count_b, cot_ref, mask_ref, total_ref, low_ref, normed1_ref, inv1_ref,
    hid_ref, slope_ref, normed2_ref, inv2_ref, ew1_ref, w3_ref, f1_ref, f2_ref, gain1_ref, gain2_ref, edge_part_ref,
    mixed_ref, up_ref, bias_ref, packed_ref, hid_grad,
):
    rows = cot_ref.shape[0]
    place = place_ref[0]
    present = present_column(mask_ref, rows)
    count = (count_a[...].astype(f32) + count_b[...].astype(f32))[:, :1]
    back = (back_a[...].astype(f32) + back_b[...].astype(f32)).astype(bf16)
    node_back = mm(back[:, :E], ew1_ref[:, :D]) + mm(back[:, E:], ew1_ref[:, D : 2 * D])
    up = present * (cot_ref[...].astype(f32) + node_back)
    normed2 = normed2_ref[...]
    sum_grad = norm_backward(up, normed2, inv2_ref[...], row_of(gain2_ref))
    branch_grad = sum_grad.astype(bf16)
    hidden_grad = (slope_ref[...].astype(f32) * mm_nt(branch_grad, f2_ref[...])).astype(bf16)
    first_grad = sum_grad + mm_nt(hidden_grad, f1_ref[...])
    normed1 = normed1_ref[...]
    mixed_grad = norm_backward(first_grad, normed1, inv1_ref[...], row_of(gain1_ref))
    mixed_ref[...] = mixed_grad
    message_grad = (mixed_grad / jnp.maximum(count, 1.0)).astype(bf16)
    up_ref[...] = mm_nt(message_grad, w3_ref[...])
    row = iota((16, 1), 0)
    hidden_sum = column_sum(hidden_grad.astype(f32))
    bias = (
        jnp.where(row == 2, column_sum(count * message_grad.astype(f32)), 0.0)
        + jnp.where(row == 3, column_sum(first_grad * normed1), 0.0)
        + jnp.where(row == 4, column_sum(first_grad), 0.0)
        + jnp.where(row == 5, column_sum(branch_grad.astype(f32)), 0.0)
        + jnp.where(row == 6, column_sum(up * normed2), 0.0)
        + jnp.where(row == 7, column_sum(up), 0.0)
    )
    for j in range(FF // D):
        bias = bias + jnp.where(row == 8 + j, hidden_sum[:, j * D : (j + 1) * D], 0.0)
    bias_ref[...] = bias * (1.0 / parts)
    wide, narrow = FF // parts, D // parts
    low = low_ref[:, pl.ds(pl.multiple_of(place * narrow, narrow), narrow)]
    for j in range(FF // D):
        packed_ref[j * narrow : (j + 1) * narrow, :] = mm_tn(low, hidden_grad[:, j * D : (j + 1) * D]).astype(bf16)
    hid = hid_ref[:, pl.ds(pl.multiple_of(place * wide, wide), wide)]
    packed_ref[D : D + wide, :] = mm_tn(hid, branch_grad).astype(bf16)
    total = total_ref[:, pl.ds(pl.multiple_of(place * narrow, narrow), narrow)]
    packed_ref[D + wide : D + wide + narrow, :] = mm_tn(total, message_grad).astype(bf16)
    at = D + wide + narrow
    half = edge_part_ref.shape[0] // 2
    packed_ref[at:, :] = jnp.zeros((packed_ref.shape[0] - at, D), bf16)
    packed_ref[at : at + half, :E] = edge_part_ref[:half, :]
    packed_ref[at : at + half, 256 : 256 + E] = edge_part_ref[half:, :]


def message_backward_kernel(
    order, row_ref, edges_ref, act1_ref, d1_ref, d2_ref, up_ref, base_ref, nodes_ref, far_ref, w1_ref, w2_ref, node_bias_ref,
    out_ref, own_ref, far_grad_ref, local_grad_ref, packed_ref,
    sums, w1_acc, w2_acc, bias_acc, own_acc,
):
    step = pl.program_id(0)
    last = pl.num_programs(0) - 1
    kt, rows, _ = edges_ref.shape
    n_far = far_ref.shape[0]
    width = sums.shape[0]

    @pl.when(step == 0)
    def _():
        for acc in (sums, w1_acc, w2_acc, own_acc):
            acc[...] = jnp.zeros_like(acc)
        bias_acc[...] = node_bias_ref[...]

    edge = edges_ref[...].reshape(kt * rows, E)
    slope2 = d2_ref[...].astype(f32).reshape(kt, rows, D)
    low2 = (slope2 * up_ref[...][None]).astype(bf16).reshape(kt * rows, D)
    w2_acc[...] += mm_tn(act1_ref[...], low2)
    low1 = (d1_ref[...].astype(f32) * mm_nt(low2, w2_ref[...])).astype(bf16)
    w1_acc[...] += mm_tn(edge, low1)
    slot_sums(row_ref, step * kt, kt, width, low1, sums)
    grad = base_ref[...] + mm_nt(low1, w1_ref[2 * D :, :])
    out_ref[...] = grad.reshape(kt, rows, E)
    own_sum = gathered(low1.astype(f32), rows)
    own_acc[...] += own_sum
    row = iota((16, 1), 0)
    bias_acc[...] += jnp.where(row == 0, column_sum(own_sum), 0.0) + jnp.where(
        row == 1, column_sum(low2.astype(f32)), 0.0
    )

    @pl.when(step == last)
    def _():
        total = sums[...]
        own_low = own_acc[...].astype(bf16)
        own_ref[...] = own_low
        far_grad_ref[...] = total[:n_far].astype(bf16)
        local_grad_ref[...] = total[n_far:].astype(bf16)
        nodes = nodes_ref[...]
        parts = len(order)
        first = (2 * D + E) // parts
        second = D // parts
        whole = jnp.concatenate(
            [
                mm_tn(nodes, own_low),
                mm_tn(far_ref[...], total[:n_far].astype(bf16)) + mm_tn(nodes, total[n_far:].astype(bf16)),
                w1_acc[...],
            ],
            axis=0,
        ).astype(bf16)
        second_w = w2_acc[...].astype(bf16)
        bias = bias_acc[...].astype(bf16)
        for q, n in enumerate(order):
            packed_ref[q, :first, :] = whole[n * first : (n + 1) * first]
            packed_ref[q, first : first + second, :] = second_w[n * second : (n + 1) * second]
            packed_ref[q, first + second : first + second + 16, :] = bias
            if packed_ref.shape[1] > first + second + 16:
                packed_ref[q, first + second + 16 :, :] = jnp.zeros(
                    (packed_ref.shape[1] - first - second - 16, D), bf16
                )


def swap(values, axis, bit):
    return lax.ppermute(values, axis, [(i, i ^ bit) for i in range(lax.axis_size(axis))])


def bits_of(axis):
    size, bit, out = lax.axis_size(axis), 1, []
    while bit < size:
        out.append(bit)
        bit *= 2
    return out


def add_low(a, b):
    return (a.astype(f32) + b.astype(f32)).astype(bf16)


def shared_sum(values, axis):
    bits = bits_of(axis)
    for bit in bits[:-1]:
        values = add_low(values, swap(values, axis, bit))
    return values, swap(values, axis, bits[-1])


def halved_sum(values, axis, bit):
    half = values.shape[0] // 2
    side = (lax.axis_index(axis) // bit) & 1
    kept = lax.dynamic_slice_in_dim(values, side * half, half, 0)
    given = lax.dynamic_slice_in_dim(values, (1 - side) * half, half, 0)
    return add_low(kept, swap(given, axis, bit))


def rejoined(values, axis, bit):
    other = swap(values, axis, bit)
    side = (lax.axis_index(axis) // bit) & 1
    return jnp.where(
        side == 0, jnp.concatenate([values, other], axis=0), jnp.concatenate([other, values], axis=0)
    )


def scattered_sum(values, axis, bits):
    for bit in bits:
        values = halved_sum(values, axis, bit)
    return values


def gathered_rows(values, axis, bits):
    for bit in bits:
        values = rejoined(values, axis, bit)
    return values


def exchange(values, blocks):
    shaped = values.reshape((blocks, values.shape[0] // blocks) + values.shape[1:])
    return lax.all_to_all(shaped, "res", 0, 0, tiled=True).reshape(values.shape)


def call(kernel, outs, scratch=(), grid=None, in_specs=None, out_specs=None, cost=None):
    extra = {}
    if grid is not None:
        extra = dict(grid=grid, in_specs=in_specs, out_specs=out_specs)
    elif in_specs is not None:
        extra = dict(in_specs=in_specs)
    return pl.pallas_call(
        kernel,
        out_shape=outs,
        scratch_shapes=list(scratch),
        compiler_params=pltpu.CompilerParams(vmem_limit_bytes=VMEM),
        cost_estimate=cost,
        **extra,
    )


def shape(dims, dtype):
    return jax.ShapeDtypeStruct(dims, dtype)


def stored(dims, dtype):
    return pltpu.HBM(dims, dtype)


def read(*values):
    return tuple(pltpu.with_memory_space_constraint(value, pltpu.HBM) for value in values)


def up_to(value, unit):
    return -(-value // unit) * unit


def on_device(
    nodes,
    edges,
    neighbours,
    residue_mask,
    msg_w1,
    msg_b1,
    msg_w2,
    msg_b2,
    msg_w3,
    msg_b3,
    norm1_gain,
    norm1_bias,
    ffn_w1,
    ffn_b1,
    ffn_w2,
    ffn_b2,
    norm2_gain,
    norm2_bias,
    edge_w1,
    edge_b1,
    edge_w2,
    edge_b2,
    edge_w3,
    edge_b3,
    norm3_gain,
    norm3_bias,
    node_cot,
    edge_cot,
):
    rows, kn = neighbours.shape
    blocks, parts = lax.axis_size("res"), lax.axis_size("nbr")
    total = rows * kn
    n_far = blocks * FAR
    width = n_far + rows
    kt = next(t for t in (KT, 3, 1) if kn % t == 0)
    grid = (kn // kt,)
    nbr_bits = bits_of("nbr")
    order = tuple(
        sum(bit for i, bit in enumerate(nbr_bits) if (q >> (len(nbr_bits) - 1 - i)) & 1) for q in range(parts)
    )
    mask_row = residue_mask.reshape(1, rows)
    edges = edges.transpose(1, 0, 2)
    edge_cot = edge_cot.transpose(1, 0, 2)
    edge_w1 = edge_w1.T
    res_place = lax.axis_index("res").astype(jnp.int32).reshape(1)
    nbr_place = lax.axis_index("nbr").astype(jnp.int32).reshape(1)

    smem = pl.BlockSpec(memory_space=pltpu.SMEM)
    vmem = pl.BlockSpec(memory_space=pltpu.VMEM)

    def fixed(*dims):
        return pl.BlockSpec(dims, lambda i: (0,) * len(dims))

    def tiled(*dims):
        return pl.BlockSpec(dims, lambda i: (i,) + (0,) * (len(dims) - 1))

    place_row, place_col, want, counts = call(
        functools.partial(index_kernel, blocks),
        (
            shape((SLOT, rows), jnp.int32),
            shape((rows, SLOT), f32),
            shape((n_far, 128), bf16),
            shape((rows, 128), bf16),
        ),
        in_specs=[smem, vmem, vmem],
    )(res_place, neighbours.T, mask_row)
    together = lax.optimization_barrier
    wanted = exchange(want, blocks)

    picks = (wanted[:, :1].astype(jnp.int32) == iota((n_far, rows), 1)).astype(bf16)
    far_nodes = exchange(mm(picks, nodes).astype(bf16), blocks)
    far_nodes, counts = together((far_nodes, counts))
    count_a, count_b = shared_sum(counts, "nbr")

    edge_tile = tiled(kt, rows, E)
    flat = tiled(kt * rows, D)
    flat_edge = tiled(kt * rows, E)
    act1, d1, d2, act_sum = call(
        message_forward_kernel,
        (stored((total, D), bf16), stored((total, D), bf16), stored((total, D), bf16), shape((rows, D), bf16)),
        scratch=[pltpu.VMEM((width, D), bf16), pltpu.VMEM((rows, D), f32), pltpu.VMEM((rows, D), f32)],
        grid=grid,
        in_specs=[
            fixed(rows, SLOT),
            edge_tile,
            fixed(rows, D),
            fixed(n_far, D),
            fixed(2 * D + E, D),
            fixed(D, D),
            fixed(D),
            fixed(D),
        ],
        out_specs=(flat, flat, flat, fixed(rows, D)),
        cost=pl.CostEstimate(flops=16 * total * D * D, bytes_accessed=total * D * 8, transcendentals=2 * total * D),
    )(*read(place_col, edges, nodes), far_nodes, *read(msg_w1, msg_w2), msg_b1, msg_b2)
    sum_a, sum_b = shared_sum(act_sum, "nbr")

    total_act, first_low, normed1, inv1, hidden, hidden_slope, normed2, inv2, sent, send = call(
        node_forward_kernel,
        (
            stored((rows, D), bf16),
            stored((rows, D), bf16),
            stored((rows, D), f32),
            stored((rows, 1), f32),
            stored((rows, FF), bf16),
            stored((rows, FF), bf16),
            stored((rows, D), f32),
            stored((rows, 1), f32),
            stored((rows, D), bf16),
            shape((n_far, D), bf16),
        ),
    )(sum_a, sum_b, count_a, count_b, nodes, mask_row, wanted, msg_w3, ffn_w1, ffn_w2,
      msg_b3, norm1_gain, norm1_bias, ffn_b1, ffn_b2, norm2_gain, norm2_bias)
    far_sent = exchange(send, blocks)

    first_rows, second_rows = (2 * D + E) // parts, E // parts
    edge_rows = up_to(first_rows + 2 * second_rows + 16, 32)
    edges_out, base, own_sum, far_sum, local_sum, edge_packed = call(
        functools.partial(edge_kernel, order),
        (
            shape((kn, rows, E), bf16),
            stored((total, E), f32),
            stored((rows, E), bf16),
            shape((n_far, E), bf16),
            stored((rows, E), bf16),
            shape((parts, edge_rows, E), bf16),
        ),
        scratch=[
            pltpu.VMEM((width, E), bf16),
            pltpu.VMEM((rows, E), f32),
            pltpu.VMEM((width, E), f32),
            pltpu.VMEM((E, E), f32),
            pltpu.VMEM((E, E), f32),
            pltpu.VMEM((E, E), f32),
            pltpu.VMEM((16, E), f32),
            pltpu.VMEM((rows, E), f32),
        ],
        grid=grid,
        in_specs=[
            fixed(SLOT, rows),
            fixed(rows, SLOT),
            edge_tile,
            edge_tile,
            fixed(rows, D),
            fixed(n_far, D),
            fixed(E, 2 * D + E),
            fixed(E, E),
            fixed(E, E),
        ]
        + [fixed(E)] * 5,
        out_specs=(
            edge_tile,
            flat_edge,
            fixed(rows, E),
            fixed(n_far, E),
            fixed(rows, E),
            fixed(parts, edge_rows, E),
        ),
        cost=pl.CostEstimate(flops=16 * total * D * D, bytes_accessed=total * E * 12, transcendentals=2 * total * E),
    )(*read(place_row, place_col, edges, edge_cot, sent), far_sent, *read(edge_w1, edge_w2, edge_w3),
      edge_b1, edge_b2, edge_b3, norm3_gain, norm3_bias)

    far_back, edge_packed = together((exchange(far_sum, blocks), edge_packed))
    back = call(returned_kernel, shape((rows, 2 * E), bf16))(own_sum, local_sum, far_back, wanted)
    back_a, back_b = shared_sum(back, "nbr")
    edge_part = scattered_sum(edge_packed, "nbr", nbr_bits).reshape(edge_rows, E)

    wide, narrow = FF // parts, D // parts
    node_rows = up_to(D + wide + narrow + edge_rows // 2, 16 * blocks)
    mixed_grad, up, node_bias, node_packed = call(
        functools.partial(node_backward_kernel, parts),
        (
            shape((rows, D), f32),
            shape((rows, D), f32),
            shape((16, D), f32),
            shape((node_rows, D), bf16),
        ),
        scratch=[pltpu.VMEM((rows, FF), bf16)],
        in_specs=[smem] + [vmem] * 21,
    )(
        nbr_place, back_a, back_b, count_a, count_b, *read(node_cot), mask_row, *read(total_act, first_low, normed1, inv1),
        *read(hidden, hidden_slope, normed2, inv2, edge_w1), msg_w3, ffn_w1, ffn_w2, norm1_gain, norm2_gain, edge_part,
    )
    bits = bits_of("res")
    order_a, order_b = bits, bits[1:2] + bits[:1] + bits[2:]
    part_a = halved_sum(node_packed[: node_rows // 2], "res", order_a[0])
    part_b = halved_sum(node_packed[node_rows // 2 :], "res", order_b[0])

    msg_rows = up_to(first_rows + narrow + 16, 8 * blocks)
    edges_grad, own_sum, far_sum, local_sum, msg_packed = call(
        functools.partial(message_backward_kernel, order),
        (
            shape((kn, rows, E), f32),
            shape((rows, D), bf16),
            shape((n_far, D), bf16),
            shape((rows, D), bf16),
            shape((parts, msg_rows, D), bf16),
        ),
        scratch=[
            pltpu.VMEM((width, D), f32),
            pltpu.VMEM((E, D), f32),
            pltpu.VMEM((D, D), f32),
            pltpu.VMEM((16, D), f32),
            pltpu.VMEM((rows, D), f32),
        ],
        grid=grid,
        in_specs=[
            fixed(SLOT, rows),
            edge_tile,
            flat,
            flat,
            flat,
            fixed(rows, D),
            flat_edge,
            fixed(rows, D),
            fixed(n_far, D),
            fixed(2 * D + E, D),
            fixed(D, D),
            fixed(16, D),
        ],
        out_specs=(edge_tile, fixed(rows, D), fixed(n_far, D), fixed(rows, D), fixed(parts, msg_rows, D)),
        cost=pl.CostEstimate(flops=16 * total * D * D, bytes_accessed=total * D * 10, transcendentals=0),
    )(*read(place_row, edges, act1, d1, d2), up, *read(base, nodes), far_nodes, *read(msg_w1, msg_w2), node_bias)

    far_sum, msg_part, part_a, part_b = together((far_sum, msg_packed, part_a, part_b))
    msg_part = halved_sum(msg_part, "nbr", nbr_bits[0])
    part_a = halved_sum(part_a, "res", order_a[1])
    part_b = halved_sum(part_b, "res", order_b[1])
    far_sum, msg_part, part_a, part_b = together((far_sum, msg_part, part_a, part_b))
    msg_part = scattered_sum(msg_part, "nbr", nbr_bits[1:]).reshape(msg_rows, D)
    far_back = exchange(far_sum, blocks)
    part_a = scattered_sum(part_a, "res", order_a[2:])
    part_b = scattered_sum(part_b, "res", order_b[2:])
    far_back, msg_part, part_a, part_b = together((far_back, msg_part, part_a, part_b))
    msg_part = halved_sum(msg_part, "res", bits[0])
    back = call(returned_last_kernel, shape((rows, D), bf16))(own_sum, local_sum, far_back, wanted, msg_w1)
    for bit in nbr_bits[:-1]:
        back = add_low(back, swap(back, "nbr", bit))
    part_a = gathered_rows(part_a, "res", order_a[:1:-1])
    part_b = gathered_rows(part_b, "res", order_b[:1:-1])
    back, msg_part, part_a, part_b = together((back, msg_part, part_a, part_b))
    msg_part = scattered_sum(msg_part, "res", bits[1:-1])
    back_b = swap(back, "nbr", nbr_bits[-1])
    part_a = rejoined(part_a, "res", order_a[1])
    part_b = rejoined(part_b, "res", order_b[1])
    back, back_b, msg_part, part_a, part_b = together((back, back_b, msg_part, part_a, part_b))
    nodes_grad = mixed_grad + (back.astype(f32) + back_b.astype(f32))
    msg_part = add_low(msg_part, swap(msg_part, "res", bits[-1]))
    part_a = rejoined(part_a, "res", order_a[0])
    part_b = rejoined(part_b, "res", order_b[0])
    msg_part, part_a, part_b = together((msg_part, part_a, part_b))
    msg_share = gathered_rows(msg_part, "res", bits[-2::-1]).astype(f32)
    node_share = jnp.concatenate([part_a, part_b], axis=0).astype(f32)

    ffn_w1_grad = jnp.concatenate([node_share[j * narrow : (j + 1) * narrow] for j in range(FF // D)], axis=1)
    ffn_w2_grad = node_share[D : D + wide]
    at = D + wide + narrow
    msg_w3_grad = node_share[D + wide : at]
    half = edge_rows // 2
    edge_share = jnp.concatenate([node_share[at : at + half, :E], node_share[at : at + half, 256 : 256 + E]], axis=0)
    edge_w1_grad = edge_share[:first_rows]
    edge_w2_grad = edge_share[first_rows : first_rows + second_rows]
    edge_w3_grad = edge_share[first_rows + second_rows : first_rows + 2 * second_rows]
    place = lax.axis_index("nbr")
    edge_bias = edge_share[first_rows + 2 * second_rows : first_rows + 2 * second_rows + 8]
    edge_bias = lax.dynamic_slice_in_dim(edge_bias, place * second_rows, second_rows, 1)
    msg_w1_grad = msg_share[:first_rows]
    msg_w2_grad = msg_share[first_rows : first_rows + narrow]
    bias_all = msg_share[first_rows + narrow : first_rows + narrow + 16]
    bias = lax.dynamic_slice_in_dim(bias_all[:8], place * narrow, narrow, 1)
    ffn_b1_grad = lax.dynamic_index_in_dim(bias_all[8 : 8 + FF // D], place, 0, keepdims=False)
    return (
        sent,
        edges_out.transpose(1, 0, 2),
        nodes_grad,
        edges_grad.transpose(1, 0, 2),
        msg_w1_grad,
        bias[0],
        msg_w2_grad,
        bias[1],
        msg_w3_grad,
        bias[2],
        bias[3],
        bias[4],
        ffn_w1_grad,
        ffn_b1_grad,
        ffn_w2_grad,
        bias[5],
        bias[6],
        bias[7],
        edge_w1_grad,
        edge_bias[0],
        edge_w2_grad,
        edge_bias[1],
        edge_w3_grad,
        edge_bias[2],
        edge_bias[3],
        edge_bias[4],
    )


def solution(mesh):
    every = P()
    in_specs = (
        (P("res", None), P("res", "nbr", None), P("res", "nbr"), P("res"))
        + (every,) * 22
        + (P("res", None), P("res", "nbr", None))
    )
    matrix, vector = P("nbr", None), P("nbr")
    out_specs = (
        (P("res", None), P("res", "nbr", None), P("res", None), P("res", "nbr", None))
        + (matrix, vector) * 3
        + (vector, vector, matrix, vector, matrix, vector, vector, vector)
        + (matrix, vector) * 3
        + (vector, vector)
    )
    return jax.shard_map(on_device, mesh=mesh, in_specs=in_specs, out_specs=out_specs, check_vma=False)
```

```python
import functools

import jax
import jax.numpy as jnp
from jax import lax
from jax.experimental import pallas as pl
from jax.experimental.pallas import tpu as pltpu
from jax.sharding import PartitionSpec as P

D = 512
E = 192
FF = 2048
FAR = 32
SLOT = 16
KT = 5
VMEM = 32 * 1024 * 1024

bf16 = jnp.bfloat16
f32 = jnp.float32


def mm(a, b):
    return jnp.dot(a, b, preferred_element_type=f32)


def mm_tn(a, b):
    return lax.dot_general(a, b, (((0,), (0,)), ((), ())), preferred_element_type=f32)


def mm_nt(a, b):
    return lax.dot_general(a, b, (((1,), (1,)), ((), ())), preferred_element_type=f32)


def gelu_pair(v):
    c0 = 0.7978845608028654
    c1 = 0.044715 * c0
    square = v * v
    t = jnp.tanh(v * (c0 + c1 * square))
    half = 0.5 + 0.5 * t
    act = v * half
    return act, half + act * (1.0 - t) * (c0 + (3.0 * c1) * square)


def norm_forward(values):
    centred = values - jnp.mean(values, axis=-1, keepdims=True)
    inverse = lax.rsqrt(jnp.mean(centred * centred, axis=-1, keepdims=True) + 1e-05)
    return centred * inverse, inverse


def norm_backward(upstream, normed, inverse, gain):
    scaled = upstream * gain
    first = jnp.mean(scaled, axis=-1, keepdims=True)
    second = jnp.mean(scaled * normed, axis=-1, keepdims=True)
    return inverse * (scaled - first - normed * second)


def row_of(ref):
    return ref[...].astype(f32).reshape(1, ref.shape[0])


def column_sum(values):
    return jnp.sum(values, axis=0, keepdims=True)


def iota(shape, dim):
    return lax.broadcasted_iota(jnp.int32, shape, dim)


def present_column(mask_ref, rows):
    real = jnp.sum(mask_ref[...].astype(f32), axis=1, keepdims=True)
    return (iota((rows, 1), 0).astype(f32) < real).astype(f32)


def pick_matrix(want_ref, rows):
    want = want_ref[...][:, :1].astype(f32)
    return (want == iota((want.shape[0], rows), 1).astype(f32)).astype(bf16)


def one_hot(column, width):
    return (column == iota((column.shape[0], width), 1)).astype(bf16)


def columns_of(col_ref, first, count):
    values = col_ref[...]
    lane = iota(values.shape, 1)
    return [
        jnp.sum(jnp.where(lane == first + j, values, 0.0), axis=1, keepdims=True).astype(jnp.int32)
        for j in range(count)
    ]


def kept_weight(columns):
    return jnp.concatenate([(column >= 0).astype(f32) for column in columns], axis=0)


def spread(rows, values):
    n, c = rows.shape
    return (values.reshape(-1, n, c) + rows[None]).reshape(values.shape)


def gathered(values, n):
    return jnp.sum(values.reshape(-1, n, values.shape[1]), axis=0)


def slot_sums(row_ref, first, count, width, values, acc):
    n = row_ref.shape[1]
    for j in range(count):
        row = row_ref[pl.ds(first + j, 1), :]
        hot = (row == iota((width, n), 0)).astype(bf16)
        acc[...] += mm(hot, values[j * n : (j + 1) * n])


def index_kernel(blocks, me_ref, near_ref, mask_ref, row_ref, col_ref, want_ref, count_ref):
    kn, rows = near_ref.shape
    me = me_ref[0].astype(f32)
    lanes = max(16, blocks)
    index = near_ref[...].astype(f32)
    block = jnp.floor((index + 0.5) * (1.0 / rows))
    slot = index - block * rows
    local = block == me
    far_block = jnp.where(local, -1.0, block)
    real = jnp.sum(mask_ref[...].astype(f32), axis=1, keepdims=True)
    own_place = iota((kn, rows), 1).astype(f32)
    kept = jnp.logical_and(jnp.logical_or(jnp.logical_not(local), slot < real), own_place < real)
    slot_line = iota((rows, rows), 0).astype(f32)
    block_line = iota((lanes, rows), 0).astype(f32)
    hot_slot = [(slot[k : k + 1] == slot_line).astype(bf16) for k in range(kn)]
    hot_block = [(far_block[k : k + 1] == block_line).astype(bf16) for k in range(kn)]
    named = mm_nt(hot_block[0], hot_slot[0])
    for k in range(1, kn):
        named = named + mm_nt(hot_block[k], hot_slot[k])
    flags = (named > 0.0).astype(f32)
    before = (iota((rows, rows), 0) < iota((rows, rows), 1)).astype(bf16)
    rank = mm(flags.astype(bf16), before)
    key = jnp.where(flags > 0.0, rank, -1.0)[:blocks]
    key = jnp.broadcast_to(key[:, None, :], (blocks, FAR, rows)).reshape(blocks * FAR, rows)
    level = (iota((blocks * FAR, 1), 0) & (FAR - 1)).astype(f32)
    hit = (key == level).astype(f32)
    place_row = iota((blocks * FAR, rows), 1).astype(f32)
    want = jnp.sum(hit * place_row, axis=1, keepdims=True)
    found = jnp.sum(hit, axis=1, keepdims=True)
    want = jnp.where(found > 0.0, want, 255.0)
    want_ref[...] = jnp.broadcast_to(want, want_ref.shape).astype(bf16)
    after = (iota((rows, rows), 0) > iota((rows, rows), 1)).astype(bf16)
    rank_down = mm_nt(after, flags.astype(bf16)).astype(bf16)
    edge_rank = jnp.concatenate(
        [
            jnp.sum(mm(rank_down, hot_block[k]) * hot_slot[k].astype(f32), axis=0, keepdims=True)
            for k in range(kn)
        ],
        axis=0,
    )
    place = jnp.where(local, blocks * FAR + slot, block * FAR + edge_rank)
    place = jnp.where(kept, place, -1.0)
    place = jnp.concatenate([place, jnp.full((SLOT - kn, rows), -1.0, f32)], axis=0)
    row_ref[...] = place.astype(jnp.int32)
    col_ref[...] = place.T
    counts = jnp.sum((col_ref[...] >= 0.0).astype(f32), axis=1, keepdims=True)
    count_ref[...] = jnp.broadcast_to(counts, count_ref.shape).astype(bf16)


def message_forward_kernel(
    col_ref, edges_ref, nodes_ref, far_ref, w1_ref, w2_ref, b1_ref, b2_ref,
    act1_ref, d1_ref, d2_ref, sum_ref, table, own, acc,
):
    step = pl.program_id(0)
    last = pl.num_programs(0) - 1
    kt, rows, _ = edges_ref.shape
    n_far = far_ref.shape[0]
    width = table.shape[0]

    @pl.when(step == 0)
    def _():
        weight = w1_ref[D : 2 * D, :]
        table[:n_far] = mm(far_ref[...], weight).astype(bf16)
        table[n_far:] = mm(nodes_ref[...], weight).astype(bf16)
        own[...] = mm(nodes_ref[...], w1_ref[:D, :]) + row_of(b1_ref)
        acc[...] = jnp.zeros_like(acc)

    edge = edges_ref[...].reshape(kt * rows, E)
    columns = columns_of(col_ref, step * kt, kt)
    hot = jnp.concatenate([one_hot(column, width) for column in columns], axis=0)
    pre1 = spread(own[...], mm(hot, table[...]) + mm(edge, w1_ref[2 * D :, :]))
    act, slope = gelu_pair(pre1)
    act1 = act.astype(bf16)
    act1_ref[...] = act1
    d1_ref[...] = slope.astype(bf16)
    act, slope = gelu_pair(mm(act1, w2_ref[...]) + row_of(b2_ref))
    weight = kept_weight(columns)
    d2_ref[...] = (slope * weight).astype(bf16)
    acc[...] += gathered(act.astype(bf16).astype(f32) * weight, rows)

    @pl.when(step == last)
    def _():
        sum_ref[...] = acc[...].astype(bf16)


def node_forward_kernel(
    sum_a, sum_b, count_a, count_b, nodes_ref, mask_ref, want_ref, w3_ref, f1_ref, f2_ref,
    b3_ref, gain1_ref, bias1_ref, fb1_ref, fb2_ref, gain2_ref, bias2_ref,
    total_ref, low_ref, normed1_ref, inv1_ref, hid_ref, slope_ref, normed2_ref, inv2_ref, sent_ref, send_ref,
):
    rows = nodes_ref.shape[0]
    present = present_column(mask_ref, rows)
    count = count_a[...].astype(f32) + count_b[...].astype(f32)
    count = count[:, :1]
    total = sum_a[...].astype(f32) + sum_b[...].astype(f32)
    high = total.astype(bf16)
    total_ref[...] = high
    rest = (total - high.astype(f32)).astype(bf16)
    summed = mm(high, w3_ref[...]) + mm(rest, w3_ref[...]) + count * row_of(b3_ref)
    mixed = nodes_ref[...].astype(f32) + summed / jnp.maximum(count, 1.0)
    normed, inverse = norm_forward(mixed)
    normed1_ref[...] = normed
    inv1_ref[...] = inverse
    first = normed * row_of(gain1_ref) + row_of(bias1_ref)
    low = first.astype(bf16)
    low_ref[...] = low
    act, slope = gelu_pair(mm(low, f1_ref[...]) + row_of(fb1_ref))
    act = act.astype(bf16)
    hid_ref[...] = act
    slope_ref[...] = slope.astype(bf16)
    branch = mm(act, f2_ref[...]) + row_of(fb2_ref)
    normed, inverse = norm_forward(first + branch)
    normed2_ref[...] = normed
    inv2_ref[...] = inverse
    sent = (present * (normed * row_of(gain2_ref) + row_of(bias2_ref))).astype(bf16)
    sent_ref[...] = sent
    send_ref[...] = mm(pick_matrix(want_ref, rows), sent).astype(bf16)


def edge_kernel(
    order, row_ref, col_ref, edges_ref, cot_ref, sent_ref, far_ref, w1_ref, w2_ref, w3_ref, b1_ref, b2_ref, b3_ref, gain_ref, shift_ref,
    out_ref, base_ref, own_ref, far_grad_ref, local_grad_ref, packed_ref,
    table, own, sums, w1_acc, w2_acc, w3_acc, bias_acc, own_acc,
):
    step = pl.program_id(0)
    last = pl.num_programs(0) - 1
    kt, rows, _ = edges_ref.shape
    n_far = far_ref.shape[0]
    width = table.shape[0]

    @pl.when(step == 0)
    def _():
        weight = w1_ref[:, D : 2 * D]
        table[:n_far] = mm_nt(far_ref[...], weight).astype(bf16)
        table[n_far:] = mm_nt(sent_ref[...], weight).astype(bf16)
        own[...] = mm_nt(sent_ref[...], w1_ref[:, :D]) + row_of(b1_ref)
        for acc in (sums, w1_acc, w2_acc, w3_acc, bias_acc, own_acc):
            acc[...] = jnp.zeros_like(acc)

    edge = edges_ref[...].reshape(kt * rows, E)
    cot = cot_ref[...].reshape(kt * rows, E)
    columns = columns_of(col_ref, step * kt, kt)
    hot = jnp.concatenate([one_hot(column, width) for column in columns], axis=0)
    edge_weight = w1_ref[:, 2 * D :]
    pre1 = spread(own[...], mm(hot, table[...]) + mm_nt(edge, edge_weight))
    act, slope1 = gelu_pair(pre1)
    act1 = act.astype(bf16)
    act, slope2 = gelu_pair(mm(act1, w2_ref[...]) + row_of(b2_ref))
    act2 = act.astype(bf16)
    branch = mm(act2, w3_ref[...]) + row_of(b3_ref)
    weight = kept_weight(columns)
    normed, inverse = norm_forward(edge.astype(f32) + branch)
    gain = row_of(gain_ref)
    out = weight * (normed * gain + row_of(shift_ref))
    out_ref[...] = out.astype(bf16).reshape(kt, rows, E)
    up = weight * cot.astype(f32)
    grad = norm_backward(up, normed, inverse, gain)
    low3 = grad.astype(bf16)
    w3_acc[...] += mm_tn(act2, low3)
    low2 = (slope2 * mm_nt(low3, w3_ref[...])).astype(bf16)
    w2_acc[...] += mm_tn(act1, low2)
    low1 = (slope1 * mm_nt(low2, w2_ref[...])).astype(bf16)
    w1_acc[...] += mm_tn(edge, low1)
    slot_sums(row_ref, step * kt, kt, width, low1, sums)
    base_ref[...] = grad + mm(low1, edge_weight)
    own_sum = gathered(low1.astype(f32), rows)
    own_acc[...] += own_sum
    row = iota((16, 1), 0)
    bias_acc[...] += (
        jnp.where(row == 0, column_sum(own_sum), 0.0)
        + jnp.where(row == 1, column_sum(low2.astype(f32)), 0.0)
        + jnp.where(row == 2, column_sum(low3.astype(f32)), 0.0)
        + jnp.where(row == 3, column_sum(up * normed), 0.0)
        + jnp.where(row == 4, column_sum(up), 0.0)
    )

    @pl.when(step == last)
    def _():
        total = sums[...]
        own_low = own_acc[...].astype(bf16)
        own_ref[...] = own_low
        far_grad_ref[...] = total[:n_far].astype(bf16)
        local_grad_ref[...] = total[n_far:].astype(bf16)
        sent = sent_ref[...]
        parts = len(order)
        first = (2 * D + E) // parts
        second = E // parts
        whole = jnp.concatenate(
            [
                mm_tn(sent, own_low),
                mm_tn(far_ref[...], total[:n_far].astype(bf16)) + mm_tn(sent, total[n_far:].astype(bf16)),
                w1_acc[...],
            ],
            axis=0,
        ).astype(bf16)
        second_w = w2_acc[...].astype(bf16)
        third_w = w3_acc[...].astype(bf16)
        bias = bias_acc[...].astype(bf16)
        for q, n in enumerate(order):
            packed_ref[q, :first, :] = whole[n * first : (n + 1) * first]
            packed_ref[q, first : first + second, :] = second_w[n * second : (n + 1) * second]
            packed_ref[q, first + second : first + 2 * second, :] = third_w[n * second : (n + 1) * second]
            packed_ref[q, first + 2 * second :, :] = bias


def returned_kernel(own_ref, local_ref, back_ref, want_ref, out_ref):
    rows = local_ref.shape[0]
    near = local_ref[...].astype(f32) + mm_tn(pick_matrix(want_ref, rows), back_ref[...])
    out_ref[...] = jnp.concatenate([own_ref[...], near.astype(bf16)], axis=1)


def returned_last_kernel(own_ref, local_ref, back_ref, want_ref, w1_ref, out_ref):
    rows = local_ref.shape[0]
    near = local_ref[...].astype(f32) + mm_tn(pick_matrix(want_ref, rows), back_ref[...])
    grad = mm_nt(own_ref[...], w1_ref[:D, :]) + mm_nt(near.astype(bf16), w1_ref[D : 2 * D, :])
    out_ref[...] = grad.astype(bf16)


def node_backward_kernel(
    parts, place_ref, back_a, back_b, count_a, count_b, cot_ref, mask_ref, inv1_ref, normed2_ref, inv2_ref, ew1_ref,
    gain1_ref, gain2_ref, f2_far, slope_far, f1_far, normed1_far, w3_far, low_far, hid_far, total_far,
    mixed_ref, up_ref, bias_ref, packed_ref, w3_grad_ref,
    f2_ref, slope_ref, f1_ref, normed1_ref, w3_ref, low_ref, hid_ref, total_ref, arrivals,
):
    rows = cot_ref.shape[0]
    fetches = [
        pltpu.make_async_copy(source, target, arrivals.at[i])
        for i, (source, target) in enumerate(
            (
                (f2_far, f2_ref),
                (slope_far, slope_ref),
                (f1_far, f1_ref),
                (normed1_far, normed1_ref),
                (w3_far, w3_ref),
                (low_far, low_ref),
                (hid_far, hid_ref),
                (total_far, total_ref),
            )
        )
    ]
    for fetch in fetches:
        fetch.start()
    place = place_ref[0]
    present = present_column(mask_ref, rows)
    count = (count_a[...].astype(f32) + count_b[...].astype(f32))[:, :1]
    back = (back_a[...].astype(f32) + back_b[...].astype(f32)).astype(bf16)
    node_back = mm(back[:, :E], ew1_ref[:, :D]) + mm(back[:, E:], ew1_ref[:, D : 2 * D])
    up = present * (cot_ref[...].astype(f32) + node_back)
    normed2 = normed2_ref[...]
    sum_grad = norm_backward(up, normed2, inv2_ref[...], row_of(gain2_ref))
    branch_grad = sum_grad.astype(bf16)
    fetches[0].wait()
    fetches[1].wait()
    hidden_grad = (slope_ref[...].astype(f32) * mm_nt(branch_grad, f2_ref[...])).astype(bf16)
    fetches[2].wait()
    first_grad = sum_grad + mm_nt(hidden_grad, f1_ref[...])
    fetches[3].wait()
    normed1 = normed1_ref[...]
    mixed_grad = norm_backward(first_grad, normed1, inv1_ref[...], row_of(gain1_ref))
    mixed_ref[...] = mixed_grad
    message_grad = (mixed_grad / jnp.maximum(count, 1.0)).astype(bf16)
    fetches[4].wait()
    up_ref[...] = mm_nt(message_grad, w3_ref[...])
    row = iota((16, 1), 0)
    hidden_sum = column_sum(hidden_grad.astype(f32))
    bias = (
        jnp.where(row == 2, column_sum(count * message_grad.astype(f32)), 0.0)
        + jnp.where(row == 3, column_sum(first_grad * normed1), 0.0)
        + jnp.where(row == 4, column_sum(first_grad), 0.0)
        + jnp.where(row == 5, column_sum(branch_grad.astype(f32)), 0.0)
        + jnp.where(row == 6, column_sum(up * normed2), 0.0)
        + jnp.where(row == 7, column_sum(up), 0.0)
    )
    for j in range(FF // D):
        bias = bias + jnp.where(row == 8 + j, hidden_sum[:, j * D : (j + 1) * D], 0.0)
    bias_ref[...] = bias * (1.0 / parts)
    wide, narrow = FF // parts, D // parts
    for fetch in fetches[5:]:
        fetch.wait()
    low = low_ref[:, pl.ds(pl.multiple_of(place * narrow, narrow), narrow)]
    for j in range(FF // D):
        packed_ref[j * narrow : (j + 1) * narrow, :] = mm_tn(low, hidden_grad[:, j * D : (j + 1) * D]).astype(bf16)
    hid = hid_ref[:, pl.ds(pl.multiple_of(place * wide, wide), wide)]
    packed_ref[D : D + wide, :] = mm_tn(hid, branch_grad).astype(bf16)
    total = total_ref[:, pl.ds(pl.multiple_of(place * narrow, narrow), narrow)]
    w3_grad_ref[...] = mm_tn(total, message_grad).astype(bf16)
    at = D + wide
    packed_ref[at:, :] = jnp.zeros((packed_ref.shape[0] - at, D), bf16)


def message_backward_kernel(
    parts, core_ref, row_ref, edges_ref, act1_ref, d1_ref, d2_ref, up_ref, base_ref, nodes_ref, far_ref, w1_ref, w2_ref, node_bias_ref,
    out_ref, own_ref, far_grad_ref, local_grad_ref, kept_ref, given_ref,
    sums, w1_acc, w2_acc, bias_acc, own_acc, whole,
):
    step = pl.program_id(0)
    last = pl.num_programs(0) - 1
    kt, rows, _ = edges_ref.shape
    n_far = far_ref.shape[0]
    width = sums.shape[0]

    @pl.when(step == 0)
    def _():
        for acc in (sums, w1_acc, w2_acc, own_acc):
            acc[...] = jnp.zeros_like(acc)
        bias_acc[...] = node_bias_ref[...]

    edge = edges_ref[...].reshape(kt * rows, E)
    slope2 = d2_ref[...].astype(f32).reshape(kt, rows, D)
    low2 = (slope2 * up_ref[...][None]).astype(bf16).reshape(kt * rows, D)
    w2_acc[...] += mm_tn(act1_ref[...], low2)
    low1 = (d1_ref[...].astype(f32) * mm_nt(low2, w2_ref[...])).astype(bf16)
    w1_acc[...] += mm_tn(edge, low1)
    slot_sums(row_ref, step * kt, kt, width, low1, sums)
    grad = base_ref[...] + mm_nt(low1, w1_ref[2 * D :, :])
    out_ref[...] = grad.reshape(kt, rows, E)
    own_sum = gathered(low1.astype(f32), rows)
    own_acc[...] += own_sum
    row = iota((16, 1), 0)
    bias_acc[...] += jnp.where(row == 0, column_sum(own_sum), 0.0) + jnp.where(
        row == 1, column_sum(low2.astype(f32)), 0.0
    )

    @pl.when(step == last)
    def _():
        total = sums[...]
        own_low = own_acc[...].astype(bf16)
        own_ref[...] = own_low
        far_grad_ref[...] = total[:n_far].astype(bf16)
        local_grad_ref[...] = total[n_far:].astype(bf16)
        nodes = nodes_ref[...]
        first = (2 * D + E) // parts
        second = D // parts
        whole[:D, :] = mm_tn(nodes, own_low).astype(bf16)
        whole[D : 2 * D, :] = (
            mm_tn(far_ref[...], total[:n_far].astype(bf16)) + mm_tn(nodes, total[n_far:].astype(bf16))
        ).astype(bf16)
        whole[2 * D : 2 * D + E, :] = w1_acc[...].astype(bf16)
        whole[2 * D + E :, :] = w2_acc[...].astype(bf16)
        bias = bias_acc[...].astype(bf16)
        half = kept_ref.shape[0]
        for ref, side in ((kept_ref, core_ref[0]), (given_ref, 1 - core_ref[0])):
            for q in range(half):
                n = q * 2 + side
                ref[q, :first, :] = whole[pl.ds(pl.multiple_of(n * first, 16), first), :]
                ref[q, first : first + second, :] = whole[
                    pl.ds(pl.multiple_of(2 * D + E + n * second, 16), second), :
                ]
                ref[q, first + second : first + second + 16, :] = bias


def picked_lanes(rows, place, parts):
    wide = rows.shape[1] // parts
    out = jnp.zeros((rows.shape[0], wide), f32)
    for n in range(parts):
        out = out + jnp.where(place == n, rows[:, n * wide : (n + 1) * wide], 0.0)
    return out


def joined(whole, index, piece):
    rows = piece.shape[0]
    whole[pl.ds(pl.multiple_of(index * rows, 16), rows), :] = piece[...]


def node_weights_kernel(
    parts, half, at_ref, a0, a1, b0, b1, mixed_ref, back_a, back_b, nodes_ref,
    f1_ref, f2_ref, ew1_ref, ew2_ref, ew3_ref, eb1_ref, eb2_ref, eb3_ref, eg_ref, es_ref, whole,
):
    nodes_ref[...] = mixed_ref[...] + (back_a[...].astype(f32) + back_b[...].astype(f32))
    top = whole.shape[0] // 2
    low, high = whole.at[:top], whole.at[top:]
    joined(low, at_ref[1], a0)
    joined(low, 1 - at_ref[1], a1)
    joined(high, at_ref[2], b0)
    joined(high, 1 - at_ref[2], b1)
    place = at_ref[0]
    wide, narrow = FF // parts, D // parts
    for j in range(FF // D):
        f1_ref[:, j * D : (j + 1) * D] = whole[j * narrow : (j + 1) * narrow, :].astype(f32)
    at = D + wide
    f2_ref[...] = whole[D:at, :].astype(f32)
    edge = jnp.concatenate([whole[at : at + half, :E], whole[at : at + half, 256 : 256 + E]], axis=0).astype(f32)
    first, second = (2 * D + E) // parts, E // parts
    ew1_ref[...] = edge[:first].T
    ew2_ref[...] = edge[first : first + second]
    ew3_ref[...] = edge[first + second : first + 2 * second]
    rows = picked_lanes(edge[first + 2 * second : first + 2 * second + 8], place, parts)
    for j, ref in enumerate((eb1_ref, eb2_ref, eb3_ref, eg_ref, es_ref)):
        ref[...] = rows[j : j + 1].reshape(second)


def message_weights_kernel(parts, at_ref, p0, p1, p2, p3, w1_ref, w2_ref, w3_ref, *refs):
    *vectors, fb1_ref, whole = refs
    for mask, piece in enumerate((p0, p1, p2, p3)):
        joined(whole, at_ref[1] ^ mask, piece)
    place = at_ref[0]
    first, narrow = (2 * D + E) // parts, D // parts
    w1_ref[...] = whole[:first, :].astype(f32)
    w2_ref[...] = whole[first : first + narrow, :].astype(f32)
    w3_ref[...] = whole[first + narrow + 16 : first + 2 * narrow + 16, :].astype(f32)
    bias = whole[first + narrow : first + narrow + 16, :].astype(f32)
    rows = picked_lanes(bias[:8], place, parts)
    for j, ref in enumerate(vectors):
        ref[...] = rows[j : j + 1].reshape(narrow)
    hidden = jnp.zeros((1, D), f32)
    for n in range(FF // D):
        hidden = hidden + jnp.where(place == n, bias[8 + n : 9 + n], 0.0)
    fb1_ref[...] = hidden.reshape(FF // parts)


def swap(values, axis, bit):
    return lax.ppermute(values, axis, [(i, i ^ bit) for i in range(lax.axis_size(axis))])


def bits_of(axis):
    size, bit, out = lax.axis_size(axis), 1, []
    while bit < size:
        out.append(bit)
        bit *= 2
    return out


def add_low(a, b):
    return (a.astype(f32) + b.astype(f32)).astype(bf16)


def shared_sum(values, axis):
    bits = bits_of(axis)
    for bit in bits[:-1]:
        values = add_low(values, swap(values, axis, bit))
    return values, swap(values, axis, bits[-1])


def after(values, *earlier):
    return lax.optimization_barrier((values, *earlier))[0]


def halved_sum(values, axis, bit, dim=0):
    half = values.shape[dim] // 2
    side = (lax.axis_index(axis) // bit) & 1
    kept = lax.dynamic_slice_in_dim(values, side * half, half, dim)
    given = lax.dynamic_slice_in_dim(values, (1 - side) * half, half, dim)
    return add_low(kept, swap(given, axis, bit))


def rejoined(values, axis, bit, dim=0):
    other = swap(values, axis, bit)
    side = (lax.axis_index(axis) // bit) & 1
    return jnp.where(
        side == 0, jnp.concatenate([values, other], axis=dim), jnp.concatenate([other, values], axis=dim)
    )


def scattered_sum(values, axis, bits):
    for bit in bits:
        values = halved_sum(values, axis, bit)
    return values


def gathered_rows(values, axis, bits):
    for bit in bits:
        values = rejoined(values, axis, bit)
    return values


def total_of(addends, rows):
    total = 0.0
    for values, start in addends:
        total = total + lax.dynamic_slice_in_dim(values, start, rows, 0).astype(f32)
    return total.astype(bf16)


def halve(addends, rows, axis, bit):
    half = rows // 2
    side = (lax.axis_index(axis) // bit) & 1
    given = total_of([(values, start + (1 - side) * half) for values, start in addends], half)
    return [(values, start + side * half) for values, start in addends] + [(swap(given, axis, bit), 0)]


def quarter_sum(values, axis, bits):
    rows = values.shape[0] // 4
    low, high = ((lax.axis_index(axis) // bit) & 1 for bit in bits)
    mine = 2 * low + high
    total = lax.dynamic_slice_in_dim(values, mine * rows, rows, 0).astype(f32)
    for mask in (1, 2, 3):
        given = lax.dynamic_slice_in_dim(values, (mine ^ mask) * rows, rows, 0)
        total = total + swap(given, axis, (mask >> 1) * bits[0] + (mask & 1) * bits[1]).astype(f32)
    return total.astype(bf16)


def held_together(*lists):
    flat = []
    for item in lists:
        flat += [values for values, _ in item] if isinstance(item, list) else [item]
    flat = iter(lax.optimization_barrier(tuple(flat)))
    return tuple(
        [(next(flat), start) for _, start in item] if isinstance(item, list) else next(flat) for item in lists
    )


def quarters(values, axis, bits):
    return [values] + [swap(values, axis, (mask >> 1) * bits[0] + (mask & 1) * bits[1]) for mask in (1, 2, 3)]


def exchange(values, blocks):
    shaped = values.reshape((blocks, values.shape[0] // blocks) + values.shape[1:])
    return lax.all_to_all(shaped, "res", 0, 0, tiled=True).reshape(values.shape)


def call(kernel, outs, scratch=(), grid=None, in_specs=None, out_specs=None, cost=None):
    extra = {}
    if grid is not None:
        extra = dict(grid=grid, in_specs=in_specs, out_specs=out_specs)
    elif in_specs is not None:
        extra = dict(in_specs=in_specs)
    return pl.pallas_call(
        kernel,
        out_shape=outs,
        scratch_shapes=list(scratch),
        compiler_params=pltpu.CompilerParams(vmem_limit_bytes=VMEM),
        cost_estimate=cost,
        **extra,
    )


def shape(dims, dtype):
    return jax.ShapeDtypeStruct(dims, dtype)


def stored(dims, dtype):
    return pltpu.HBM(dims, dtype)


def read(*values):
    return tuple(pltpu.with_memory_space_constraint(value, pltpu.HBM) for value in values)


def up_to(value, unit):
    return -(-value // unit) * unit


def on_device(
    nodes,
    edges,
    neighbours,
    residue_mask,
    msg_w1,
    msg_b1,
    msg_w2,
    msg_b2,
    msg_w3,
    msg_b3,
    norm1_gain,
    norm1_bias,
    ffn_w1,
    ffn_b1,
    ffn_w2,
    ffn_b2,
    norm2_gain,
    norm2_bias,
    edge_w1,
    edge_b1,
    edge_w2,
    edge_b2,
    edge_w3,
    edge_b3,
    norm3_gain,
    norm3_bias,
    node_cot,
    edge_cot,
):
    rows, kn = neighbours.shape
    blocks, parts = lax.axis_size("res"), lax.axis_size("nbr")
    total = rows * kn
    n_far = blocks * FAR
    width = n_far + rows
    kt = next(t for t in (KT, 3, 1) if kn % t == 0)
    grid = (kn // kt,)
    nbr_bits = bits_of("nbr")
    order = tuple(
        sum(bit for i, bit in enumerate(nbr_bits) if (q >> (len(nbr_bits) - 1 - i)) & 1) for q in range(parts)
    )
    mask_row = residue_mask.reshape(1, rows)
    edges = edges.transpose(1, 0, 2)
    edge_cot = edge_cot.transpose(1, 0, 2)
    edge_w1 = edge_w1.T
    res_place = lax.axis_index("res").astype(jnp.int32).reshape(1)
    nbr_place = lax.axis_index("nbr").astype(jnp.int32).reshape(1)

    smem = pl.BlockSpec(memory_space=pltpu.SMEM)
    vmem = pl.BlockSpec(memory_space=pltpu.VMEM)

    def fixed(*dims):
        return pl.BlockSpec(dims, lambda i: (0,) * len(dims))

    def tiled(*dims):
        return pl.BlockSpec(dims, lambda i: (i,) + (0,) * (len(dims) - 1))

    place_row, place_col, want, counts = call(
        functools.partial(index_kernel, blocks),
        (
            shape((SLOT, rows), jnp.int32),
            shape((rows, SLOT), f32),
            shape((n_far, 128), bf16),
            shape((rows, 128), bf16),
        ),
        in_specs=[smem, vmem, vmem],
    )(res_place, *read(neighbours.T, mask_row))
    together = lax.optimization_barrier
    wanted = exchange(want, blocks)

    picks = (wanted[:, :1].astype(jnp.int32) == iota((n_far, rows), 1)).astype(bf16)
    far_nodes = exchange(mm(picks, nodes).astype(bf16), blocks)
    far_nodes, counts = together((far_nodes, counts))
    count_a, count_b = shared_sum(counts, "nbr")

    edge_tile = tiled(kt, rows, E)
    flat = tiled(kt * rows, D)
    flat_edge = tiled(kt * rows, E)
    act1, d1, d2, act_sum = call(
        message_forward_kernel,
        (stored((total, D), bf16), stored((total, D), bf16), stored((total, D), bf16), shape((rows, D), bf16)),
        scratch=[pltpu.VMEM((width, D), bf16), pltpu.VMEM((rows, D), f32), pltpu.VMEM((rows, D), f32)],
        grid=grid,
        in_specs=[
            fixed(rows, SLOT),
            edge_tile,
            fixed(rows, D),
            fixed(n_far, D),
            fixed(2 * D + E, D),
            fixed(D, D),
            fixed(D),
            fixed(D),
        ],
        out_specs=(flat, flat, flat, fixed(rows, D)),
        cost=pl.CostEstimate(flops=16 * total * D * D, bytes_accessed=total * D * 8, transcendentals=2 * total * D),
    )(*read(place_col, edges, nodes), far_nodes, *read(msg_w1, msg_w2, msg_b1, msg_b2))
    sum_a, sum_b = shared_sum(act_sum, "nbr")

    total_act, first_low, normed1, inv1, hidden, hidden_slope, normed2, inv2, sent, send = call(
        node_forward_kernel,
        (
            stored((rows, D), bf16),
            stored((rows, D), bf16),
            stored((rows, D), f32),
            stored((rows, 1), f32),
            stored((rows, FF), bf16),
            stored((rows, FF), bf16),
            stored((rows, D), f32),
            stored((rows, 1), f32),
            stored((rows, D), bf16),
            shape((n_far, D), bf16),
        ),
    )(sum_a, sum_b, count_a, count_b, nodes, mask_row, wanted, msg_w3, ffn_w1, ffn_w2,
      msg_b3, norm1_gain, norm1_bias, ffn_b1, ffn_b2, norm2_gain, norm2_bias)
    far_sent = exchange(send, blocks)

    first_rows, second_rows = (2 * D + E) // parts, E // parts
    edge_rows = up_to(first_rows + 2 * second_rows + 16, 32)
    edges_out, base, own_sum, far_sum, local_sum, edge_packed = call(
        functools.partial(edge_kernel, order),
        (
            shape((kn, rows, E), bf16),
            stored((total, E), f32),
            stored((rows, E), bf16),
            stored((n_far, E), bf16),
            stored((rows, E), bf16),
            shape((parts, edge_rows, E), bf16),
        ),
        scratch=[
            pltpu.VMEM((width, E), bf16),
            pltpu.VMEM((rows, E), f32),
            pltpu.VMEM((width, E), f32),
            pltpu.VMEM((E, E), f32),
            pltpu.VMEM((E, E), f32),
            pltpu.VMEM((E, E), f32),
            pltpu.VMEM((16, E), f32),
            pltpu.VMEM((rows, E), f32),
        ],
        grid=grid,
        in_specs=[
            fixed(SLOT, rows),
            fixed(rows, SLOT),
            edge_tile,
            edge_tile,
            fixed(rows, D),
            fixed(n_far, D),
            fixed(E, 2 * D + E),
            fixed(E, E),
            fixed(E, E),
        ]
        + [fixed(E)] * 5,
        out_specs=(
            edge_tile,
            flat_edge,
            fixed(rows, E),
            fixed(n_far, E),
            fixed(rows, E),
            fixed(parts, edge_rows, E),
        ),
        cost=pl.CostEstimate(flops=16 * total * D * D, bytes_accessed=total * E * 12, transcendentals=2 * total * E),
    )(*read(place_row, place_col, edges, edge_cot, sent), far_sent, *read(edge_w1, edge_w2, edge_w3),
      *read(edge_b1, edge_b2, edge_b3, norm3_gain, norm3_bias))

    far_back, edge_packed = together((exchange(far_sum, blocks), edge_packed))
    back = call(returned_kernel, shape((rows, 2 * E), bf16))(*read(own_sum, local_sum), far_back, wanted)
    for bit in nbr_bits[:-1]:
        back = add_low(back, swap(back, "nbr", bit))
    back, edge_packed = together((back, edge_packed))
    back_a, back_b = back, swap(back, "nbr", nbr_bits[-1])
    edge_part = scattered_sum(edge_packed, "nbr", nbr_bits).reshape(edge_rows, E)

    wide, narrow = FF // parts, D // parts
    node_rows = up_to(D + wide + edge_rows // 2, 16 * blocks)
    mixed_grad, up, node_bias, node_packed, msg_w3_part = call(
        functools.partial(node_backward_kernel, parts),
        (
            shape((rows, D), f32),
            shape((rows, D), f32),
            shape((16, D), f32),
            shape((node_rows, D), bf16),
            shape((narrow, D), bf16),
        ),
        scratch=[
            pltpu.VMEM((FF, D), bf16),
            pltpu.VMEM((rows, FF), bf16),
            pltpu.VMEM((D, FF), bf16),
            pltpu.VMEM((rows, D), f32),
            pltpu.VMEM((D, D), bf16),
            pltpu.VMEM((rows, D), bf16),
            pltpu.VMEM((rows, FF), bf16),
            pltpu.VMEM((rows, D), bf16),
            pltpu.SemaphoreType.DMA((8,)),
        ],
        in_specs=[smem] + [vmem] * 12 + [pl.BlockSpec(memory_space=pltpu.HBM)] * 8,
    )(
        nbr_place, back_a, back_b, count_a, count_b, *read(node_cot, mask_row, inv1, normed2, inv2, edge_w1),
        *read(norm1_gain, norm2_gain, ffn_w2, hidden_slope, ffn_w1, normed1, msg_w3, first_low, hidden, total_act),
    )
    bits = bits_of("res")
    order_a, order_b = bits, bits[1:2] + bits[:1] + bits[2:]
    rows_ab = node_rows // 2
    part_a = halve([(node_packed, 0)], rows_ab, "res", order_a[0])
    lead = D + wide - rows_ab
    edge_pair = jnp.pad(edge_part.reshape(2, edge_rows // 2, E), ((0, 0), (0, 0), (0, 256 - E)))
    edge_pair = jnp.concatenate([edge_pair[0], edge_pair[1]], axis=1)
    edge_pair = jnp.pad(edge_pair, ((lead, rows_ab - lead - edge_rows // 2), (0, 0)))
    part_b = halve([(node_packed, rows_ab), (edge_pair, 0)], rows_ab, "res", order_b[0])

    msg_rows = first_rows + narrow + 16
    share_rows = up_to(msg_rows + narrow, 8 * blocks)
    edges_grad, own_sum, far_sum, local_sum, msg_kept, msg_given = call(
        functools.partial(message_backward_kernel, parts),
        (
            shape((kn, rows, E), f32),
            shape((rows, D), bf16),
            shape((n_far, D), bf16),
            shape((rows, D), bf16),
            shape((parts // 2, msg_rows, D), bf16),
            shape((parts // 2, msg_rows, D), bf16),
        ),
        scratch=[
            pltpu.VMEM((width, D), f32),
            pltpu.VMEM((E, D), f32),
            pltpu.VMEM((D, D), f32),
            pltpu.VMEM((16, D), f32),
            pltpu.VMEM((rows, D), f32),
            pltpu.VMEM((3 * D + E, D), bf16),
        ],
        grid=grid,
        in_specs=[
            smem,
            fixed(SLOT, rows),
            edge_tile,
            flat,
            flat,
            flat,
            fixed(rows, D),
            flat_edge,
            fixed(rows, D),
            fixed(n_far, D),
            fixed(2 * D + E, D),
            fixed(D, D),
            fixed(16, D),
        ],
        out_specs=(edge_tile, fixed(rows, D), fixed(n_far, D), fixed(rows, D))
        + (fixed(parts // 2, msg_rows, D),) * 2,
        cost=pl.CostEstimate(flops=16 * total * D * D, bytes_accessed=total * D * 10, transcendentals=0),
    )(nbr_place & 1, *read(place_row, edges, act1, d1, d2), up, *read(base, nodes), far_nodes, *read(msg_w1, msg_w2), node_bias)

    far_sum, msg_kept, msg_given, part_a, part_b = held_together(far_sum, msg_kept, msg_given, part_a, part_b)
    flat_rows = parts // 2 * msg_rows
    msg_part = add_low(msg_kept, swap(msg_given, "nbr", 1)).reshape(flat_rows, D)
    part_a = halved_sum(total_of(part_a, rows_ab // 2), "res", order_a[1])
    part_b = halved_sum(total_of(part_b, rows_ab // 2), "res", order_b[1])
    middle, last = bits[2:-1], bits[-1]
    part_a = scattered_sum(part_a, "res", middle)
    part_b = scattered_sum(part_b, "res", middle)
    both = after(jnp.stack([part_a, part_b]), msg_part)
    msg_sum = scattered_sum(msg_part, "nbr", nbr_bits[1:])
    both = halved_sum(both, "res", last, 1)
    msg_sum = jnp.concatenate([msg_sum, msg_w3_part, jnp.zeros((share_rows - msg_rows - narrow, D), bf16)], axis=0)
    msg_quarter = quarter_sum(msg_sum, "res", bits[:2])
    both = rejoined(after(both, msg_sum) if 4 == 4 else both, "res", last, 1)
    far_back = exchange(after(far_sum, both), blocks)
    back = call(returned_last_kernel, shape((rows, D), bf16))(own_sum, local_sum, far_back, wanted, msg_w1)
    for bit in nbr_bits[:-1]:
        back = add_low(back, swap(back, "nbr", bit))
    back_b = swap(back, "nbr", nbr_bits[-1])
    msg_part = scattered_sum(msg_quarter, "res", middle)
    msg_part = add_low(msg_part, swap(msg_part, "res", last))
    part_a, part_b = after(both[0], msg_quarter), after(both[1], msg_quarter)
    part_a = rejoined(gathered_rows(part_a, "res", middle[::-1]), "res", order_a[1])
    part_b = rejoined(gathered_rows(part_b, "res", middle[::-1]), "res", order_b[1])
    part_a, part_b = after(part_a, msg_part), after(part_b, msg_part)
    other_a = swap(part_a, "res", order_a[0])
    other_b = swap(part_b, "res", order_b[0])
    msg_parts = quarters(gathered_rows(msg_part, "res", middle[::-1]), "res", bits[:2])

    def side(bit):
        return (lax.axis_index("res") // bit) & 1

    node_at = jnp.stack([lax.axis_index("nbr"), side(order_a[0]), side(order_b[0])]).astype(jnp.int32)
    msg_at = jnp.stack([lax.axis_index("nbr"), 2 * side(bits[0]) + side(bits[1])]).astype(jnp.int32)
    (
        nodes_grad, ffn_w1_grad, ffn_w2_grad, edge_w1_grad, edge_w2_grad, edge_w3_grad,
        edge_b1_grad, edge_b2_grad, edge_b3_grad, norm3_gain_grad, norm3_bias_grad,
    ) = call(
        functools.partial(node_weights_kernel, parts, edge_rows // 2),
        (
            shape((rows, D), f32),
            shape((narrow, FF), f32),
            shape((wide, D), f32),
            shape((E, first_rows), f32),
            shape((second_rows, E), f32),
            shape((second_rows, E), f32),
        )
        + (shape((second_rows,), f32),) * 5,
        scratch=[pltpu.VMEM((node_rows, D), bf16)],
        in_specs=[smem] + [vmem] * 7,
    )(node_at, part_a, other_a, part_b, other_b, mixed_grad, back, back_b)
    (
        msg_w1_grad, msg_w2_grad, msg_w3_grad, msg_b1_grad, msg_b2_grad, msg_b3_grad, norm1_gain_grad, norm1_bias_grad,
        ffn_b2_grad, norm2_gain_grad, norm2_bias_grad, ffn_b1_grad,
    ) = call(
        functools.partial(message_weights_kernel, parts),
        (shape((first_rows, D), f32), shape((narrow, D), f32), shape((narrow, D), f32))
        + (shape((narrow,), f32),) * 8
        + (shape((wide,), f32),),
        scratch=[pltpu.VMEM((share_rows, D), bf16)],
        in_specs=[smem] + [vmem] * 4,
    )(msg_at, *msg_parts)
    return (
        sent,
        edges_out.transpose(1, 0, 2),
        nodes_grad,
        edges_grad.transpose(1, 0, 2),
        msg_w1_grad,
        msg_b1_grad,
        msg_w2_grad,
        msg_b2_grad,
        msg_w3_grad,
        msg_b3_grad,
        norm1_gain_grad,
        norm1_bias_grad,
        ffn_w1_grad,
        ffn_b1_grad,
        ffn_w2_grad,
        ffn_b2_grad,
        norm2_gain_grad,
        norm2_bias_grad,
        edge_w1_grad.T,
        edge_b1_grad,
        edge_w2_grad,
        edge_b2_grad,
        edge_w3_grad,
        edge_b3_grad,
        norm3_gain_grad,
        norm3_bias_grad,
    )


def solution(mesh):
    every = P()
    in_specs = (
        (P("res", None), P("res", "nbr", None), P("res", "nbr"), P("res"))
        + (every,) * 22
        + (P("res", None), P("res", "nbr", None))
    )
    matrix, vector = P("nbr", None), P("nbr")
    out_specs = (
        (P("res", None), P("res", "nbr", None), P("res", None), P("res", "nbr", None))
        + (matrix, vector) * 3
        + (vector, vector, matrix, vector, matrix, vector, vector, vector)
        + (matrix, vector) * 3
        + (vector, vector)
    )
    return jax.shard_map(on_device, mesh=mesh, in_specs=in_specs, out_specs=out_specs, check_vma=False)
```

```python
import functools

import jax
import jax.numpy as jnp
from jax import lax
from jax.experimental import pallas as pl
from jax.experimental.pallas import tpu as pltpu
from jax.sharding import PartitionSpec as P

D = 512
E = 192
FF = 2048
FAR = 32
SLOT = 16
KT = 5
VMEM = 32 * 1024 * 1024

bf16 = jnp.bfloat16
f32 = jnp.float32


def mm(a, b):
    return jnp.dot(a, b, preferred_element_type=f32)


def mm_tn(a, b):
    return lax.dot_general(a, b, (((0,), (0,)), ((), ())), preferred_element_type=f32)


def mm_nt(a, b):
    return lax.dot_general(a, b, (((1,), (1,)), ((), ())), preferred_element_type=f32)


def gelu_pair(v):
    c0 = 0.7978845608028654
    c1 = 0.044715 * c0
    square = v * v
    t = jnp.tanh(v * (c0 + c1 * square))
    half = 0.5 + 0.5 * t
    act = v * half
    return act, half + act * (1.0 - t) * (c0 + (3.0 * c1) * square)


def gelu(v):
    t = jnp.tanh(v * (0.7978845608028654 + (0.044715 * 0.7978845608028654) * (v * v)))
    half = 0.5 * v
    return half + half * t


def norm_forward(values):
    centred = values - jnp.mean(values, axis=-1, keepdims=True)
    inverse = lax.rsqrt(jnp.mean(centred * centred, axis=-1, keepdims=True) + 1e-05)
    return centred * inverse, inverse


def norm_backward(upstream, normed, inverse, gain):
    scaled = upstream * gain
    first = jnp.mean(scaled, axis=-1, keepdims=True)
    second = jnp.mean(scaled * normed, axis=-1, keepdims=True)
    return inverse * (scaled - first - normed * second)


def row_of(ref):
    return ref[...].astype(f32).reshape(1, ref.shape[0])


def column_sum(values):
    return jnp.sum(values, axis=0, keepdims=True)


def iota(shape, dim):
    return lax.broadcasted_iota(jnp.int32, shape, dim)


def present_column(mask_ref, rows):
    real = jnp.sum(mask_ref[...].astype(f32), axis=1, keepdims=True)
    return (iota((rows, 1), 0).astype(f32) < real).astype(f32)


def pick_matrix(want_ref, rows):
    want = want_ref[...][:, :1].astype(f32)
    return (want == iota((want.shape[0], rows), 1).astype(f32)).astype(bf16)


def one_hot(column, width):
    return (column == iota((column.shape[0], width), 1)).astype(bf16)


def columns_of(col_ref, first, count):
    values = col_ref[...]
    lane = iota(values.shape, 1)
    return [
        jnp.sum(jnp.where(lane == first + j, values, 0.0), axis=1, keepdims=True).astype(jnp.int32)
        for j in range(count)
    ]


def kept_weight(columns):
    return jnp.concatenate([(column >= 0).astype(f32) for column in columns], axis=0)


def spread(rows, values):
    n, c = rows.shape
    return (values.reshape(-1, n, c) + rows[None]).reshape(values.shape)


def gathered(values, n):
    return jnp.sum(values.reshape(-1, n, values.shape[1]), axis=0)


def slot_sums(row_ref, first, count, width, values, acc):
    n = row_ref.shape[1]
    for j in range(count):
        row = row_ref[pl.ds(first + j, 1), :]
        hot = (row == iota((width, n), 0)).astype(bf16)
        acc[...] += mm(hot, values[j * n : (j + 1) * n])


def index_kernel(blocks, me_ref, near_ref, mask_ref, row_ref, col_ref, want_ref, count_ref):
    kn, rows = near_ref.shape
    me = me_ref[0].astype(f32)
    lanes = max(16, blocks)
    index = near_ref[...].astype(f32)
    block = jnp.floor((index + 0.5) * (1.0 / rows))
    slot = index - block * rows
    local = block == me
    far_block = jnp.where(local, -1.0, block)
    real = jnp.sum(mask_ref[...].astype(f32), axis=1, keepdims=True)
    own_place = iota((kn, rows), 1).astype(f32)
    kept = jnp.logical_and(jnp.logical_or(jnp.logical_not(local), slot < real), own_place < real)
    slot_line = iota((rows, rows), 0).astype(f32)
    block_line = iota((lanes, rows), 0).astype(f32)
    hot_slot = [(slot[k : k + 1] == slot_line).astype(bf16) for k in range(kn)]
    hot_block = [(far_block[k : k + 1] == block_line).astype(bf16) for k in range(kn)]
    named = mm_nt(hot_block[0], hot_slot[0])
    for k in range(1, kn):
        named = named + mm_nt(hot_block[k], hot_slot[k])
    flags = (named > 0.0).astype(f32)
    before = (iota((rows, rows), 0) < iota((rows, rows), 1)).astype(bf16)
    rank = mm(flags.astype(bf16), before)
    key = jnp.where(flags > 0.0, rank, -1.0)[:blocks]
    key = jnp.broadcast_to(key[:, None, :], (blocks, FAR, rows)).reshape(blocks * FAR, rows)
    level = (iota((blocks * FAR, 1), 0) & (FAR - 1)).astype(f32)
    hit = (key == level).astype(f32)
    place_row = iota((blocks * FAR, rows), 1).astype(f32)
    want = jnp.sum(hit * place_row, axis=1, keepdims=True)
    found = jnp.sum(hit, axis=1, keepdims=True)
    want = jnp.where(found > 0.0, want, 255.0)
    want_ref[...] = jnp.broadcast_to(want, want_ref.shape).astype(bf16)
    after = (iota((rows, rows), 0) > iota((rows, rows), 1)).astype(bf16)
    rank_down = mm_nt(after, flags.astype(bf16)).astype(bf16)
    edge_rank = jnp.concatenate(
        [
            jnp.sum(mm(rank_down, hot_block[k]) * hot_slot[k].astype(f32), axis=0, keepdims=True)
            for k in range(kn)
        ],
        axis=0,
    )
    place = jnp.where(local, blocks * FAR + slot, block * FAR + edge_rank)
    place = jnp.where(kept, place, -1.0)
    place = jnp.concatenate([place, jnp.full((SLOT - kn, rows), -1.0, f32)], axis=0)
    row_ref[...] = place.astype(jnp.int32)
    col_ref[...] = place.T
    counts = jnp.sum((col_ref[...] >= 0.0).astype(f32), axis=1, keepdims=True)
    count_ref[...] = jnp.broadcast_to(counts, count_ref.shape).astype(bf16)


def message_forward_kernel(
    col_ref, edges_ref, nodes_ref, far_ref, w1_ref, w2_ref, b1_ref, b2_ref,
    act1_ref, pre1_ref, pre2_ref, sum_ref, table, own, acc,
):
    step = pl.program_id(0)
    last = pl.num_programs(0) - 1
    kt, rows, _ = edges_ref.shape
    n_far = far_ref.shape[0]
    width = table.shape[0]

    @pl.when(step == 0)
    def _():
        weight = w1_ref[D : 2 * D, :]
        table[:n_far] = mm(far_ref[...], weight).astype(bf16)
        table[n_far:] = mm(nodes_ref[...], weight).astype(bf16)
        own[...] = mm(nodes_ref[...], w1_ref[:D, :]) + row_of(b1_ref)
        acc[...] = jnp.zeros_like(acc)

    edge = edges_ref[...].reshape(kt * rows, E)
    columns = columns_of(col_ref, step * kt, kt)
    hot = jnp.concatenate([one_hot(column, width) for column in columns], axis=0)
    pre1 = spread(own[...], mm(hot, table[...]) + mm(edge, w1_ref[2 * D :, :]))
    pre1_ref[...] = pre1.astype(bf16)
    act1 = gelu(pre1).astype(bf16)
    act1_ref[...] = act1
    pre2 = jnp.where(kept_weight(columns) > 0.0, mm(act1, w2_ref[...]) + row_of(b2_ref), -30.0)
    pre2_ref[...] = pre2.astype(bf16)
    acc[...] += gathered(gelu(pre2), rows)

    @pl.when(step == last)
    def _():
        sum_ref[...] = acc[...].astype(bf16)


def slope_kernel(pre_ref, slope_ref):
    slope_ref[...] = gelu_pair(pre_ref[...].astype(f32))[1].astype(bf16)


def node_forward_kernel(
    sum_a, sum_b, count_a, count_b, nodes_ref, mask_ref, want_ref, w3_ref, f1_ref, f2_ref,
    b3_ref, gain1_ref, bias1_ref, fb1_ref, fb2_ref, gain2_ref, bias2_ref,
    total_ref, low_ref, normed1_ref, inv1_ref, hid_ref, slope_ref, normed2_ref, inv2_ref, sent_ref, send_ref,
):
    rows = nodes_ref.shape[0]
    present = present_column(mask_ref, rows)
    count = count_a[...].astype(f32) + count_b[...].astype(f32)
    count = count[:, :1]
    total = sum_a[...].astype(f32) + sum_b[...].astype(f32)
    high = total.astype(bf16)
    total_ref[...] = high
    rest = (total - high.astype(f32)).astype(bf16)
    summed = mm(high, w3_ref[...]) + mm(rest, w3_ref[...]) + count * row_of(b3_ref)
    mixed = nodes_ref[...].astype(f32) + summed / jnp.maximum(count, 1.0)
    normed, inverse = norm_forward(mixed)
    normed1_ref[...] = normed
    inv1_ref[...] = inverse
    first = normed * row_of(gain1_ref) + row_of(bias1_ref)
    low = first.astype(bf16)
    low_ref[...] = low
    act, slope = gelu_pair(mm(low, f1_ref[...]) + row_of(fb1_ref))
    act = act.astype(bf16)
    hid_ref[...] = act
    slope_ref[...] = slope.astype(bf16)
    branch = mm(act, f2_ref[...]) + row_of(fb2_ref)
    normed, inverse = norm_forward(first + branch)
    normed2_ref[...] = normed
    inv2_ref[...] = inverse
    sent = (present * (normed * row_of(gain2_ref) + row_of(bias2_ref))).astype(bf16)
    sent_ref[...] = sent
    send_ref[...] = mm(pick_matrix(want_ref, rows), sent).astype(bf16)


def edge_kernel(
    row_ref, col_ref, edges_ref, cot_ref, sent_ref, far_ref, w1_ref, w2_ref, w3_ref, b1_ref, b2_ref, b3_ref, gain_ref, shift_ref,
    out_ref, base_ref, own_ref, far_grad_ref, local_grad_ref, w1_acc, w2_acc, w3_acc, bias_acc,
    table, own, sums, own_acc,
):
    step = pl.program_id(0)
    last = pl.num_programs(0) - 1
    kt, rows, _ = edges_ref.shape
    n_far = far_ref.shape[0]
    width = table.shape[0]

    @pl.when(step == 0)
    def _():
        weight = w1_ref[:, D : 2 * D]
        table[:n_far] = mm_nt(far_ref[...], weight).astype(bf16)
        table[n_far:] = mm_nt(sent_ref[...], weight).astype(bf16)
        own[...] = mm_nt(sent_ref[...], w1_ref[:, :D]) + row_of(b1_ref)
        for acc in (sums, w1_acc, w2_acc, w3_acc, bias_acc, own_acc):
            acc[...] = jnp.zeros_like(acc)

    edge = edges_ref[...].reshape(kt * rows, E)
    cot = cot_ref[...].reshape(kt * rows, E)
    columns = columns_of(col_ref, step * kt, kt)
    hot = jnp.concatenate([one_hot(column, width) for column in columns], axis=0)
    edge_weight = w1_ref[:, 2 * D :]
    pre1 = spread(own[...], mm(hot, table[...]) + mm_nt(edge, edge_weight))
    act, slope1 = gelu_pair(pre1)
    act1 = act.astype(bf16)
    act, slope2 = gelu_pair(mm(act1, w2_ref[...]) + row_of(b2_ref))
    act2 = act.astype(bf16)
    branch = mm(act2, w3_ref[...]) + row_of(b3_ref)
    weight = kept_weight(columns)
    normed, inverse = norm_forward(edge.astype(f32) + branch)
    gain = row_of(gain_ref)
    out = weight * (normed * gain + row_of(shift_ref))
    out_ref[...] = out.astype(bf16).reshape(kt, rows, E)
    up = weight * cot.astype(f32)
    grad = norm_backward(up, normed, inverse, gain)
    low3 = grad.astype(bf16)
    w3_acc[...] += mm_tn(act2, low3)
    low2 = (slope2 * mm_nt(low3, w3_ref[...])).astype(bf16)
    w2_acc[...] += mm_tn(act1, low2)
    low1 = (slope1 * mm_nt(low2, w2_ref[...])).astype(bf16)
    w1_acc[...] += mm_tn(edge, low1)
    slot_sums(row_ref, step * kt, kt, width, low1, sums)
    base_ref[...] = grad + mm(low1, edge_weight)
    own_sum = gathered(low1.astype(f32), rows)
    own_acc[...] += own_sum
    row = iota((16, 1), 0)
    bias_acc[...] += (
        jnp.where(row == 0, column_sum(own_sum), 0.0)
        + jnp.where(row == 1, column_sum(low2.astype(f32)), 0.0)
        + jnp.where(row == 2, column_sum(low3.astype(f32)), 0.0)
        + jnp.where(row == 3, column_sum(up * normed), 0.0)
        + jnp.where(row == 4, column_sum(up), 0.0)
    )

    @pl.when(step == last)
    def _():
        total = sums[...]
        own_ref[...] = own_acc[...].astype(bf16)
        far_grad_ref[...] = total[:n_far].astype(bf16)
        local_grad_ref[...] = total[n_far:].astype(bf16)


def edge_weights_kernel(
    order, sent_ref, far_ref, own_ref, far_grad_ref, local_grad_ref, w1_ref, w2_ref, w3_ref, bias_ref, packed_ref
):
    parts = len(order)
    first, second = (2 * D + E) // parts, E // parts
    sent = sent_ref[...]
    whole = jnp.concatenate(
        [
            mm_tn(sent, own_ref[...]),
            mm_tn(far_ref[...], far_grad_ref[...]) + mm_tn(sent, local_grad_ref[...]),
            w1_ref[...],
        ],
        axis=0,
    ).astype(bf16)
    second_w = w2_ref[...].astype(bf16)
    third_w = w3_ref[...].astype(bf16)
    bias = bias_ref[...].astype(bf16)
    half = packed_ref.shape[1]
    for q, n in enumerate(order):
        rows = jnp.concatenate(
            [
                whole[n * first : (n + 1) * first],
                second_w[n * second : (n + 1) * second],
                third_w[n * second : (n + 1) * second],
                bias,
            ],
            axis=0,
        )
        packed_ref[q, :, :E] = rows[:half]
        packed_ref[q, :, 256 : 256 + E] = rows[half:]
        packed_ref[q, :, E:256] = jnp.zeros((half, 256 - E), bf16)
        packed_ref[q, :, 256 + E :] = jnp.zeros((half, 256 - E), bf16)


def returned_kernel(own_ref, local_ref, back_ref, want_ref, out_ref):
    rows = local_ref.shape[0]
    near = local_ref[...].astype(f32) + mm_tn(pick_matrix(want_ref, rows), back_ref[...])
    out_ref[...] = jnp.concatenate([own_ref[...], near.astype(bf16)], axis=1)


def returned_last_kernel(own_ref, local_ref, back_ref, want_ref, w1_ref, out_ref):
    rows = local_ref.shape[0]
    near = local_ref[...].astype(f32) + mm_tn(pick_matrix(want_ref, rows), back_ref[...])
    grad = mm_nt(own_ref[...], w1_ref[:D, :]) + mm_nt(near.astype(bf16), w1_ref[D : 2 * D, :])
    out_ref[...] = grad.astype(bf16)


def fetch_kernel(*refs):
    *refs, arrivals = refs
    count = len(refs) // 2
    copies = [pltpu.make_async_copy(refs[i], refs[count + i], arrivals.at[i]) for i in range(count)]
    for copy in copies:
        copy.start()
    for copy in copies:
        copy.wait()


def fetched(*values):
    size = sum(value.size * value.dtype.itemsize for value in values)
    return pl.pallas_call(
        fetch_kernel,
        out_shape=tuple(pltpu.VMEM(value.shape, value.dtype) for value in values),
        in_specs=[pl.BlockSpec(memory_space=pltpu.HBM)] * len(values),
        out_specs=tuple(pl.BlockSpec(memory_space=pltpu.VMEM) for _ in values),
        scratch_shapes=[pltpu.SemaphoreType.DMA((len(values),))],
        compiler_params=pltpu.CompilerParams(vmem_limit_bytes=VMEM),
        cost_estimate=pl.CostEstimate(flops=0, bytes_accessed=2 * size, transcendentals=0),
    )(*read(*values))


def node_backward_kernel(
    parts, place_ref, back_a, back_b, count_a, count_b, cot_ref, normed2_ref, ew1_ref, f2_ref, slope_ref, f1_ref,
    normed1_ref, w3_ref, low_ref, hid_ref, total_ref, mask_ref, inv1_ref, inv2_ref, gain1_ref, gain2_ref,
    mixed_ref, up_ref, bias_ref, packed_ref,
):
    rows = cot_ref.shape[0]
    place = place_ref[0]
    present = present_column(mask_ref, rows)
    count = (count_a[...].astype(f32) + count_b[...].astype(f32))[:, :1]
    back = (back_a[...].astype(f32) + back_b[...].astype(f32)).astype(bf16)
    node_back = mm(back[:, :E], ew1_ref[:, :D]) + mm(back[:, E:], ew1_ref[:, D : 2 * D])
    up = present * (cot_ref[...].astype(f32) + node_back)
    normed2 = normed2_ref[...]
    sum_grad = norm_backward(up, normed2, inv2_ref[...], row_of(gain2_ref))
    branch_grad = sum_grad.astype(bf16)
    hidden_grad = (slope_ref[...].astype(f32) * mm_nt(branch_grad, f2_ref[...])).astype(bf16)
    first_grad = sum_grad + mm_nt(hidden_grad, f1_ref[...])
    normed1 = normed1_ref[...]
    mixed_grad = norm_backward(first_grad, normed1, inv1_ref[...], row_of(gain1_ref))
    mixed_ref[...] = mixed_grad
    message_grad = (mixed_grad / jnp.maximum(count, 1.0)).astype(bf16)
    up_ref[...] = mm_nt(message_grad, w3_ref[...])
    row = iota((16, 1), 0)
    hidden_sum = column_sum(hidden_grad.astype(f32))
    bias = (
        jnp.where(row == 2, column_sum(count * message_grad.astype(f32)), 0.0)
        + jnp.where(row == 3, column_sum(first_grad * normed1), 0.0)
        + jnp.where(row == 4, column_sum(first_grad), 0.0)
        + jnp.where(row == 5, column_sum(branch_grad.astype(f32)), 0.0)
        + jnp.where(row == 6, column_sum(up * normed2), 0.0)
        + jnp.where(row == 7, column_sum(up), 0.0)
    )
    for j in range(FF // D):
        bias = bias + jnp.where(row == 8 + j, hidden_sum[:, j * D : (j + 1) * D], 0.0)
    bias_ref[...] = bias * (1.0 / parts)
    wide, narrow = FF // parts, D // parts
    low = low_ref[:, pl.ds(pl.multiple_of(place * narrow, narrow), narrow)]
    for j in range(FF // D):
        packed_ref[j * narrow : (j + 1) * narrow, :] = mm_tn(low, hidden_grad[:, j * D : (j + 1) * D]).astype(bf16)
    hid = hid_ref[:, pl.ds(pl.multiple_of(place * wide, wide), wide)]
    packed_ref[D : D + wide, :] = mm_tn(hid, branch_grad).astype(bf16)
    total = total_ref[:, pl.ds(pl.multiple_of(place * narrow, narrow), narrow)]
    packed_ref[D + wide : D + wide + narrow, :] = mm_tn(total, message_grad).astype(bf16)
    at = D + wide + narrow
    if packed_ref.shape[0] > at:
        packed_ref[at:, :] = jnp.zeros((packed_ref.shape[0] - at, D), bf16)


def message_backward_kernel(
    parts, core_ref, row_ref, edges_ref, act1_ref, d1_ref, d2_ref, up_ref, base_ref, nodes_ref, far_ref, w1_ref, w2_ref, node_bias_ref,
    out_ref, own_ref, far_grad_ref, local_grad_ref, kept_ref, given_ref,
    sums, w1_acc, w2_acc, bias_acc, own_acc, whole,
):
    step = pl.program_id(0)
    last = pl.num_programs(0) - 1
    kt, rows, _ = edges_ref.shape
    n_far = far_ref.shape[0]
    width = sums.shape[0]

    @pl.when(step == 0)
    def _():
        for acc in (sums, w1_acc, w2_acc, own_acc):
            acc[...] = jnp.zeros_like(acc)
        bias_acc[...] = node_bias_ref[...]

    edge = edges_ref[...].reshape(kt * rows, E)
    slope2 = d2_ref[...].astype(f32).reshape(kt, rows, D)
    grad2 = (slope2 * up_ref[...][None]).reshape(kt * rows, D)
    low2 = grad2.astype(bf16)
    w2_acc[...] += mm_tn(act1_ref[...], low2)
    grad1 = d1_ref[...].astype(f32) * mm_nt(low2, w2_ref[...])
    low1 = grad1.astype(bf16)
    w1_acc[...] += mm_tn(edge, low1)
    slot_sums(row_ref, step * kt, kt, width, low1, sums)
    grad = base_ref[...] + mm_nt(low1, w1_ref[2 * D :, :])
    out_ref[...] = grad.reshape(kt, rows, E)
    own_sum = gathered(grad1, rows)
    own_acc[...] += own_sum
    row = iota((16, 1), 0)
    bias_acc[...] += jnp.where(row == 0, column_sum(own_sum), 0.0) + jnp.where(
        row == 1, column_sum(grad2), 0.0
    )

    @pl.when(step == last)
    def _():
        total = sums[...]
        own_low = own_acc[...].astype(bf16)
        own_ref[...] = own_low
        far_grad_ref[...] = total[:n_far].astype(bf16)
        local_grad_ref[...] = total[n_far:].astype(bf16)
        nodes = nodes_ref[...]
        first = (2 * D + E) // parts
        second = D // parts
        whole[:D, :] = mm_tn(nodes, own_low).astype(bf16)
        whole[D : 2 * D, :] = (
            mm_tn(far_ref[...], total[:n_far].astype(bf16)) + mm_tn(nodes, total[n_far:].astype(bf16))
        ).astype(bf16)
        whole[2 * D : 2 * D + E, :] = w1_acc[...].astype(bf16)
        whole[2 * D + E :, :] = w2_acc[...].astype(bf16)
        bias = bias_acc[...].astype(bf16)
        half = kept_ref.shape[0]
        for ref, side in ((kept_ref, core_ref[0]), (given_ref, 1 - core_ref[0])):
            for q in range(half):
                n = q * 2 + side
                ref[q, :first, :] = whole[pl.ds(pl.multiple_of(n * first, 16), first), :]
                ref[q, first : first + second, :] = whole[
                    pl.ds(pl.multiple_of(2 * D + E + n * second, 16), second), :
                ]
                ref[q, first + second : first + second + 16, :] = bias


def picked_lanes(rows, place, parts):
    wide = rows.shape[1] // parts
    out = jnp.zeros((rows.shape[0], wide), f32)
    for n in range(parts):
        out = out + jnp.where(place == n, rows[:, n * wide : (n + 1) * wide], 0.0)
    return out


def joined(whole, index, piece):
    rows = piece.shape[0]
    whole[pl.ds(pl.multiple_of(index * rows, 16), rows), :] = piece[...]


def node_weights_kernel(
    parts, at_ref, a0, a1, b0, b1, mixed_ref, back_a, back_b, nodes_ref, f1_ref, f2_ref, w3_ref, whole
):
    nodes_ref[...] = mixed_ref[...] + (back_a[...].astype(f32) + back_b[...].astype(f32))
    top = whole.shape[0] // 2
    low, high = whole.at[:top], whole.at[top:]
    joined(low, at_ref[0], a0)
    joined(low, 1 - at_ref[0], a1)
    joined(high, at_ref[1], b0)
    joined(high, 1 - at_ref[1], b1)
    wide, narrow = FF // parts, D // parts
    for j in range(FF // D):
        f1_ref[:, j * D : (j + 1) * D] = whole[j * narrow : (j + 1) * narrow, :].astype(f32)
    f2_ref[...] = whole[D : D + wide, :].astype(f32)
    w3_ref[...] = whole[D + wide : D + wide + narrow, :].astype(f32)


def edge_message_weights_kernel(
    parts, half, at_ref, p0, p1, p2, p3, w1_ref, w2_ref, ew1_ref, ew2_ref, ew3_ref, *refs
):
    *vectors, fb1_ref, whole = refs
    for mask, piece in enumerate((p0, p1, p2, p3)):
        joined(whole, at_ref[1] ^ mask, piece)
    place = at_ref[0]
    first, narrow, second = (2 * D + E) // parts, D // parts, E // parts
    w1_ref[...] = whole[:first, :].astype(f32)
    w2_ref[...] = whole[first : first + narrow, :].astype(f32)
    at = first + narrow
    bias = whole[at : at + 16, :].astype(f32)
    rows = picked_lanes(bias[:8], place, parts)
    for j, ref in enumerate(vectors[5:]):
        ref[...] = rows[j : j + 1].reshape(narrow)
    hidden = jnp.zeros((1, D), f32)
    for n in range(FF // D):
        hidden = hidden + jnp.where(place == n, bias[8 + n : 9 + n], 0.0)
    fb1_ref[...] = hidden.reshape(FF // parts)
    at += 16
    edge = jnp.concatenate([whole[at : at + half, :E], whole[at : at + half, 256 : 256 + E]], axis=0).astype(f32)
    ew1_ref[...] = edge[:first].T
    ew2_ref[...] = edge[first : first + second]
    ew3_ref[...] = edge[first + second : first + 2 * second]
    rows = picked_lanes(edge[first + 2 * second : first + 2 * second + 8], place, parts)
    for j, ref in enumerate(vectors[:5]):
        ref[...] = rows[j : j + 1].reshape(second)


def swap(values, axis, bit):
    return lax.ppermute(values, axis, [(i, i ^ bit) for i in range(lax.axis_size(axis))])


def bits_of(axis):
    size, bit, out = lax.axis_size(axis), 1, []
    while bit < size:
        out.append(bit)
        bit *= 2
    return out


def add_low(a, b):
    return (a.astype(f32) + b.astype(f32)).astype(bf16)


def shared_sum(values, axis):
    bits = bits_of(axis)
    for bit in bits[:-1]:
        values = add_low(values, swap(values, axis, bit))
    return values, swap(values, axis, bits[-1])


def after(values, *earlier):
    return lax.optimization_barrier((values, *earlier))[0]


def halved_sum(values, axis, bit, dim=0):
    half = values.shape[dim] // 2
    side = (lax.axis_index(axis) // bit) & 1
    kept = lax.dynamic_slice_in_dim(values, side * half, half, dim)
    given = lax.dynamic_slice_in_dim(values, (1 - side) * half, half, dim)
    return add_low(kept, swap(given, axis, bit))


def rejoined(values, axis, bit, dim=0):
    other = swap(values, axis, bit)
    side = (lax.axis_index(axis) // bit) & 1
    return jnp.where(
        side == 0, jnp.concatenate([values, other], axis=dim), jnp.concatenate([other, values], axis=dim)
    )


def scattered_sum(values, axis, bits):
    for bit in bits:
        values = halved_sum(values, axis, bit)
    return values


def gathered_rows(values, axis, bits):
    for bit in bits:
        values = rejoined(values, axis, bit)
    return values


def total_of(addends, rows):
    total = 0.0
    for values, start in addends:
        total = total + lax.dynamic_slice_in_dim(values, start, rows, 0).astype(f32)
    return total.astype(bf16)


def halve(addends, rows, axis, bit):
    half = rows // 2
    side = (lax.axis_index(axis) // bit) & 1
    given = total_of([(values, start + (1 - side) * half) for values, start in addends], half)
    return [(values, start + side * half) for values, start in addends] + [(swap(given, axis, bit), 0)]


def quarter_sum(values, axis, bits):
    rows = values.shape[0] // 4
    low, high = ((lax.axis_index(axis) // bit) & 1 for bit in bits)
    mine = 2 * low + high
    total = lax.dynamic_slice_in_dim(values, mine * rows, rows, 0).astype(f32)
    for mask in (1, 2, 3):
        given = lax.dynamic_slice_in_dim(values, (mine ^ mask) * rows, rows, 0)
        total = total + swap(given, axis, (mask >> 1) * bits[0] + (mask & 1) * bits[1]).astype(f32)
    return total.astype(bf16)


def held_together(*lists):
    flat = []
    for item in lists:
        flat += [values for values, _ in item] if isinstance(item, list) else [item]
    flat = iter(lax.optimization_barrier(tuple(flat)))
    return tuple(
        [(next(flat), start) for _, start in item] if isinstance(item, list) else next(flat) for item in lists
    )


def quarters(values, axis, bits):
    return [values] + [swap(values, axis, (mask >> 1) * bits[0] + (mask & 1) * bits[1]) for mask in (1, 2, 3)]


def exchange(values, blocks):
    shaped = values.reshape((blocks, values.shape[0] // blocks) + values.shape[1:])
    return lax.all_to_all(shaped, "res", 0, 0, tiled=True).reshape(values.shape)


def call(kernel, outs, scratch=(), grid=None, in_specs=None, out_specs=None, cost=None):
    extra = {}
    if grid is not None:
        extra = dict(grid=grid, in_specs=in_specs, out_specs=out_specs)
    elif in_specs is not None:
        extra = dict(in_specs=in_specs)
    return pl.pallas_call(
        kernel,
        out_shape=outs,
        scratch_shapes=list(scratch),
        compiler_params=pltpu.CompilerParams(vmem_limit_bytes=VMEM),
        cost_estimate=cost,
        **extra,
    )


def shape(dims, dtype):
    return jax.ShapeDtypeStruct(dims, dtype)


def stored(dims, dtype):
    return pltpu.HBM(dims, dtype)


def read(*values):
    return tuple(pltpu.with_memory_space_constraint(value, pltpu.HBM) for value in values)


def up_to(value, unit):
    return -(-value // unit) * unit


def on_device(
    nodes,
    edges,
    neighbours,
    residue_mask,
    msg_w1,
    msg_b1,
    msg_w2,
    msg_b2,
    msg_w3,
    msg_b3,
    norm1_gain,
    norm1_bias,
    ffn_w1,
    ffn_b1,
    ffn_w2,
    ffn_b2,
    norm2_gain,
    norm2_bias,
    edge_w1,
    edge_b1,
    edge_w2,
    edge_b2,
    edge_w3,
    edge_b3,
    norm3_gain,
    norm3_bias,
    node_cot,
    edge_cot,
):
    rows, kn = neighbours.shape
    blocks, parts = lax.axis_size("res"), lax.axis_size("nbr")
    total = rows * kn
    n_far = blocks * FAR
    width = n_far + rows
    kt = next(t for t in (KT, 3, 1) if kn % t == 0)
    grid = (kn // kt,)
    nbr_bits = bits_of("nbr")
    order = tuple(
        sum(bit for i, bit in enumerate(nbr_bits) if (q >> (len(nbr_bits) - 1 - i)) & 1) for q in range(parts)
    )
    mask_row = residue_mask.reshape(1, rows)
    edges = edges.transpose(1, 0, 2)
    edge_cot = edge_cot.transpose(1, 0, 2)
    edge_w1 = edge_w1.T
    res_place = lax.axis_index("res").astype(jnp.int32).reshape(1)
    nbr_place = lax.axis_index("nbr").astype(jnp.int32).reshape(1)

    smem = pl.BlockSpec(memory_space=pltpu.SMEM)
    vmem = pl.BlockSpec(memory_space=pltpu.VMEM)

    def fixed(*dims):
        return pl.BlockSpec(dims, lambda i: (0,) * len(dims))

    def tiled(*dims):
        return pl.BlockSpec(dims, lambda i: (i,) + (0,) * (len(dims) - 1))

    place_row, place_col, want, counts = call(
        functools.partial(index_kernel, blocks),
        (
            shape((SLOT, rows), jnp.int32),
            shape((rows, SLOT), f32),
            shape((n_far, 128), bf16),
            shape((rows, 128), bf16),
        ),
        in_specs=[smem, vmem, vmem],
    )(res_place, *read(neighbours.T, mask_row))
    together = lax.optimization_barrier
    wanted = exchange(want, blocks)

    picks = (wanted[:, :1].astype(jnp.int32) == iota((n_far, rows), 1)).astype(bf16)
    far_nodes = exchange(mm(picks, nodes).astype(bf16), blocks)
    far_nodes, counts = together((far_nodes, counts))
    count_a, count_b = shared_sum(counts, "nbr")

    edge_tile = tiled(kt, rows, E)
    flat = tiled(kt * rows, D)
    flat_edge = tiled(kt * rows, E)
    act1, pre1, pre2, act_sum = call(
        message_forward_kernel,
        (stored((total, D), bf16), stored((total, D), bf16), stored((total, D), bf16), shape((rows, D), bf16)),
        scratch=[pltpu.VMEM((width, D), bf16), pltpu.VMEM((rows, D), f32), pltpu.VMEM((rows, D), f32)],
        grid=grid,
        in_specs=[
            fixed(rows, SLOT),
            edge_tile,
            fixed(rows, D),
            fixed(n_far, D),
            fixed(2 * D + E, D),
            fixed(D, D),
            fixed(D),
            fixed(D),
        ],
        out_specs=(flat, flat, flat, fixed(rows, D)),
        cost=pl.CostEstimate(flops=16 * total * D * D, bytes_accessed=total * D * 8, transcendentals=2 * total * D),
    )(*read(place_col, edges, nodes), far_nodes, *read(msg_w1, msg_w2, msg_b1, msg_b2))

    def slope_of(pre):
        return call(
            slope_kernel,
            stored((total, D), bf16),
            grid=grid,
            in_specs=[flat],
            out_specs=flat,
            cost=pl.CostEstimate(flops=10 * total * D, bytes_accessed=total * D * 4, transcendentals=total * D),
        )(*read(pre))

    d1 = slope_of(pre1)
    sum_a, sum_b = shared_sum(act_sum, "nbr")
    sum_b = after(sum_b, d1)

    total_act, first_low, normed1, inv1, hidden, hidden_slope, normed2, inv2, sent, send = call(
        node_forward_kernel,
        (
            stored((rows, D), bf16),
            stored((rows, D), bf16),
            stored((rows, D), f32),
            stored((rows, 1), f32),
            stored((rows, FF), bf16),
            stored((rows, FF), bf16),
            stored((rows, D), f32),
            stored((rows, 1), f32),
            stored((rows, D), bf16),
            shape((n_far, D), bf16),
        ),
    )(sum_a, sum_b, count_a, count_b, nodes, mask_row, wanted, msg_w3, ffn_w1, ffn_w2,
      msg_b3, norm1_gain, norm1_bias, ffn_b1, ffn_b2, norm2_gain, norm2_bias)
    d2 = slope_of(after(pre2, send))
    far_sent = after(exchange(send, blocks), d2)

    first_rows, second_rows = (2 * D + E) // parts, E // parts
    edge_rows = up_to(first_rows + 2 * second_rows + 16, 32) // 2
    edges_out, base, own_sum, far_sum, local_sum, *edge_sums = call(
        edge_kernel,
        (
            shape((kn, rows, E), bf16),
            stored((total, E), f32),
            stored((rows, E), bf16),
            stored((n_far, E), bf16),
            stored((rows, E), bf16),
            stored((E, E), f32),
            stored((E, E), f32),
            stored((E, E), f32),
            stored((16, E), f32),
        ),
        scratch=[
            pltpu.VMEM((width, E), bf16),
            pltpu.VMEM((rows, E), f32),
            pltpu.VMEM((width, E), f32),
            pltpu.VMEM((rows, E), f32),
        ],
        grid=grid,
        in_specs=[
            fixed(SLOT, rows),
            fixed(rows, SLOT),
            edge_tile,
            edge_tile,
            fixed(rows, D),
            fixed(n_far, D),
            fixed(E, 2 * D + E),
            fixed(E, E),
            fixed(E, E),
        ]
        + [fixed(E)] * 5,
        out_specs=(
            edge_tile,
            flat_edge,
            fixed(rows, E),
            fixed(n_far, E),
            fixed(rows, E),
            fixed(E, E),
            fixed(E, E),
            fixed(E, E),
            fixed(16, E),
        ),
        cost=pl.CostEstimate(flops=16 * total * D * D, bytes_accessed=total * E * 12, transcendentals=2 * total * E),
    )(*read(place_row, place_col, edges, edge_cot, sent), far_sent, *read(edge_w1, edge_w2, edge_w3),
      *read(edge_b1, edge_b2, edge_b3, norm3_gain, norm3_bias))

    edge_packed = call(
        functools.partial(edge_weights_kernel, order),
        stored((parts, edge_rows, D), bf16),
        cost=pl.CostEstimate(flops=10**9, bytes_accessed=10**6, transcendentals=0),
    )(*read(sent, far_sent, own_sum, far_sum, local_sum, *edge_sums))
    far_back = after(exchange(far_sum, blocks), edge_packed)
    back = call(returned_kernel, shape((rows, 2 * E), bf16))(*read(own_sum, local_sum), far_back, wanted)
    for bit in nbr_bits[:-1]:
        back = add_low(back, swap(back, "nbr", bit))
    kept = fetched(
        after(node_cot, back), normed2, edge_w1, ffn_w2, hidden_slope, ffn_w1, normed1, msg_w3, first_low, hidden, total_act
    )
    back_a, back_b = back, swap(back, "nbr", nbr_bits[-1])

    wide, narrow = FF // parts, D // parts
    node_rows = up_to(D + wide + narrow, 16 * blocks)
    mixed_grad, up, node_bias, node_packed = call(
        functools.partial(node_backward_kernel, parts),
        (
            shape((rows, D), f32),
            shape((rows, D), f32),
            shape((16, D), f32),
            shape((node_rows, D), bf16),
        ),
        in_specs=[smem] + [vmem] * 20,
    )(
        nbr_place, back_a, back_b, count_a, count_b, *kept, mask_row, inv1, inv2, norm1_gain, norm2_gain,
    )
    bits = bits_of("res")
    order_a, order_b = bits, bits[1:2] + bits[:1] + bits[2:]
    rows_ab = node_rows // 2
    part_a = halve([(node_packed, 0)], rows_ab, "res", order_a[0])
    part_b = halve([(node_packed, rows_ab)], rows_ab, "res", order_b[0])
    edge_packed = after(edge_packed, up)
    edge_part = scattered_sum(edge_packed.reshape(parts * edge_rows, D), "nbr", nbr_bits)

    msg_rows = first_rows + narrow + 16
    share_rows = up_to(msg_rows + edge_rows, max(64, 8 * blocks))
    edges_grad, own_sum, far_sum, local_sum, msg_kept, msg_given = call(
        functools.partial(message_backward_kernel, parts),
        (
            shape((kn, rows, E), f32),
            shape((rows, D), bf16),
            shape((n_far, D), bf16),
            shape((rows, D), bf16),
            shape((parts // 2, msg_rows, D), bf16),
            shape((parts // 2, msg_rows, D), bf16),
        ),
        scratch=[
            pltpu.VMEM((width, D), f32),
            pltpu.VMEM((E, D), f32),
            pltpu.VMEM((D, D), f32),
            pltpu.VMEM((16, D), f32),
            pltpu.VMEM((rows, D), f32),
            pltpu.VMEM((3 * D + E, D), bf16),
        ],
        grid=grid,
        in_specs=[
            smem,
            fixed(SLOT, rows),
            edge_tile,
            flat,
            flat,
            flat,
            fixed(rows, D),
            flat_edge,
            fixed(rows, D),
            fixed(n_far, D),
            fixed(2 * D + E, D),
            fixed(D, D),
            fixed(16, D),
        ],
        out_specs=(edge_tile, fixed(rows, D), fixed(n_far, D), fixed(rows, D))
        + (fixed(parts // 2, msg_rows, D),) * 2,
        cost=pl.CostEstimate(flops=16 * total * D * D, bytes_accessed=total * D * 10, transcendentals=0),
    )(nbr_place & 1, *read(place_row, edges, act1, d1, d2), up, *read(base, nodes), far_nodes, *read(msg_w1, msg_w2), node_bias)

    far_sum, msg_kept, msg_given, part_a, part_b = held_together(far_sum, msg_kept, msg_given, part_a, part_b)
    flat_rows = parts // 2 * msg_rows
    msg_part = add_low(msg_kept, swap(msg_given, "nbr", 1)).reshape(flat_rows, D)
    part_a = halved_sum(total_of(part_a, rows_ab // 2), "res", order_a[1])
    part_b = halved_sum(total_of(part_b, rows_ab // 2), "res", order_b[1])
    middle, last = bits[2:-1], bits[-1]
    part_a = scattered_sum(part_a, "res", middle)
    part_b = scattered_sum(part_b, "res", middle)
    both = after(jnp.stack([part_a, part_b]), msg_part)
    msg_sum = scattered_sum(msg_part, "nbr", nbr_bits[1:])
    both = halved_sum(both, "res", last, 1)
    msg_sum = jnp.concatenate([msg_sum, edge_part, jnp.zeros((share_rows - msg_rows - edge_rows, D), bf16)], axis=0)
    msg_quarter = quarter_sum(msg_sum, "res", bits[:2])
    both = rejoined(after(both, msg_sum), "res", last, 1)
    far_back = exchange(after(far_sum, msg_sum), blocks)
    back = call(returned_last_kernel, shape((rows, D), bf16))(own_sum, local_sum, far_back, wanted, msg_w1)
    for bit in nbr_bits[:-1]:
        back = add_low(back, swap(back, "nbr", bit))
    back_b = swap(back, "nbr", nbr_bits[-1])
    msg_part = scattered_sum(msg_quarter, "res", middle)
    msg_part = add_low(msg_part, swap(msg_part, "res", last))
    part_a, part_b = both[0], both[1]
    part_a = rejoined(gathered_rows(part_a, "res", middle[::-1]), "res", order_a[1])
    part_b = rejoined(gathered_rows(part_b, "res", middle[::-1]), "res", order_b[1])
    part_a, part_b = after(part_a, msg_part), after(part_b, msg_part)
    other_a = swap(part_a, "res", order_a[0])
    other_b = swap(part_b, "res", order_b[0])
    msg_parts = quarters(gathered_rows(msg_part, "res", middle[::-1]), "res", bits[:2])

    def side(bit):
        return (lax.axis_index("res") // bit) & 1

    node_at = jnp.stack([side(order_a[0]), side(order_b[0])]).astype(jnp.int32)
    msg_at = jnp.stack([lax.axis_index("nbr"), 2 * side(bits[0]) + side(bits[1])]).astype(jnp.int32)
    nodes_grad, ffn_w1_grad, ffn_w2_grad, msg_w3_grad = call(
        functools.partial(node_weights_kernel, parts),
        (shape((rows, D), f32), shape((narrow, FF), f32), shape((wide, D), f32), shape((narrow, D), f32)),
        scratch=[pltpu.VMEM((node_rows, D), bf16)],
        in_specs=[smem] + [vmem] * 7,
    )(node_at, part_a, other_a, part_b, other_b, mixed_grad, back, back_b)
    (
        msg_w1_grad, msg_w2_grad, edge_w1_grad, edge_w2_grad, edge_w3_grad,
        edge_b1_grad, edge_b2_grad, edge_b3_grad, norm3_gain_grad, norm3_bias_grad,
        msg_b1_grad, msg_b2_grad, msg_b3_grad, norm1_gain_grad, norm1_bias_grad,
        ffn_b2_grad, norm2_gain_grad, norm2_bias_grad, ffn_b1_grad,
    ) = call(
        functools.partial(edge_message_weights_kernel, parts, edge_rows),
        (
            shape((first_rows, D), f32),
            shape((narrow, D), f32),
            shape((E, first_rows), f32),
            shape((second_rows, E), f32),
            shape((second_rows, E), f32),
        )
        + (shape((second_rows,), f32),) * 5
        + (shape((narrow,), f32),) * 8
        + (shape((wide,), f32),),
        scratch=[pltpu.VMEM((share_rows, D), bf16)],
        in_specs=[smem] + [vmem] * 4,
    )(msg_at, *msg_parts)
    return (
        sent,
        edges_out.transpose(1, 0, 2),
        nodes_grad,
        edges_grad.transpose(1, 0, 2),
        msg_w1_grad,
        msg_b1_grad,
        msg_w2_grad,
        msg_b2_grad,
        msg_w3_grad,
        msg_b3_grad,
        norm1_gain_grad,
        norm1_bias_grad,
        ffn_w1_grad,
        ffn_b1_grad,
        ffn_w2_grad,
        ffn_b2_grad,
        norm2_gain_grad,
        norm2_bias_grad,
        edge_w1_grad.T,
        edge_b1_grad,
        edge_w2_grad,
        edge_b2_grad,
        edge_w3_grad,
        edge_b3_grad,
        norm3_gain_grad,
        norm3_bias_grad,
    )


def solution(mesh):
    every = P()
    in_specs = (
        (P("res", None), P("res", "nbr", None), P("res", "nbr"), P("res"))
        + (every,) * 22
        + (P("res", None), P("res", "nbr", None))
    )
    matrix, vector = P("nbr", None), P("nbr")
    out_specs = (
        (P("res", None), P("res", "nbr", None), P("res", None), P("res", "nbr", None))
        + (matrix, vector) * 3
        + (vector, vector, matrix, vector, matrix, vector, vector, vector)
        + (matrix, vector) * 3
        + (vector, vector)
    )
    return jax.shard_map(on_device, mesh=mesh, in_specs=in_specs, out_specs=out_specs, check_vma=False)
```

```python
import functools

import jax
import jax.numpy as jnp
from jax import lax
from jax.experimental import pallas as pl
from jax.experimental.pallas import tpu as pltpu
from jax.sharding import PartitionSpec as P

D = 512
E = 192
FF = 2048
FAR = 32
SLOT = 16
KT = 5
VMEM = 32 * 1024 * 1024

bf16 = jnp.bfloat16
f32 = jnp.float32


def mm(a, b):
    return jnp.dot(a, b, preferred_element_type=f32)


def mm_tn(a, b):
    return lax.dot_general(a, b, (((0,), (0,)), ((), ())), preferred_element_type=f32)


def mm_nt(a, b):
    return lax.dot_general(a, b, (((1,), (1,)), ((), ())), preferred_element_type=f32)


def gelu_pair(v):
    c0 = 0.7978845608028654
    c1 = 0.044715 * c0
    square = v * v
    t = jnp.tanh(v * (c0 + c1 * square))
    half = 0.5 + 0.5 * t
    act = v * half
    return act, half + act * (1.0 - t) * (c0 + (3.0 * c1) * square)


def gelu(v):
    t = jnp.tanh(v * (0.7978845608028654 + (0.044715 * 0.7978845608028654) * (v * v)))
    half = 0.5 * v
    return half + half * t


def norm_forward(values):
    centred = values - jnp.mean(values, axis=-1, keepdims=True)
    inverse = lax.rsqrt(jnp.mean(centred * centred, axis=-1, keepdims=True) + 1e-05)
    return centred * inverse, inverse


def norm_backward(upstream, normed, inverse, gain):
    scaled = upstream * gain
    first = jnp.mean(scaled, axis=-1, keepdims=True)
    second = jnp.mean(scaled * normed, axis=-1, keepdims=True)
    return inverse * (scaled - first - normed * second)


def row_of(ref):
    return ref[...].astype(f32).reshape(1, ref.shape[0])


def column_sum(values):
    return jnp.sum(values, axis=0, keepdims=True)


def iota(shape, dim):
    return lax.broadcasted_iota(jnp.int32, shape, dim)


def present_column(mask_ref, rows):
    real = jnp.sum(mask_ref[...].astype(f32), axis=1, keepdims=True)
    return (iota((rows, 1), 0).astype(f32) < real).astype(f32)


def pick_matrix(want_ref, rows):
    want = want_ref[...][:, :1].astype(f32)
    return (want == iota((want.shape[0], rows), 1).astype(f32)).astype(bf16)


def one_hot(column, width):
    return (column == iota((column.shape[0], width), 1)).astype(bf16)


def columns_of(col_ref, first, count):
    values = col_ref[...]
    lane = iota(values.shape, 1)
    return [
        jnp.sum(jnp.where(lane == first + j, values, 0.0), axis=1, keepdims=True).astype(jnp.int32)
        for j in range(count)
    ]


def kept_weight(columns):
    return jnp.concatenate([(column >= 0).astype(f32) for column in columns], axis=0)


def spread(rows, values):
    n, c = rows.shape
    return (values.reshape(-1, n, c) + rows[None]).reshape(values.shape)


def gathered(values, n):
    return jnp.sum(values.reshape(-1, n, values.shape[1]), axis=0)


def slot_sums(row_ref, first, count, width, values, acc):
    n = row_ref.shape[1]
    for j in range(count):
        row = row_ref[pl.ds(first + j, 1), :]
        hot = (row == iota((width, n), 0)).astype(bf16)
        acc[...] += mm(hot, values[j * n : (j + 1) * n])


def index_kernel(blocks, me_ref, near_ref, mask_ref, row_ref, col_ref, want_ref, count_ref):
    kn, rows = near_ref.shape
    me = me_ref[0].astype(f32)
    lanes = max(16, blocks)
    index = near_ref[...].astype(f32)
    block = jnp.floor((index + 0.5) * (1.0 / rows))
    slot = index - block * rows
    local = block == me
    far_block = jnp.where(local, -1.0, block)
    real = jnp.sum(mask_ref[...].astype(f32), axis=1, keepdims=True)
    own_place = iota((kn, rows), 1).astype(f32)
    kept = jnp.logical_and(jnp.logical_or(jnp.logical_not(local), slot < real), own_place < real)
    slot_line = iota((rows, rows), 0).astype(f32)
    block_line = iota((lanes, rows), 0).astype(f32)
    hot_slot = [(slot[k : k + 1] == slot_line).astype(bf16) for k in range(kn)]
    hot_block = [(far_block[k : k + 1] == block_line).astype(bf16) for k in range(kn)]
    named = mm_nt(hot_block[0], hot_slot[0])
    for k in range(1, kn):
        named = named + mm_nt(hot_block[k], hot_slot[k])
    flags = (named > 0.0).astype(f32)
    before = (iota((rows, rows), 0) < iota((rows, rows), 1)).astype(bf16)
    rank = mm(flags.astype(bf16), before)
    key = jnp.where(flags > 0.0, rank, -1.0)[:blocks]
    key = jnp.broadcast_to(key[:, None, :], (blocks, FAR, rows)).reshape(blocks * FAR, rows)
    level = (iota((blocks * FAR, 1), 0) & (FAR - 1)).astype(f32)
    hit = (key == level).astype(f32)
    place_row = iota((blocks * FAR, rows), 1).astype(f32)
    want = jnp.sum(hit * place_row, axis=1, keepdims=True)
    found = jnp.sum(hit, axis=1, keepdims=True)
    want = jnp.where(found > 0.0, want, 255.0)
    want_ref[...] = jnp.broadcast_to(want, want_ref.shape).astype(bf16)
    after = (iota((rows, rows), 0) > iota((rows, rows), 1)).astype(bf16)
    rank_down = mm_nt(after, flags.astype(bf16)).astype(bf16)
    edge_rank = jnp.concatenate(
        [
            jnp.sum(mm(rank_down, hot_block[k]) * hot_slot[k].astype(f32), axis=0, keepdims=True)
            for k in range(kn)
        ],
        axis=0,
    )
    place = jnp.where(local, blocks * FAR + slot, block * FAR + edge_rank)
    place = jnp.where(kept, place, -1.0)
    place = jnp.concatenate([place, jnp.full((SLOT - kn, rows), -1.0, f32)], axis=0)
    row_ref[...] = place.astype(jnp.int32)
    col_ref[...] = place.T
    counts = jnp.sum((col_ref[...] >= 0.0).astype(f32), axis=1, keepdims=True)
    count_ref[...] = jnp.broadcast_to(counts, count_ref.shape).astype(bf16)


def message_forward_kernel(
    col_ref, edges_ref, nodes_ref, far_ref, w1_ref, w2_ref, b1_ref, b2_ref,
    act1_ref, pre1_ref, pre2_ref, sum_ref, table, own, acc,
):
    step = pl.program_id(0)
    last = pl.num_programs(0) - 1
    kt, rows, _ = edges_ref.shape
    n_far = far_ref.shape[0]
    width = table.shape[0]

    @pl.when(step == 0)
    def _():
        weight = w1_ref[D : 2 * D, :]
        table[:n_far] = mm(far_ref[...], weight).astype(bf16)
        table[n_far:] = mm(nodes_ref[...], weight).astype(bf16)
        own[...] = mm(nodes_ref[...], w1_ref[:D, :]) + row_of(b1_ref)
        acc[...] = jnp.zeros_like(acc)

    each = range(kt)
    places = [pl.ds(j * rows, rows) for j in each]
    columns = columns_of(col_ref, step * kt, kt)
    pre1 = [mm(one_hot(columns[j], width), table[...]) + mm(edges_ref[j], w1_ref[2 * D :, :]) for j in each]
    act1 = []
    for j in each:
        total = pre1[j] + own[...]
        pre1_ref[places[j], :] = total.astype(bf16)
        act1.append(gelu(total).astype(bf16))
        act1_ref[places[j], :] = act1[j]
    pre2 = [mm(act1[j], w2_ref[...]) for j in each]
    for j in each:
        total = jnp.where(columns[j] >= 0, pre2[j] + row_of(b2_ref), -30.0)
        pre2_ref[places[j], :] = total.astype(bf16)
        acc[...] += gelu(total)

    @pl.when(step == last)
    def _():
        sum_ref[...] = acc[...].astype(bf16)


def slope_kernel(pre_ref, slope_ref):
    slope_ref[...] = gelu_pair(pre_ref[...].astype(f32))[1].astype(bf16)


def node_forward_kernel(
    sum_a, sum_b, count_a, count_b, nodes_ref, mask_ref, want_ref, w3_ref, f1_ref, f2_ref,
    b3_ref, gain1_ref, bias1_ref, fb1_ref, fb2_ref, gain2_ref, bias2_ref,
    total_ref, low_ref, normed1_ref, inv1_ref, hid_ref, slope_ref, normed2_ref, inv2_ref, sent_ref, send_ref,
):
    rows = nodes_ref.shape[0]
    present = present_column(mask_ref, rows)
    count = count_a[...].astype(f32) + count_b[...].astype(f32)
    count = count[:, :1]
    total = sum_a[...].astype(f32) + sum_b[...].astype(f32)
    high = total.astype(bf16)
    total_ref[...] = high
    rest = (total - high.astype(f32)).astype(bf16)
    summed = mm(high, w3_ref[...]) + mm(rest, w3_ref[...]) + count * row_of(b3_ref)
    mixed = nodes_ref[...].astype(f32) + summed / jnp.maximum(count, 1.0)
    normed, inverse = norm_forward(mixed)
    normed1_ref[...] = normed
    inv1_ref[...] = inverse
    first = normed * row_of(gain1_ref) + row_of(bias1_ref)
    low = first.astype(bf16)
    low_ref[...] = low
    act, slope = gelu_pair(mm(low, f1_ref[...]) + row_of(fb1_ref))
    act = act.astype(bf16)
    hid_ref[...] = act
    slope_ref[...] = slope.astype(bf16)
    branch = mm(act, f2_ref[...]) + row_of(fb2_ref)
    normed, inverse = norm_forward(first + branch)
    normed2_ref[...] = normed
    inv2_ref[...] = inverse
    sent = (present * (normed * row_of(gain2_ref) + row_of(bias2_ref))).astype(bf16)
    sent_ref[...] = sent
    send_ref[...] = mm(pick_matrix(want_ref, rows), sent).astype(bf16)


def edge_kernel(
    row_ref, col_ref, edges_ref, cot_ref, sent_ref, far_ref, w1_ref, w2_ref, w3_ref, b1_ref, b2_ref, b3_ref, gain_ref, shift_ref,
    out_ref, base_ref, own_ref, far_grad_ref, local_grad_ref, w1_acc, w2_acc, w3_acc, bias_acc,
    table, own, sums, own_acc,
):
    step = pl.program_id(0)
    last = pl.num_programs(0) - 1
    kt, rows, _ = edges_ref.shape
    n_far = far_ref.shape[0]
    width = table.shape[0]

    @pl.when(step == 0)
    def _():
        weight = w1_ref[:, D : 2 * D]
        table[:n_far] = mm_nt(far_ref[...], weight).astype(bf16)
        table[n_far:] = mm_nt(sent_ref[...], weight).astype(bf16)
        own[...] = mm_nt(sent_ref[...], w1_ref[:, :D]) + row_of(b1_ref)
        for acc in (sums, w1_acc, w2_acc, w3_acc, bias_acc, own_acc):
            acc[...] = jnp.zeros_like(acc)

    edge = edges_ref[...].reshape(kt * rows, E)
    cot = cot_ref[...].reshape(kt * rows, E)
    columns = columns_of(col_ref, step * kt, kt)
    hot = jnp.concatenate([one_hot(column, width) for column in columns], axis=0)
    edge_weight = w1_ref[:, 2 * D :]
    pre1 = spread(own[...], mm(hot, table[...]) + mm_nt(edge, edge_weight))
    act, slope1 = gelu_pair(pre1)
    act1 = act.astype(bf16)
    act, slope2 = gelu_pair(mm(act1, w2_ref[...]) + row_of(b2_ref))
    act2 = act.astype(bf16)
    branch = mm(act2, w3_ref[...]) + row_of(b3_ref)
    weight = kept_weight(columns)
    normed, inverse = norm_forward(edge.astype(f32) + branch)
    gain = row_of(gain_ref)
    out = weight * (normed * gain + row_of(shift_ref))
    out_ref[...] = out.astype(bf16).reshape(kt, rows, E)
    up = weight * cot.astype(f32)
    grad = norm_backward(up, normed, inverse, gain)
    low3 = grad.astype(bf16)
    w3_acc[...] += mm_tn(act2, low3)
    low2 = (slope2 * mm_nt(low3, w3_ref[...])).astype(bf16)
    w2_acc[...] += mm_tn(act1, low2)
    low1 = (slope1 * mm_nt(low2, w2_ref[...])).astype(bf16)
    w1_acc[...] += mm_tn(edge, low1)
    slot_sums(row_ref, step * kt, kt, width, low1, sums)
    base_ref[...] = grad + mm(low1, edge_weight)
    own_sum = gathered(low1.astype(f32), rows)
    own_acc[...] += own_sum
    row = iota((16, 1), 0)
    bias_acc[...] += (
        jnp.where(row == 0, column_sum(own_sum), 0.0)
        + jnp.where(row == 1, column_sum(low2.astype(f32)), 0.0)
        + jnp.where(row == 2, column_sum(low3.astype(f32)), 0.0)
        + jnp.where(row == 3, column_sum(up * normed), 0.0)
        + jnp.where(row == 4, column_sum(up), 0.0)
    )

    @pl.when(step == last)
    def _():
        total = sums[...]
        own_ref[...] = own_acc[...].astype(bf16)
        far_grad_ref[...] = total[:n_far].astype(bf16)
        local_grad_ref[...] = total[n_far:].astype(bf16)


def edge_weights_kernel(
    order, sent_ref, far_ref, own_ref, far_grad_ref, local_grad_ref, w1_ref, w2_ref, w3_ref, bias_ref, packed_ref
):
    parts = len(order)
    first, second = (2 * D + E) // parts, E // parts
    sent = sent_ref[...]
    whole = jnp.concatenate(
        [
            mm_tn(sent, own_ref[...]),
            mm_tn(far_ref[...], far_grad_ref[...]) + mm_tn(sent, local_grad_ref[...]),
            w1_ref[...],
        ],
        axis=0,
    ).astype(bf16)
    second_w = w2_ref[...].astype(bf16)
    third_w = w3_ref[...].astype(bf16)
    bias = bias_ref[...].astype(bf16)
    half = packed_ref.shape[1]
    for q, n in enumerate(order):
        rows = jnp.concatenate(
            [
                whole[n * first : (n + 1) * first],
                second_w[n * second : (n + 1) * second],
                third_w[n * second : (n + 1) * second],
                bias,
            ],
            axis=0,
        )
        packed_ref[q, :, :E] = rows[:half]
        packed_ref[q, :, 256 : 256 + E] = rows[half:]
        packed_ref[q, :, E:256] = jnp.zeros((half, 256 - E), bf16)
        packed_ref[q, :, 256 + E :] = jnp.zeros((half, 256 - E), bf16)


def returned_kernel(own_ref, local_ref, back_ref, want_ref, out_ref):
    rows = local_ref.shape[0]
    near = local_ref[...].astype(f32) + mm_tn(pick_matrix(want_ref, rows), back_ref[...])
    out_ref[...] = jnp.concatenate([own_ref[...], near.astype(bf16)], axis=1)


def returned_last_kernel(own_ref, local_ref, back_ref, want_ref, w1_ref, out_ref):
    rows = local_ref.shape[0]
    near = local_ref[...].astype(f32) + mm_tn(pick_matrix(want_ref, rows), back_ref[...])
    grad = mm_nt(own_ref[...], w1_ref[:D, :]) + mm_nt(near.astype(bf16), w1_ref[D : 2 * D, :])
    out_ref[...] = grad.astype(bf16)


def fetch_kernel(*refs):
    *refs, arrivals = refs
    count = len(refs) // 2
    copies = [pltpu.make_async_copy(refs[i], refs[count + i], arrivals.at[i]) for i in range(count)]
    for copy in copies:
        copy.start()
    for copy in copies:
        copy.wait()


def fetched(*values):
    size = sum(value.size * value.dtype.itemsize for value in values)
    return pl.pallas_call(
        fetch_kernel,
        out_shape=tuple(pltpu.VMEM(value.shape, value.dtype) for value in values),
        in_specs=[pl.BlockSpec(memory_space=pltpu.HBM)] * len(values),
        out_specs=tuple(pl.BlockSpec(memory_space=pltpu.VMEM) for _ in values),
        scratch_shapes=[pltpu.SemaphoreType.DMA((len(values),))],
        compiler_params=pltpu.CompilerParams(vmem_limit_bytes=VMEM),
        cost_estimate=pl.CostEstimate(flops=0, bytes_accessed=2 * size, transcendentals=0),
    )(*read(*values))


def node_backward_kernel(
    parts, place_ref, back_a, back_b, count_a, count_b, cot_ref, normed2_ref, ew1_ref, f2_ref, slope_ref, f1_ref,
    normed1_ref, w3_ref, low_ref, hid_ref, total_ref, mask_ref, inv1_ref, inv2_ref, gain1_ref, gain2_ref,
    mixed_ref, up_ref, bias_ref, packed_ref,
):
    rows = cot_ref.shape[0]
    place = place_ref[0]
    present = present_column(mask_ref, rows)
    count = (count_a[...].astype(f32) + count_b[...].astype(f32))[:, :1]
    back = (back_a[...].astype(f32) + back_b[...].astype(f32)).astype(bf16)
    node_back = mm(back[:, :E], ew1_ref[:, :D]) + mm(back[:, E:], ew1_ref[:, D : 2 * D])
    up = present * (cot_ref[...].astype(f32) + node_back)
    normed2 = normed2_ref[...]
    sum_grad = norm_backward(up, normed2, inv2_ref[...], row_of(gain2_ref))
    branch_grad = sum_grad.astype(bf16)
    hidden_grad = (slope_ref[...].astype(f32) * mm_nt(branch_grad, f2_ref[...])).astype(bf16)
    first_grad = sum_grad + mm_nt(hidden_grad, f1_ref[...])
    normed1 = normed1_ref[...]
    mixed_grad = norm_backward(first_grad, normed1, inv1_ref[...], row_of(gain1_ref))
    mixed_ref[...] = mixed_grad
    message_grad = (mixed_grad / jnp.maximum(count, 1.0)).astype(bf16)
    up_ref[...] = mm_nt(message_grad, w3_ref[...])
    row = iota((16, 1), 0)
    hidden_sum = column_sum(hidden_grad.astype(f32))
    bias = (
        jnp.where(row == 2, column_sum(count * message_grad.astype(f32)), 0.0)
        + jnp.where(row == 3, column_sum(first_grad * normed1), 0.0)
        + jnp.where(row == 4, column_sum(first_grad), 0.0)
        + jnp.where(row == 5, column_sum(branch_grad.astype(f32)), 0.0)
        + jnp.where(row == 6, column_sum(up * normed2), 0.0)
        + jnp.where(row == 7, column_sum(up), 0.0)
    )
    for j in range(FF // D):
        bias = bias + jnp.where(row == 8 + j, hidden_sum[:, j * D : (j + 1) * D], 0.0)
    bias_ref[...] = bias * (1.0 / parts)
    wide, narrow = FF // parts, D // parts
    low = low_ref[:, pl.ds(pl.multiple_of(place * narrow, narrow), narrow)]
    for j in range(FF // D):
        packed_ref[j * narrow : (j + 1) * narrow, :] = mm_tn(low, hidden_grad[:, j * D : (j + 1) * D]).astype(bf16)
    hid = hid_ref[:, pl.ds(pl.multiple_of(place * wide, wide), wide)]
    packed_ref[D : D + wide, :] = mm_tn(hid, branch_grad).astype(bf16)
    total = total_ref[:, pl.ds(pl.multiple_of(place * narrow, narrow), narrow)]
    packed_ref[D + wide : D + wide + narrow, :] = mm_tn(total, message_grad).astype(bf16)
    at = D + wide + narrow
    if packed_ref.shape[0] > at:
        packed_ref[at:, :] = jnp.zeros((packed_ref.shape[0] - at, D), bf16)


def message_backward_kernel(
    parts, core_ref, row_ref, edges_ref, act1_ref, d1_ref, d2_ref, up_ref, base_ref, nodes_ref, far_ref, w1_ref, w2_ref, node_bias_ref,
    out_ref, own_ref, far_grad_ref, local_grad_ref, kept_ref, given_ref,
    sums, w1_acc, w2_acc, bias_acc, own_acc, whole,
):
    step = pl.program_id(0)
    last = pl.num_programs(0) - 1
    kt, rows, _ = edges_ref.shape
    n_far = far_ref.shape[0]
    width = sums.shape[0]

    @pl.when(step == 0)
    def _():
        for acc in (sums, w1_acc, w2_acc, own_acc):
            acc[...] = jnp.zeros_like(acc)
        bias_acc[...] = node_bias_ref[...]

    edge = edges_ref[...].reshape(kt * rows, E)
    slope2 = d2_ref[...].astype(f32).reshape(kt, rows, D)
    grad2 = (slope2 * up_ref[...][None]).reshape(kt * rows, D)
    low2 = grad2.astype(bf16)
    w2_acc[...] += mm_tn(act1_ref[...], low2)
    grad1 = d1_ref[...].astype(f32) * mm_nt(low2, w2_ref[...])
    low1 = grad1.astype(bf16)
    w1_acc[...] += mm_tn(edge, low1)
    slot_sums(row_ref, step * kt, kt, width, low1, sums)
    grad = base_ref[...] + mm_nt(low1, w1_ref[2 * D :, :])
    out_ref[...] = grad.reshape(kt, rows, E)
    own_sum = gathered(grad1, rows)
    own_acc[...] += own_sum
    row = iota((16, 1), 0)
    bias_acc[...] += jnp.where(row == 0, column_sum(own_sum), 0.0) + jnp.where(
        row == 1, column_sum(grad2), 0.0
    )

    @pl.when(step == last)
    def _():
        total = sums[...]
        own_low = own_acc[...].astype(bf16)
        own_ref[...] = own_low
        far_grad_ref[...] = total[:n_far].astype(bf16)
        local_grad_ref[...] = total[n_far:].astype(bf16)
        nodes = nodes_ref[...]
        first = (2 * D + E) // parts
        second = D // parts
        whole[:D, :] = mm_tn(nodes, own_low).astype(bf16)
        whole[D : 2 * D, :] = (
            mm_tn(far_ref[...], total[:n_far].astype(bf16)) + mm_tn(nodes, total[n_far:].astype(bf16))
        ).astype(bf16)
        whole[2 * D : 2 * D + E, :] = w1_acc[...].astype(bf16)
        whole[2 * D + E :, :] = w2_acc[...].astype(bf16)
        bias = bias_acc[...].astype(bf16)
        half = kept_ref.shape[0]
        for ref, side in ((kept_ref, core_ref[0]), (given_ref, 1 - core_ref[0])):
            for q in range(half):
                n = q * 2 + side
                ref[q, :first, :] = whole[pl.ds(pl.multiple_of(n * first, 16), first), :]
                ref[q, first : first + second, :] = whole[
                    pl.ds(pl.multiple_of(2 * D + E + n * second, 16), second), :
                ]
                ref[q, first + second : first + second + 16, :] = bias


def picked_lanes(rows, place, parts):
    wide = rows.shape[1] // parts
    out = jnp.zeros((rows.shape[0], wide), f32)
    for n in range(parts):
        out = out + jnp.where(place == n, rows[:, n * wide : (n + 1) * wide], 0.0)
    return out


def joined(whole, index, piece):
    rows = piece.shape[0]
    whole[pl.ds(pl.multiple_of(index * rows, 16), rows), :] = piece[...]


def node_weights_kernel(
    parts, at_ref, a0, a1, b0, b1, mixed_ref, back_a, back_b, nodes_ref, f1_ref, f2_ref, w3_ref, whole
):
    nodes_ref[...] = mixed_ref[...] + (back_a[...].astype(f32) + back_b[...].astype(f32))
    top = whole.shape[0] // 2
    low, high = whole.at[:top], whole.at[top:]
    joined(low, at_ref[0], a0)
    joined(low, 1 - at_ref[0], a1)
    joined(high, at_ref[1], b0)
    joined(high, 1 - at_ref[1], b1)
    wide, narrow = FF // parts, D // parts
    for j in range(FF // D):
        f1_ref[:, j * D : (j + 1) * D] = whole[j * narrow : (j + 1) * narrow, :].astype(f32)
    f2_ref[...] = whole[D : D + wide, :].astype(f32)
    w3_ref[...] = whole[D + wide : D + wide + narrow, :].astype(f32)


def edge_message_weights_kernel(
    parts, half, at_ref, p0, p1, p2, p3, w1_ref, w2_ref, ew1_ref, ew2_ref, ew3_ref, *refs
):
    *vectors, fb1_ref, whole = refs
    for mask, piece in enumerate((p0, p1, p2, p3)):
        joined(whole, at_ref[1] ^ mask, piece)
    place = at_ref[0]
    first, narrow, second = (2 * D + E) // parts, D // parts, E // parts
    w1_ref[...] = whole[:first, :].astype(f32)
    w2_ref[...] = whole[first : first + narrow, :].astype(f32)
    at = first + narrow
    bias = whole[at : at + 16, :].astype(f32)
    rows = picked_lanes(bias[:8], place, parts)
    for j, ref in enumerate(vectors[5:]):
        ref[...] = rows[j : j + 1].reshape(narrow)
    hidden = jnp.zeros((1, D), f32)
    for n in range(FF // D):
        hidden = hidden + jnp.where(place == n, bias[8 + n : 9 + n], 0.0)
    fb1_ref[...] = hidden.reshape(FF // parts)
    at += 16
    edge = jnp.concatenate([whole[at : at + half, :E], whole[at : at + half, 256 : 256 + E]], axis=0).astype(f32)
    ew1_ref[...] = edge[:first].T
    ew2_ref[...] = edge[first : first + second]
    ew3_ref[...] = edge[first + second : first + 2 * second]
    rows = picked_lanes(edge[first + 2 * second : first + 2 * second + 8], place, parts)
    for j, ref in enumerate(vectors[:5]):
        ref[...] = rows[j : j + 1].reshape(second)


def swap(values, axis, bit):
    return lax.ppermute(values, axis, [(i, i ^ bit) for i in range(lax.axis_size(axis))])


def bits_of(axis):
    size, bit, out = lax.axis_size(axis), 1, []
    while bit < size:
        out.append(bit)
        bit *= 2
    return out


def add_low(a, b):
    return (a.astype(f32) + b.astype(f32)).astype(bf16)


def shared_sum(values, axis):
    bits = bits_of(axis)
    for bit in bits[:-1]:
        values = add_low(values, swap(values, axis, bit))
    return values, swap(values, axis, bits[-1])


def after(values, *earlier):
    return lax.optimization_barrier((values, *earlier))[0]


def halved_sum(values, axis, bit, dim=0):
    half = values.shape[dim] // 2
    side = (lax.axis_index(axis) // bit) & 1
    kept = lax.dynamic_slice_in_dim(values, side * half, half, dim)
    given = lax.dynamic_slice_in_dim(values, (1 - side) * half, half, dim)
    return add_low(kept, swap(given, axis, bit))


def rejoined(values, axis, bit, dim=0):
    other = swap(values, axis, bit)
    side = (lax.axis_index(axis) // bit) & 1
    return jnp.where(
        side == 0, jnp.concatenate([values, other], axis=dim), jnp.concatenate([other, values], axis=dim)
    )


def scattered_sum(values, axis, bits):
    for bit in bits:
        values = halved_sum(values, axis, bit)
    return values


def gathered_rows(values, axis, bits):
    for bit in bits:
        values = rejoined(values, axis, bit)
    return values


def total_of(addends, rows):
    total = 0.0
    for values, start in addends:
        total = total + lax.dynamic_slice_in_dim(values, start, rows, 0).astype(f32)
    return total.astype(bf16)


def halve(addends, rows, axis, bit):
    half = rows // 2
    side = (lax.axis_index(axis) // bit) & 1
    given = total_of([(values, start + (1 - side) * half) for values, start in addends], half)
    return [(values, start + side * half) for values, start in addends] + [(swap(given, axis, bit), 0)]


def quarter_sum(values, axis, bits):
    rows = values.shape[0] // 4
    low, high = ((lax.axis_index(axis) // bit) & 1 for bit in bits)
    mine = 2 * low + high
    total = lax.dynamic_slice_in_dim(values, mine * rows, rows, 0).astype(f32)
    for mask in (1, 2, 3):
        given = lax.dynamic_slice_in_dim(values, (mine ^ mask) * rows, rows, 0)
        total = total + swap(given, axis, (mask >> 1) * bits[0] + (mask & 1) * bits[1]).astype(f32)
    return total.astype(bf16)


def held_together(*lists):
    flat = []
    for item in lists:
        flat += [values for values, _ in item] if isinstance(item, list) else [item]
    flat = iter(lax.optimization_barrier(tuple(flat)))
    return tuple(
        [(next(flat), start) for _, start in item] if isinstance(item, list) else next(flat) for item in lists
    )


def quarters(values, axis, bits):
    return [values] + [swap(values, axis, (mask >> 1) * bits[0] + (mask & 1) * bits[1]) for mask in (1, 2, 3)]


def exchange(values, blocks):
    shaped = values.reshape((blocks, values.shape[0] // blocks) + values.shape[1:])
    return lax.all_to_all(shaped, "res", 0, 0, tiled=True).reshape(values.shape)


def call(kernel, outs, scratch=(), grid=None, in_specs=None, out_specs=None, cost=None):
    extra = {}
    if grid is not None:
        extra = dict(grid=grid, in_specs=in_specs, out_specs=out_specs)
    elif in_specs is not None:
        extra = dict(in_specs=in_specs)
    return pl.pallas_call(
        kernel,
        out_shape=outs,
        scratch_shapes=list(scratch),
        compiler_params=pltpu.CompilerParams(vmem_limit_bytes=VMEM),
        cost_estimate=cost,
        **extra,
    )


def shape(dims, dtype):
    return jax.ShapeDtypeStruct(dims, dtype)


def stored(dims, dtype):
    return pltpu.HBM(dims, dtype)


def read(*values):
    return tuple(pltpu.with_memory_space_constraint(value, pltpu.HBM) for value in values)


def up_to(value, unit):
    return -(-value // unit) * unit


def on_device(
    nodes,
    edges,
    neighbours,
    residue_mask,
    msg_w1,
    msg_b1,
    msg_w2,
    msg_b2,
    msg_w3,
    msg_b3,
    norm1_gain,
    norm1_bias,
    ffn_w1,
    ffn_b1,
    ffn_w2,
    ffn_b2,
    norm2_gain,
    norm2_bias,
    edge_w1,
    edge_b1,
    edge_w2,
    edge_b2,
    edge_w3,
    edge_b3,
    norm3_gain,
    norm3_bias,
    node_cot,
    edge_cot,
):
    rows, kn = neighbours.shape
    blocks, parts = lax.axis_size("res"), lax.axis_size("nbr")
    total = rows * kn
    n_far = blocks * FAR
    width = n_far + rows
    kt = next(t for t in (KT, 3, 1) if kn % t == 0)
    grid = (kn // kt,)
    nbr_bits = bits_of("nbr")
    order = tuple(
        sum(bit for i, bit in enumerate(nbr_bits) if (q >> (len(nbr_bits) - 1 - i)) & 1) for q in range(parts)
    )
    mask_row = residue_mask.reshape(1, rows)
    edges = edges.transpose(1, 0, 2)
    edge_cot = edge_cot.transpose(1, 0, 2)
    edge_w1 = edge_w1.T
    res_place = lax.axis_index("res").astype(jnp.int32).reshape(1)
    nbr_place = lax.axis_index("nbr").astype(jnp.int32).reshape(1)

    smem = pl.BlockSpec(memory_space=pltpu.SMEM)
    vmem = pl.BlockSpec(memory_space=pltpu.VMEM)

    def fixed(*dims):
        return pl.BlockSpec(dims, lambda i: (0,) * len(dims))

    def tiled(*dims):
        return pl.BlockSpec(dims, lambda i: (i,) + (0,) * (len(dims) - 1))

    place_row, place_col, want, counts = call(
        functools.partial(index_kernel, blocks),
        (
            shape((SLOT, rows), jnp.int32),
            shape((rows, SLOT), f32),
            shape((n_far, 128), bf16),
            shape((rows, 128), bf16),
        ),
        in_specs=[smem, vmem, vmem],
    )(res_place, *read(neighbours.T, mask_row))
    together = lax.optimization_barrier
    wanted = exchange(want, blocks)

    picks = (wanted[:, :1].astype(jnp.int32) == iota((n_far, rows), 1)).astype(bf16)
    far_nodes = exchange(mm(picks, nodes).astype(bf16), blocks)
    far_nodes, counts = together((far_nodes, counts))
    count_a, count_b = shared_sum(counts, "nbr")

    edge_tile = tiled(kt, rows, E)
    flat = tiled(kt * rows, D)
    flat_edge = tiled(kt * rows, E)
    kf = 3 if kn % 3 == 0 else 1
    act1, pre1, pre2, act_sum = call(
        message_forward_kernel,
        (stored((total, D), bf16), stored((total, D), bf16), stored((total, D), bf16), shape((rows, D), bf16)),
        scratch=[pltpu.VMEM((width, D), bf16), pltpu.VMEM((rows, D), f32), pltpu.VMEM((rows, D), f32)],
        grid=(kn // kf,),
        in_specs=[
            fixed(rows, SLOT),
            tiled(kf, rows, E),
            fixed(rows, D),
            fixed(n_far, D),
            fixed(2 * D + E, D),
            fixed(D, D),
            fixed(D),
            fixed(D),
        ],
        out_specs=(tiled(kf * rows, D),) * 3 + (fixed(rows, D),),
        cost=pl.CostEstimate(flops=16 * total * D * D, bytes_accessed=total * D * 8, transcendentals=2 * total * D),
    )(*read(place_col, edges, nodes), far_nodes, *read(msg_w1, msg_w2, msg_b1, msg_b2))

    def slope_of(pre):
        return call(
            slope_kernel,
            stored((total, D), bf16),
            grid=grid,
            in_specs=[flat],
            out_specs=flat,
            cost=pl.CostEstimate(flops=10 * total * D, bytes_accessed=total * D * 4, transcendentals=total * D),
        )(*read(pre))

    d1 = slope_of(pre1)
    sum_a, sum_b = shared_sum(act_sum, "nbr")
    sum_b = after(sum_b, d1)

    total_act, first_low, normed1, inv1, hidden, hidden_slope, normed2, inv2, sent, send = call(
        node_forward_kernel,
        (
            stored((rows, D), bf16),
            stored((rows, D), bf16),
            stored((rows, D), f32),
            stored((rows, 1), f32),
            stored((rows, FF), bf16),
            stored((rows, FF), bf16),
            stored((rows, D), f32),
            stored((rows, 1), f32),
            stored((rows, D), bf16),
            shape((n_far, D), bf16),
        ),
    )(sum_a, sum_b, count_a, count_b, nodes, mask_row, wanted, msg_w3, ffn_w1, ffn_w2,
      msg_b3, norm1_gain, norm1_bias, ffn_b1, ffn_b2, norm2_gain, norm2_bias)
    d2 = slope_of(after(pre2, send))
    far_sent = after(exchange(send, blocks), d2)

    first_rows, second_rows = (2 * D + E) // parts, E // parts
    edge_rows = up_to(first_rows + 2 * second_rows + 16, 32) // 2
    edges_out, base, own_sum, far_sum, local_sum, *edge_sums = call(
        edge_kernel,
        (
            shape((kn, rows, E), bf16),
            stored((total, E), f32),
            stored((rows, E), bf16),
            stored((n_far, E), bf16),
            stored((rows, E), bf16),
            stored((E, E), f32),
            stored((E, E), f32),
            stored((E, E), f32),
            stored((16, E), f32),
        ),
        scratch=[
            pltpu.VMEM((width, E), bf16),
            pltpu.VMEM((rows, E), f32),
            pltpu.VMEM((width, E), f32),
            pltpu.VMEM((rows, E), f32),
        ],
        grid=grid,
        in_specs=[
            fixed(SLOT, rows),
            fixed(rows, SLOT),
            edge_tile,
            edge_tile,
            fixed(rows, D),
            fixed(n_far, D),
            fixed(E, 2 * D + E),
            fixed(E, E),
            fixed(E, E),
        ]
        + [fixed(E)] * 5,
        out_specs=(
            edge_tile,
            flat_edge,
            fixed(rows, E),
            fixed(n_far, E),
            fixed(rows, E),
            fixed(E, E),
            fixed(E, E),
            fixed(E, E),
            fixed(16, E),
        ),
        cost=pl.CostEstimate(flops=16 * total * D * D, bytes_accessed=total * E * 12, transcendentals=2 * total * E),
    )(*read(place_row, place_col, edges, edge_cot, sent), far_sent, *read(edge_w1, edge_w2, edge_w3),
      *read(edge_b1, edge_b2, edge_b3, norm3_gain, norm3_bias))

    edge_packed = call(
        functools.partial(edge_weights_kernel, order),
        stored((parts, edge_rows, D), bf16),
        cost=pl.CostEstimate(flops=10**9, bytes_accessed=10**6, transcendentals=0),
    )(*read(sent, far_sent, own_sum, far_sum, local_sum, *edge_sums))
    far_back = after(exchange(far_sum, blocks), edge_packed)
    back = call(returned_kernel, shape((rows, 2 * E), bf16))(*read(own_sum, local_sum), far_back, wanted)
    for bit in nbr_bits[:-1]:
        back = add_low(back, swap(back, "nbr", bit))
    kept = fetched(
        after(node_cot, back), normed2, edge_w1, ffn_w2, hidden_slope, ffn_w1, normed1, msg_w3, first_low, hidden, total_act,
        msg_w1, msg_w2, nodes, far_nodes
    )
    *kept, ready_w1, ready_w2, ready_nodes, ready_far = kept
    back_a, back_b = back, swap(back, "nbr", nbr_bits[-1])

    wide, narrow = FF // parts, D // parts
    node_rows = up_to(D + wide + narrow, 16 * blocks)
    mixed_grad, up, node_bias, node_packed = call(
        functools.partial(node_backward_kernel, parts),
        (
            shape((rows, D), f32),
            shape((rows, D), f32),
            shape((16, D), f32),
            shape((node_rows, D), bf16),
        ),
        in_specs=[smem] + [vmem] * 20,
    )(
        nbr_place, back_a, back_b, count_a, count_b, *kept, mask_row, inv1, inv2, norm1_gain, norm2_gain,
    )
    bits = bits_of("res")
    order_a, order_b = bits, bits[1:2] + bits[:1] + bits[2:]
    rows_ab = node_rows // 2
    part_a = halve([(node_packed, 0)], rows_ab, "res", order_a[0])
    part_b = halve([(node_packed, rows_ab)], rows_ab, "res", order_b[0])
    edge_packed = after(edge_packed, up)
    edge_part = scattered_sum(edge_packed.reshape(parts * edge_rows, D), "nbr", nbr_bits)

    msg_rows = first_rows + narrow + 16
    share_rows = up_to(msg_rows + edge_rows, max(64, 8 * blocks))
    edges_grad, own_sum, far_sum, local_sum, msg_kept, msg_given = call(
        functools.partial(message_backward_kernel, parts),
        (
            shape((kn, rows, E), f32),
            shape((rows, D), bf16),
            shape((n_far, D), bf16),
            shape((rows, D), bf16),
            shape((parts // 2, msg_rows, D), bf16),
            shape((parts // 2, msg_rows, D), bf16),
        ),
        scratch=[
            pltpu.VMEM((width, D), f32),
            pltpu.VMEM((E, D), f32),
            pltpu.VMEM((D, D), f32),
            pltpu.VMEM((16, D), f32),
            pltpu.VMEM((rows, D), f32),
            pltpu.VMEM((3 * D + E, D), bf16),
        ],
        grid=grid,
        in_specs=[
            smem,
            fixed(SLOT, rows),
            edge_tile,
            flat,
            flat,
            flat,
            fixed(rows, D),
            flat_edge,
            fixed(rows, D),
            fixed(n_far, D),
            fixed(2 * D + E, D),
            fixed(D, D),
            fixed(16, D),
        ],
        out_specs=(edge_tile, fixed(rows, D), fixed(n_far, D), fixed(rows, D))
        + (fixed(parts // 2, msg_rows, D),) * 2,
        cost=pl.CostEstimate(flops=16 * total * D * D, bytes_accessed=total * D * 10, transcendentals=0),
    )(nbr_place & 1, *read(place_row, edges, act1, d1, d2), up, *read(base), ready_nodes, ready_far, ready_w1, ready_w2, node_bias)

    far_sum, msg_kept, msg_given, part_a, part_b = held_together(far_sum, msg_kept, msg_given, part_a, part_b)
    flat_rows = parts // 2 * msg_rows
    msg_part = add_low(msg_kept, swap(msg_given, "nbr", 1)).reshape(flat_rows, D)
    part_a = halved_sum(total_of(part_a, rows_ab // 2), "res", order_a[1])
    part_b = halved_sum(total_of(part_b, rows_ab // 2), "res", order_b[1])
    middle, last = bits[2:-1], bits[-1]
    part_a = scattered_sum(part_a, "res", middle)
    part_b = scattered_sum(part_b, "res", middle)
    both = after(jnp.stack([part_a, part_b]), msg_part)
    msg_sum = scattered_sum(msg_part, "nbr", nbr_bits[1:])
    both = halved_sum(both, "res", last, 1)
    msg_sum = jnp.concatenate([msg_sum, edge_part, jnp.zeros((share_rows - msg_rows - edge_rows, D), bf16)], axis=0)
    msg_quarter = quarter_sum(msg_sum, "res", bits[:2])
    both = rejoined(after(both, msg_sum), "res", last, 1)
    far_back = exchange(after(far_sum, msg_sum), blocks)
    back = call(returned_last_kernel, shape((rows, D), bf16))(own_sum, local_sum, far_back, wanted, msg_w1)
    for bit in nbr_bits[:-1]:
        back = add_low(back, swap(back, "nbr", bit))
    back_b = swap(back, "nbr", nbr_bits[-1])
    msg_part = scattered_sum(msg_quarter, "res", middle)
    msg_part = add_low(msg_part, swap(msg_part, "res", last))
    part_a, part_b = both[0], both[1]
    part_a = rejoined(gathered_rows(part_a, "res", middle[::-1]), "res", order_a[1])
    part_b = rejoined(gathered_rows(part_b, "res", middle[::-1]), "res", order_b[1])
    part_a, part_b = after(part_a, msg_part), after(part_b, msg_part)
    other_a = swap(part_a, "res", order_a[0])
    other_b = swap(part_b, "res", order_b[0])
    msg_parts = quarters(gathered_rows(msg_part, "res", middle[::-1]), "res", bits[:2])

    def side(bit):
        return (lax.axis_index("res") // bit) & 1

    node_at = jnp.stack([side(order_a[0]), side(order_b[0])]).astype(jnp.int32)
    msg_at = jnp.stack([lax.axis_index("nbr"), 2 * side(bits[0]) + side(bits[1])]).astype(jnp.int32)
    nodes_grad, ffn_w1_grad, ffn_w2_grad, msg_w3_grad = call(
        functools.partial(node_weights_kernel, parts),
        (shape((rows, D), f32), shape((narrow, FF), f32), shape((wide, D), f32), shape((narrow, D), f32)),
        scratch=[pltpu.VMEM((node_rows, D), bf16)],
        in_specs=[smem] + [vmem] * 7,
    )(node_at, part_a, other_a, part_b, other_b, mixed_grad, back, back_b)
    (
        msg_w1_grad, msg_w2_grad, edge_w1_grad, edge_w2_grad, edge_w3_grad,
        edge_b1_grad, edge_b2_grad, edge_b3_grad, norm3_gain_grad, norm3_bias_grad,
        msg_b1_grad, msg_b2_grad, msg_b3_grad, norm1_gain_grad, norm1_bias_grad,
        ffn_b2_grad, norm2_gain_grad, norm2_bias_grad, ffn_b1_grad,
    ) = call(
        functools.partial(edge_message_weights_kernel, parts, edge_rows),
        (
            shape((first_rows, D), f32),
            shape((narrow, D), f32),
            shape((E, first_rows), f32),
            shape((second_rows, E), f32),
            shape((second_rows, E), f32),
        )
        + (shape((second_rows,), f32),) * 5
        + (shape((narrow,), f32),) * 8
        + (shape((wide,), f32),),
        scratch=[pltpu.VMEM((share_rows, D), bf16)],
        in_specs=[smem] + [vmem] * 4,
    )(msg_at, *msg_parts)
    return (
        sent,
        edges_out.transpose(1, 0, 2),
        nodes_grad,
        edges_grad.transpose(1, 0, 2),
        msg_w1_grad,
        msg_b1_grad,
        msg_w2_grad,
        msg_b2_grad,
        msg_w3_grad,
        msg_b3_grad,
        norm1_gain_grad,
        norm1_bias_grad,
        ffn_w1_grad,
        ffn_b1_grad,
        ffn_w2_grad,
        ffn_b2_grad,
        norm2_gain_grad,
        norm2_bias_grad,
        edge_w1_grad.T,
        edge_b1_grad,
        edge_w2_grad,
        edge_b2_grad,
        edge_w3_grad,
        edge_b3_grad,
        norm3_gain_grad,
        norm3_bias_grad,
    )


def solution(mesh):
    every = P()
    in_specs = (
        (P("res", None), P("res", "nbr", None), P("res", "nbr"), P("res"))
        + (every,) * 22
        + (P("res", None), P("res", "nbr", None))
    )
    matrix, vector = P("nbr", None), P("nbr")
    out_specs = (
        (P("res", None), P("res", "nbr", None), P("res", None), P("res", "nbr", None))
        + (matrix, vector) * 3
        + (vector, vector, matrix, vector, matrix, vector, vector, vector)
        + (matrix, vector) * 3
        + (vector, vector)
    )
    return jax.shard_map(on_device, mesh=mesh, in_specs=in_specs, out_specs=out_specs, check_vma=False)
```

```python
import functools

import jax
import jax.numpy as jnp
from jax import lax
from jax.experimental import pallas as pl
from jax.experimental.pallas import tpu as pltpu
from jax.sharding import PartitionSpec as P

D = 512
E = 192
FF = 2048
FAR = 32
SLOT = 16
KT = 5
VMEM = 32 * 1024 * 1024

bf16 = jnp.bfloat16
f32 = jnp.float32


def mm(a, b):
    return jnp.dot(a, b, preferred_element_type=f32)


def mm_tn(a, b):
    return lax.dot_general(a, b, (((0,), (0,)), ((), ())), preferred_element_type=f32)


def mm_nt(a, b):
    return lax.dot_general(a, b, (((1,), (1,)), ((), ())), preferred_element_type=f32)


def gelu_pair(v):
    c0 = 0.7978845608028654
    c1 = 0.044715 * c0
    square = v * v
    t = jnp.tanh(v * (c0 + c1 * square))
    half = 0.5 + 0.5 * t
    act = v * half
    return act, half + act * (1.0 - t) * (c0 + (3.0 * c1) * square)


def gelu(v):
    t = jnp.tanh(v * (0.7978845608028654 + (0.044715 * 0.7978845608028654) * (v * v)))
    half = 0.5 * v
    return half + half * t


def norm_forward(values):
    centred = values - jnp.mean(values, axis=-1, keepdims=True)
    inverse = lax.rsqrt(jnp.mean(centred * centred, axis=-1, keepdims=True) + 1e-05)
    return centred * inverse, inverse


def norm_backward(upstream, normed, inverse, gain):
    scaled = upstream * gain
    first = jnp.mean(scaled, axis=-1, keepdims=True)
    second = jnp.mean(scaled * normed, axis=-1, keepdims=True)
    return inverse * (scaled - first - normed * second)


def row_of(ref):
    return ref[...].astype(f32).reshape(1, ref.shape[0])


def column_sum(values):
    return jnp.sum(values, axis=0, keepdims=True)


def iota(shape, dim):
    return lax.broadcasted_iota(jnp.int32, shape, dim)


def present_column(mask_ref, rows):
    real = jnp.sum(mask_ref[...].astype(f32), axis=1, keepdims=True)
    return (iota((rows, 1), 0).astype(f32) < real).astype(f32)


def pick_matrix(want_ref, rows):
    want = want_ref[...][:, :1].astype(f32)
    return (want == iota((want.shape[0], rows), 1).astype(f32)).astype(bf16)


def one_hot(column, width):
    return (column == iota((column.shape[0], width), 1)).astype(bf16)


def columns_of(col_ref, first, count):
    values = col_ref[...]
    lane = iota(values.shape, 1)
    return [
        jnp.sum(jnp.where(lane == first + j, values, 0.0), axis=1, keepdims=True).astype(jnp.int32)
        for j in range(count)
    ]


def kept_weight(columns):
    return jnp.concatenate([(column >= 0).astype(f32) for column in columns], axis=0)


def spread(rows, values):
    n, c = rows.shape
    return (values.reshape(-1, n, c) + rows[None]).reshape(values.shape)


def gathered(values, n):
    return jnp.sum(values.reshape(-1, n, values.shape[1]), axis=0)


def slot_sums(row_ref, first, count, width, values, acc):
    n = row_ref.shape[1]
    for j in range(count):
        row = row_ref[pl.ds(first + j, 1), :]
        hot = (row == iota((width, n), 0)).astype(bf16)
        acc[...] += mm(hot, values[j * n : (j + 1) * n])


def index_kernel(blocks, me_ref, near_ref, mask_ref, row_ref, col_ref, want_ref):
    kn, rows = near_ref.shape
    me = me_ref[0].astype(f32)
    lanes = max(16, blocks)
    index = near_ref[...].astype(f32)
    block = jnp.floor((index + 0.5) * (1.0 / rows))
    slot = index - block * rows
    local = block == me
    far_block = jnp.where(local, -1.0, block)
    real = jnp.sum(mask_ref[...].astype(f32), axis=1, keepdims=True)
    own_place = iota((kn, rows), 1).astype(f32)
    kept = jnp.logical_and(jnp.logical_or(jnp.logical_not(local), slot < real), own_place < real)
    slot_line = iota((rows, rows), 0).astype(f32)
    block_line = iota((lanes, rows), 0).astype(f32)
    hot_slot = [(slot[k : k + 1] == slot_line).astype(bf16) for k in range(kn)]
    hot_block = [(far_block[k : k + 1] == block_line).astype(bf16) for k in range(kn)]
    named = mm_nt(hot_block[0], hot_slot[0])
    for k in range(1, kn):
        named = named + mm_nt(hot_block[k], hot_slot[k])
    flags = (named > 0.0).astype(f32)
    before = (iota((rows, rows), 0) < iota((rows, rows), 1)).astype(bf16)
    rank = mm(flags.astype(bf16), before)
    key = jnp.where(flags > 0.0, rank, -1.0)[:blocks]
    key = jnp.broadcast_to(key[:, None, :], (blocks, FAR, rows)).reshape(blocks * FAR, rows)
    level = (iota((blocks * FAR, 1), 0) & (FAR - 1)).astype(f32)
    hit = (key == level).astype(f32)
    place_row = iota((blocks * FAR, rows), 1).astype(f32)
    want = jnp.sum(hit * place_row, axis=1, keepdims=True)
    found = jnp.sum(hit, axis=1, keepdims=True)
    want = jnp.where(found > 0.0, want, 255.0)
    want_ref[...] = jnp.broadcast_to(want, want_ref.shape).astype(bf16)
    after = (iota((rows, rows), 0) > iota((rows, rows), 1)).astype(bf16)
    rank_down = mm_nt(after, flags.astype(bf16)).astype(bf16)
    edge_rank = jnp.concatenate(
        [
            jnp.sum(mm(rank_down, hot_block[k]) * hot_slot[k].astype(f32), axis=0, keepdims=True)
            for k in range(kn)
        ],
        axis=0,
    )
    place = jnp.where(local, blocks * FAR + slot, block * FAR + edge_rank)
    place = jnp.where(kept, place, -1.0)
    place = jnp.concatenate([place, jnp.full((SLOT - kn, rows), -1.0, f32)], axis=0)
    row_ref[...] = place.astype(jnp.int32)
    col_ref[...] = place.T


def message_forward_kernel(
    col_ref, edges_ref, nodes_ref, far_ref, w1_ref, w2_ref, b1_ref, b2_ref,
    act1_ref, pre1_ref, pre2_ref, sum_ref, table, own, acc,
):
    step = pl.program_id(0)
    last = pl.num_programs(0) - 1
    kt, rows, _ = edges_ref.shape
    n_far = far_ref.shape[0]
    width = table.shape[0]

    @pl.when(step == 0)
    def _():
        weight = w1_ref[D : 2 * D, :]
        table[:n_far] = mm(far_ref[...], weight).astype(bf16)
        table[n_far:] = mm(nodes_ref[...], weight).astype(bf16)
        own[...] = mm(nodes_ref[...], w1_ref[:D, :]) + row_of(b1_ref)
        acc[...] = jnp.zeros_like(acc)

    each = range(kt)
    places = [pl.ds(j * rows, rows) for j in each]
    columns = columns_of(col_ref, step * kt, kt)
    pre1 = [mm(one_hot(columns[j], width), table[...]) + mm(edges_ref[j], w1_ref[2 * D :, :]) for j in each]
    act1 = []
    for j in each:
        total = pre1[j] + own[...]
        pre1_ref[places[j], :] = total.astype(bf16)
        act1.append(gelu(total).astype(bf16))
        act1_ref[places[j], :] = act1[j]
    pre2 = [mm(act1[j], w2_ref[...]) for j in each]
    for j in each:
        total = jnp.where(columns[j] >= 0, pre2[j] + row_of(b2_ref), -30.0)
        pre2_ref[places[j], :] = total.astype(bf16)
        acc[...] += gelu(total)

    @pl.when(step == last)
    def _():
        sum_ref[:, :D] = acc[...].astype(bf16)
        counts = jnp.sum((col_ref[...] >= 0.0).astype(f32), axis=1, keepdims=True)
        sum_ref[:, D:] = jnp.broadcast_to(counts, (sum_ref.shape[0], 128)).astype(bf16)


def slope_kernel(pre_ref, slope_ref):
    slope_ref[...] = gelu_pair(pre_ref[...].astype(f32))[1].astype(bf16)


def node_forward_kernel(
    sum_a, sum_b, nodes_ref, mask_ref, want_ref, w3_ref, f1_ref, f2_ref,
    b3_ref, gain1_ref, bias1_ref, fb1_ref, fb2_ref, gain2_ref, bias2_ref,
    total_ref, low_ref, normed1_ref, inv1_ref, hid_ref, slope_ref, normed2_ref, inv2_ref, count_ref, sent_ref, send_ref,
):
    rows = nodes_ref.shape[0]
    present = present_column(mask_ref, rows)
    counts = sum_a[:, D:].astype(f32) + sum_b[:, D:].astype(f32)
    count_ref[...] = counts
    count = counts[:, :1]
    total = sum_a[:, :D].astype(f32) + sum_b[:, :D].astype(f32)
    high = total.astype(bf16)
    total_ref[...] = high
    rest = (total - high.astype(f32)).astype(bf16)
    summed = mm(high, w3_ref[...]) + mm(rest, w3_ref[...]) + count * row_of(b3_ref)
    mixed = nodes_ref[...].astype(f32) + summed / jnp.maximum(count, 1.0)
    normed, inverse = norm_forward(mixed)
    normed1_ref[...] = normed
    inv1_ref[...] = inverse
    first = normed * row_of(gain1_ref) + row_of(bias1_ref)
    low = first.astype(bf16)
    low_ref[...] = low
    act, slope = gelu_pair(mm(low, f1_ref[...]) + row_of(fb1_ref))
    act = act.astype(bf16)
    hid_ref[...] = act
    slope_ref[...] = slope.astype(bf16)
    branch = mm(act, f2_ref[...]) + row_of(fb2_ref)
    normed, inverse = norm_forward(first + branch)
    normed2_ref[...] = normed
    inv2_ref[...] = inverse
    sent = (present * (normed * row_of(gain2_ref) + row_of(bias2_ref))).astype(bf16)
    sent_ref[...] = sent
    send_ref[...] = mm(pick_matrix(want_ref, rows), sent).astype(bf16)


def edge_kernel(
    row_ref, col_ref, edges_ref, cot_ref, sent_ref, far_ref, w1_ref, w2_ref, w3_ref, b1_ref, b2_ref, b3_ref, gain_ref, shift_ref,
    out_ref, base_ref, own_ref, far_grad_ref, local_grad_ref, w1_acc, w2_acc, w3_acc, bias_acc,
    table, own, sums, own_acc,
):
    step = pl.program_id(0)
    last = pl.num_programs(0) - 1
    kt, rows, _ = edges_ref.shape
    n_far = far_ref.shape[0]
    width = table.shape[0]

    @pl.when(step == 0)
    def _():
        weight = w1_ref[:, D : 2 * D]
        table[:n_far] = mm_nt(far_ref[...], weight).astype(bf16)
        table[n_far:] = mm_nt(sent_ref[...], weight).astype(bf16)
        own[...] = mm_nt(sent_ref[...], w1_ref[:, :D]) + row_of(b1_ref)
        for acc in (sums, w1_acc, w2_acc, w3_acc, bias_acc, own_acc):
            acc[...] = jnp.zeros_like(acc)

    edge = edges_ref[...].reshape(kt * rows, E)
    cot = cot_ref[...].reshape(kt * rows, E)
    columns = columns_of(col_ref, step * kt, kt)
    hot = jnp.concatenate([one_hot(column, width) for column in columns], axis=0)
    edge_weight = w1_ref[:, 2 * D :]
    pre1 = spread(own[...], mm(hot, table[...]) + mm_nt(edge, edge_weight))
    act, slope1 = gelu_pair(pre1)
    act1 = act.astype(bf16)
    act, slope2 = gelu_pair(mm(act1, w2_ref[...]) + row_of(b2_ref))
    act2 = act.astype(bf16)
    branch = mm(act2, w3_ref[...]) + row_of(b3_ref)
    weight = kept_weight(columns)
    normed, inverse = norm_forward(edge.astype(f32) + branch)
    gain = row_of(gain_ref)
    out = weight * (normed * gain + row_of(shift_ref))
    out_ref[...] = out.astype(bf16).reshape(kt, rows, E)
    up = weight * cot.astype(f32)
    grad = norm_backward(up, normed, inverse, gain)
    low3 = grad.astype(bf16)
    w3_acc[...] += mm_tn(act2, low3)
    low2 = (slope2 * mm_nt(low3, w3_ref[...])).astype(bf16)
    w2_acc[...] += mm_tn(act1, low2)
    low1 = (slope1 * mm_nt(low2, w2_ref[...])).astype(bf16)
    w1_acc[...] += mm_tn(edge, low1)
    slot_sums(row_ref, step * kt, kt, width, low1, sums)
    base_ref[...] = grad + mm(low1, edge_weight)
    own_sum = gathered(low1.astype(f32), rows)
    own_acc[...] += own_sum
    row = iota((16, 1), 0)
    bias_acc[...] += (
        jnp.where(row == 0, column_sum(own_sum), 0.0)
        + jnp.where(row == 1, column_sum(low2.astype(f32)), 0.0)
        + jnp.where(row == 2, column_sum(low3.astype(f32)), 0.0)
        + jnp.where(row == 3, column_sum(up * normed), 0.0)
        + jnp.where(row == 4, column_sum(up), 0.0)
    )

    @pl.when(step == last)
    def _():
        total = sums[...]
        own_ref[...] = own_acc[...].astype(bf16)
        far_grad_ref[...] = total[:n_far].astype(bf16)
        local_grad_ref[...] = total[n_far:].astype(bf16)


def edge_weights_kernel(
    order, sent_ref, far_ref, own_ref, far_grad_ref, local_grad_ref, w1_ref, w2_ref, w3_ref, bias_ref, packed_ref
):
    parts = len(order)
    first, second = (2 * D + E) // parts, E // parts
    sent = sent_ref[...]
    whole = jnp.concatenate(
        [
            mm_tn(sent, own_ref[...]),
            mm_tn(far_ref[...], far_grad_ref[...]) + mm_tn(sent, local_grad_ref[...]),
            w1_ref[...],
        ],
        axis=0,
    ).astype(bf16)
    second_w = w2_ref[...].astype(bf16)
    third_w = w3_ref[...].astype(bf16)
    bias = bias_ref[...].astype(bf16)
    half = packed_ref.shape[1]
    for q, n in enumerate(order):
        rows = jnp.concatenate(
            [
                whole[n * first : (n + 1) * first],
                second_w[n * second : (n + 1) * second],
                third_w[n * second : (n + 1) * second],
                bias,
            ],
            axis=0,
        )
        packed_ref[q, :, :E] = rows[:half]
        packed_ref[q, :, 256 : 256 + E] = rows[half:]
        packed_ref[q, :, E:256] = jnp.zeros((half, 256 - E), bf16)
        packed_ref[q, :, 256 + E :] = jnp.zeros((half, 256 - E), bf16)


def returned_kernel(own_ref, local_ref, back_ref, want_ref, out_ref):
    rows = local_ref.shape[0]
    near = local_ref[...].astype(f32) + mm_tn(pick_matrix(want_ref, rows), back_ref[...])
    out_ref[...] = jnp.concatenate([own_ref[...], near.astype(bf16)], axis=1)


def returned_last_kernel(own_ref, local_ref, back_ref, want_ref, w1_ref, out_ref):
    rows = local_ref.shape[0]
    near = local_ref[...].astype(f32) + mm_tn(pick_matrix(want_ref, rows), back_ref[...])
    grad = mm_nt(own_ref[...], w1_ref[:D, :]) + mm_nt(near.astype(bf16), w1_ref[D : 2 * D, :])
    out_ref[...] = grad.astype(bf16)


def fetch_kernel(*refs):
    *refs, arrivals = refs
    count = len(refs) // 2
    copies = [pltpu.make_async_copy(refs[i], refs[count + i], arrivals.at[i]) for i in range(count)]
    for copy in copies:
        copy.start()
    for copy in copies:
        copy.wait()


def fetched(*values):
    size = sum(value.size * value.dtype.itemsize for value in values)
    return pl.pallas_call(
        fetch_kernel,
        out_shape=tuple(pltpu.VMEM(value.shape, value.dtype) for value in values),
        in_specs=[pl.BlockSpec(memory_space=pltpu.HBM)] * len(values),
        out_specs=tuple(pl.BlockSpec(memory_space=pltpu.VMEM) for _ in values),
        scratch_shapes=[pltpu.SemaphoreType.DMA((len(values),))],
        compiler_params=pltpu.CompilerParams(vmem_limit_bytes=VMEM),
        cost_estimate=pl.CostEstimate(flops=0, bytes_accessed=2 * size, transcendentals=0),
    )(*read(*values))


def node_backward_kernel(
    parts, place_ref, back_a, back_b, count_ref, cot_ref, normed2_ref, ew1_ref, f2_ref, slope_ref, f1_ref,
    normed1_ref, w3_ref, low_ref, hid_ref, total_ref, mask_ref, inv1_ref, inv2_ref, gain1_ref, gain2_ref,
    mixed_ref, up_ref, bias_ref, packed_ref,
):
    rows = cot_ref.shape[0]
    place = place_ref[0]
    present = present_column(mask_ref, rows)
    count = count_ref[...][:, :1]
    back = (back_a[...].astype(f32) + back_b[...].astype(f32)).astype(bf16)
    node_back = mm(back[:, :E], ew1_ref[:, :D]) + mm(back[:, E:], ew1_ref[:, D : 2 * D])
    up = present * (cot_ref[...].astype(f32) + node_back)
    normed2 = normed2_ref[...]
    sum_grad = norm_backward(up, normed2, inv2_ref[...], row_of(gain2_ref))
    branch_grad = sum_grad.astype(bf16)
    hidden_grad = (slope_ref[...].astype(f32) * mm_nt(branch_grad, f2_ref[...])).astype(bf16)
    first_grad = sum_grad + mm_nt(hidden_grad, f1_ref[...])
    normed1 = normed1_ref[...]
    mixed_grad = norm_backward(first_grad, normed1, inv1_ref[...], row_of(gain1_ref))
    mixed_ref[...] = mixed_grad
    message_grad = (mixed_grad / jnp.maximum(count, 1.0)).astype(bf16)
    up_ref[...] = mm_nt(message_grad, w3_ref[...])
    row = iota((16, 1), 0)
    hidden_sum = column_sum(hidden_grad.astype(f32))
    bias = (
        jnp.where(row == 2, column_sum(count * message_grad.astype(f32)), 0.0)
        + jnp.where(row == 3, column_sum(first_grad * normed1), 0.0)
        + jnp.where(row == 4, column_sum(first_grad), 0.0)
        + jnp.where(row == 5, column_sum(branch_grad.astype(f32)), 0.0)
        + jnp.where(row == 6, column_sum(up * normed2), 0.0)
        + jnp.where(row == 7, column_sum(up), 0.0)
    )
    for j in range(FF // D):
        bias = bias + jnp.where(row == 8 + j, hidden_sum[:, j * D : (j + 1) * D], 0.0)
    bias_ref[...] = bias * (1.0 / parts)
    wide, narrow = FF // parts, D // parts
    low = low_ref[:, pl.ds(pl.multiple_of(place * narrow, narrow), narrow)]
    for j in range(FF // D):
        packed_ref[j * narrow : (j + 1) * narrow, :] = mm_tn(low, hidden_grad[:, j * D : (j + 1) * D]).astype(bf16)
    hid = hid_ref[:, pl.ds(pl.multiple_of(place * wide, wide), wide)]
    packed_ref[D : D + wide, :] = mm_tn(hid, branch_grad).astype(bf16)
    total = total_ref[:, pl.ds(pl.multiple_of(place * narrow, narrow), narrow)]
    packed_ref[D + wide : D + wide + narrow, :] = mm_tn(total, message_grad).astype(bf16)
    at = D + wide + narrow
    if packed_ref.shape[0] > at:
        packed_ref[at:, :] = jnp.zeros((packed_ref.shape[0] - at, D), bf16)


def message_backward_kernel(
    parts, core_ref, row_ref, edges_ref, act1_ref, d1_ref, d2_ref, up_ref, base_ref, nodes_ref, far_ref, w1_ref, w2_ref, node_bias_ref,
    out_ref, own_ref, far_grad_ref, local_grad_ref, kept_ref, given_ref,
    sums, w1_acc, w2_acc, bias_acc, own_acc, whole,
):
    step = pl.program_id(0)
    last = pl.num_programs(0) - 1
    kt, rows, _ = edges_ref.shape
    n_far = far_ref.shape[0]
    width = sums.shape[0]

    @pl.when(step == 0)
    def _():
        for acc in (sums, w1_acc, w2_acc, own_acc):
            acc[...] = jnp.zeros_like(acc)
        bias_acc[...] = node_bias_ref[...]

    edge = edges_ref[...].reshape(kt * rows, E)
    slope2 = d2_ref[...].astype(f32).reshape(kt, rows, D)
    grad2 = (slope2 * up_ref[...][None]).reshape(kt * rows, D)
    low2 = grad2.astype(bf16)
    w2_acc[...] += mm_tn(act1_ref[...], low2)
    grad1 = d1_ref[...].astype(f32) * mm_nt(low2, w2_ref[...])
    low1 = grad1.astype(bf16)
    w1_acc[...] += mm_tn(edge, low1)
    slot_sums(row_ref, step * kt, kt, width, low1, sums)
    grad = base_ref[...] + mm_nt(low1, w1_ref[2 * D :, :])
    out_ref[...] = grad.reshape(kt, rows, E)
    own_sum = gathered(grad1, rows)
    own_acc[...] += own_sum
    row = iota((16, 1), 0)
    bias_acc[...] += jnp.where(row == 0, column_sum(own_sum), 0.0) + jnp.where(
        row == 1, column_sum(grad2), 0.0
    )

    @pl.when(step == last)
    def _():
        total = sums[...]
        own_low = own_acc[...].astype(bf16)
        own_ref[...] = own_low
        far_grad_ref[...] = total[:n_far].astype(bf16)
        local_grad_ref[...] = total[n_far:].astype(bf16)
        nodes = nodes_ref[...]
        first = (2 * D + E) // parts
        second = D // parts
        whole[:D, :] = mm_tn(nodes, own_low).astype(bf16)
        whole[D : 2 * D, :] = (
            mm_tn(far_ref[...], total[:n_far].astype(bf16)) + mm_tn(nodes, total[n_far:].astype(bf16))
        ).astype(bf16)
        whole[2 * D : 2 * D + E, :] = w1_acc[...].astype(bf16)
        whole[2 * D + E :, :] = w2_acc[...].astype(bf16)
        bias = bias_acc[...].astype(bf16)
        half = kept_ref.shape[0]
        for ref, side in ((kept_ref, core_ref[0]), (given_ref, 1 - core_ref[0])):
            for q in range(half):
                n = q * 2 + side
                ref[q, :first, :] = whole[pl.ds(pl.multiple_of(n * first, 16), first), :]
                ref[q, first : first + second, :] = whole[
                    pl.ds(pl.multiple_of(2 * D + E + n * second, 16), second), :
                ]
                ref[q, first + second : first + second + 16, :] = bias


def picked_lanes(rows, place, parts):
    wide = rows.shape[1] // parts
    out = jnp.zeros((rows.shape[0], wide), f32)
    for n in range(parts):
        out = out + jnp.where(place == n, rows[:, n * wide : (n + 1) * wide], 0.0)
    return out


def joined(whole, index, piece):
    rows = piece.shape[0]
    whole[pl.ds(pl.multiple_of(index * rows, 16), rows), :] = piece[...]


def node_weights_kernel(
    parts, at_ref, a0, a1, b0, b1, mixed_ref, back_a, back_b, nodes_ref, f1_ref, f2_ref, w3_ref, whole
):
    nodes_ref[...] = mixed_ref[...] + (back_a[...].astype(f32) + back_b[...].astype(f32))
    top = whole.shape[0] // 2
    low, high = whole.at[:top], whole.at[top:]
    joined(low, at_ref[0], a0)
    joined(low, 1 - at_ref[0], a1)
    joined(high, at_ref[1], b0)
    joined(high, 1 - at_ref[1], b1)
    wide, narrow = FF // parts, D // parts
    for j in range(FF // D):
        f1_ref[:, j * D : (j + 1) * D] = whole[j * narrow : (j + 1) * narrow, :].astype(f32)
    f2_ref[...] = whole[D : D + wide, :].astype(f32)
    w3_ref[...] = whole[D + wide : D + wide + narrow, :].astype(f32)


def edge_message_weights_kernel(
    parts, half, at_ref, p0, p1, p2, p3, w1_ref, w2_ref, ew1_ref, ew2_ref, ew3_ref, *refs
):
    *vectors, fb1_ref, whole = refs
    for mask, piece in enumerate((p0, p1, p2, p3)):
        joined(whole, at_ref[1] ^ mask, piece)
    place = at_ref[0]
    first, narrow, second = (2 * D + E) // parts, D // parts, E // parts
    w1_ref[...] = whole[:first, :].astype(f32)
    w2_ref[...] = whole[first : first + narrow, :].astype(f32)
    at = first + narrow
    bias = whole[at : at + 16, :].astype(f32)
    rows = picked_lanes(bias[:8], place, parts)
    for j, ref in enumerate(vectors[5:]):
        ref[...] = rows[j : j + 1].reshape(narrow)
    hidden = jnp.zeros((1, D), f32)
    for n in range(FF // D):
        hidden = hidden + jnp.where(place == n, bias[8 + n : 9 + n], 0.0)
    fb1_ref[...] = hidden.reshape(FF // parts)
    at += 16
    edge = jnp.concatenate([whole[at : at + half, :E], whole[at : at + half, 256 : 256 + E]], axis=0).astype(f32)
    ew1_ref[...] = edge[:first].T
    ew2_ref[...] = edge[first : first + second]
    ew3_ref[...] = edge[first + second : first + 2 * second]
    rows = picked_lanes(edge[first + 2 * second : first + 2 * second + 8], place, parts)
    for j, ref in enumerate(vectors[:5]):
        ref[...] = rows[j : j + 1].reshape(second)


def swap(values, axis, bit):
    return lax.ppermute(values, axis, [(i, i ^ bit) for i in range(lax.axis_size(axis))])


def bits_of(axis):
    size, bit, out = lax.axis_size(axis), 1, []
    while bit < size:
        out.append(bit)
        bit *= 2
    return out


def add_low(a, b):
    return (a.astype(f32) + b.astype(f32)).astype(bf16)


def shared_sum(values, axis):
    bits = bits_of(axis)
    for bit in bits[:-1]:
        values = add_low(values, swap(values, axis, bit))
    return values, swap(values, axis, bits[-1])


def after(values, *earlier):
    return lax.optimization_barrier((values, *earlier))[0]


def halved_sum(values, axis, bit, dim=0):
    half = values.shape[dim] // 2
    side = (lax.axis_index(axis) // bit) & 1
    kept = lax.dynamic_slice_in_dim(values, side * half, half, dim)
    given = lax.dynamic_slice_in_dim(values, (1 - side) * half, half, dim)
    return add_low(kept, swap(given, axis, bit))


def rejoined(values, axis, bit, dim=0):
    other = swap(values, axis, bit)
    side = (lax.axis_index(axis) // bit) & 1
    return jnp.where(
        side == 0, jnp.concatenate([values, other], axis=dim), jnp.concatenate([other, values], axis=dim)
    )


def scattered_sum(values, axis, bits):
    for bit in bits:
        values = halved_sum(values, axis, bit)
    return values


def gathered_rows(values, axis, bits):
    for bit in bits:
        values = rejoined(values, axis, bit)
    return values


def total_of(addends, rows):
    total = 0.0
    for values, start in addends:
        total = total + lax.dynamic_slice_in_dim(values, start, rows, 0).astype(f32)
    return total.astype(bf16)


def halve(addends, rows, axis, bit):
    half = rows // 2
    side = (lax.axis_index(axis) // bit) & 1
    given = total_of([(values, start + (1 - side) * half) for values, start in addends], half)
    return [(values, start + side * half) for values, start in addends] + [(swap(given, axis, bit), 0)]


def quarter_sum(values, axis, bits):
    rows = values.shape[0] // 4
    low, high = ((lax.axis_index(axis) // bit) & 1 for bit in bits)
    mine = 2 * low + high
    total = lax.dynamic_slice_in_dim(values, mine * rows, rows, 0).astype(f32)
    for mask in (1, 2, 3):
        given = lax.dynamic_slice_in_dim(values, (mine ^ mask) * rows, rows, 0)
        total = total + swap(given, axis, (mask >> 1) * bits[0] + (mask & 1) * bits[1]).astype(f32)
    return total.astype(bf16)


def held_together(*lists):
    flat = []
    for item in lists:
        flat += [values for values, _ in item] if isinstance(item, list) else [item]
    flat = iter(lax.optimization_barrier(tuple(flat)))
    return tuple(
        [(next(flat), start) for _, start in item] if isinstance(item, list) else next(flat) for item in lists
    )


def quarters(values, axis, bits):
    return [values] + [swap(values, axis, (mask >> 1) * bits[0] + (mask & 1) * bits[1]) for mask in (1, 2, 3)]


def exchange(values, blocks):
    shaped = values.reshape((blocks, values.shape[0] // blocks) + values.shape[1:])
    return lax.all_to_all(shaped, "res", 0, 0, tiled=True).reshape(values.shape)


def call(kernel, outs, scratch=(), grid=None, in_specs=None, out_specs=None, cost=None):
    extra = {}
    if grid is not None:
        extra = dict(grid=grid, in_specs=in_specs, out_specs=out_specs)
    elif in_specs is not None:
        extra = dict(in_specs=in_specs)
    return pl.pallas_call(
        kernel,
        out_shape=outs,
        scratch_shapes=list(scratch),
        compiler_params=pltpu.CompilerParams(vmem_limit_bytes=VMEM),
        cost_estimate=cost,
        **extra,
    )


def shape(dims, dtype):
    return jax.ShapeDtypeStruct(dims, dtype)


def stored(dims, dtype):
    return pltpu.HBM(dims, dtype)


def read(*values):
    return tuple(pltpu.with_memory_space_constraint(value, pltpu.HBM) for value in values)


def up_to(value, unit):
    return -(-value // unit) * unit


def on_device(
    nodes,
    edges,
    neighbours,
    residue_mask,
    msg_w1,
    msg_b1,
    msg_w2,
    msg_b2,
    msg_w3,
    msg_b3,
    norm1_gain,
    norm1_bias,
    ffn_w1,
    ffn_b1,
    ffn_w2,
    ffn_b2,
    norm2_gain,
    norm2_bias,
    edge_w1,
    edge_b1,
    edge_w2,
    edge_b2,
    edge_w3,
    edge_b3,
    norm3_gain,
    norm3_bias,
    node_cot,
    edge_cot,
):
    rows, kn = neighbours.shape
    blocks, parts = lax.axis_size("res"), lax.axis_size("nbr")
    total = rows * kn
    n_far = blocks * FAR
    width = n_far + rows
    kt = next(t for t in (KT, 3, 1) if kn % t == 0)
    grid = (kn // kt,)
    nbr_bits = bits_of("nbr")
    order = tuple(
        sum(bit for i, bit in enumerate(nbr_bits) if (q >> (len(nbr_bits) - 1 - i)) & 1) for q in range(parts)
    )
    mask_row = residue_mask.reshape(1, rows)
    edges = edges.transpose(1, 0, 2)
    edge_cot = edge_cot.transpose(1, 0, 2)
    edge_w1 = edge_w1.T
    res_place = lax.axis_index("res").astype(jnp.int32).reshape(1)
    nbr_place = lax.axis_index("nbr").astype(jnp.int32).reshape(1)

    smem = pl.BlockSpec(memory_space=pltpu.SMEM)
    vmem = pl.BlockSpec(memory_space=pltpu.VMEM)

    def fixed(*dims):
        return pl.BlockSpec(dims, lambda i: (0,) * len(dims))

    def tiled(*dims):
        return pl.BlockSpec(dims, lambda i: (i,) + (0,) * (len(dims) - 1))

    place_row, place_col, want = call(
        functools.partial(index_kernel, blocks),
        (
            shape((SLOT, rows), jnp.int32),
            shape((rows, SLOT), f32),
            shape((n_far, 128), bf16),
        ),
        in_specs=[smem, vmem, vmem],
    )(res_place, *read(neighbours.T, mask_row))
    together = lax.optimization_barrier
    wanted = exchange(want, blocks)

    picks = (wanted[:, :1].astype(jnp.int32) == iota((n_far, rows), 1)).astype(bf16)
    far_nodes = exchange(mm(picks, nodes).astype(bf16), blocks)

    edge_tile = tiled(kt, rows, E)
    flat = tiled(kt * rows, D)
    flat_edge = tiled(kt * rows, E)
    kf = 3 if kn % 3 == 0 else 1
    act1, pre1, pre2, act_sum = call(
        message_forward_kernel,
        (stored((total, D), bf16),) * 3 + (shape((rows, D + 128), bf16),),
        scratch=[pltpu.VMEM((width, D), bf16), pltpu.VMEM((rows, D), f32), pltpu.VMEM((rows, D), f32)],
        grid=(kn // kf,),
        in_specs=[
            fixed(rows, SLOT),
            tiled(kf, rows, E),
            fixed(rows, D),
            fixed(n_far, D),
            fixed(2 * D + E, D),
            fixed(D, D),
            fixed(D),
            fixed(D),
        ],
        out_specs=(tiled(kf * rows, D),) * 3 + (fixed(rows, D + 128),),
        cost=pl.CostEstimate(flops=16 * total * D * D, bytes_accessed=total * D * 8, transcendentals=2 * total * D),
    )(*read(place_col, edges, nodes), far_nodes, *read(msg_w1, msg_w2, msg_b1, msg_b2))

    def slope_of(pre):
        return call(
            slope_kernel,
            stored((total, D), bf16),
            grid=grid,
            in_specs=[flat],
            out_specs=flat,
            cost=pl.CostEstimate(flops=10 * total * D, bytes_accessed=total * D * 4, transcendentals=total * D),
        )(*read(pre))

    d1 = slope_of(pre1)
    sum_a, sum_b = shared_sum(act_sum, "nbr")
    sum_b = after(sum_b, d1)

    total_act, first_low, normed1, inv1, hidden, hidden_slope, normed2, inv2, counts, sent, send = call(
        node_forward_kernel,
        (
            stored((rows, D), bf16),
            stored((rows, D), bf16),
            stored((rows, D), f32),
            stored((rows, 1), f32),
            stored((rows, FF), bf16),
            stored((rows, FF), bf16),
            stored((rows, D), f32),
            stored((rows, 1), f32),
            stored((rows, 128), f32),
            stored((rows, D), bf16),
            shape((n_far, D), bf16),
        ),
    )(sum_a, sum_b, nodes, mask_row, wanted, msg_w3, ffn_w1, ffn_w2,
      msg_b3, norm1_gain, norm1_bias, ffn_b1, ffn_b2, norm2_gain, norm2_bias)
    d2 = slope_of(after(pre2, send))
    far_sent = after(exchange(send, blocks), d2)

    first_rows, second_rows = (2 * D + E) // parts, E // parts
    edge_rows = up_to(first_rows + 2 * second_rows + 16, 32) // 2
    edges_out, base, own_sum, far_sum, local_sum, *edge_sums = call(
        edge_kernel,
        (
            shape((kn, rows, E), bf16),
            stored((total, E), f32),
            stored((rows, E), bf16),
            stored((n_far, E), bf16),
            stored((rows, E), bf16),
            stored((E, E), f32),
            stored((E, E), f32),
            stored((E, E), f32),
            stored((16, E), f32),
        ),
        scratch=[
            pltpu.VMEM((width, E), bf16),
            pltpu.VMEM((rows, E), f32),
            pltpu.VMEM((width, E), f32),
            pltpu.VMEM((rows, E), f32),
        ],
        grid=grid,
        in_specs=[
            fixed(SLOT, rows),
            fixed(rows, SLOT),
            edge_tile,
            edge_tile,
            fixed(rows, D),
            fixed(n_far, D),
            fixed(E, 2 * D + E),
            fixed(E, E),
            fixed(E, E),
        ]
        + [fixed(E)] * 5,
        out_specs=(
            edge_tile,
            flat_edge,
            fixed(rows, E),
            fixed(n_far, E),
            fixed(rows, E),
            fixed(E, E),
            fixed(E, E),
            fixed(E, E),
            fixed(16, E),
        ),
        cost=pl.CostEstimate(flops=16 * total * D * D, bytes_accessed=total * E * 12, transcendentals=2 * total * E),
    )(*read(place_row, place_col, edges, edge_cot, sent), far_sent, *read(edge_w1, edge_w2, edge_w3),
      *read(edge_b1, edge_b2, edge_b3, norm3_gain, norm3_bias))

    edge_packed = call(
        functools.partial(edge_weights_kernel, order),
        stored((parts, edge_rows, D), bf16),
        cost=pl.CostEstimate(flops=10**9, bytes_accessed=10**6, transcendentals=0),
    )(*read(sent, far_sent, own_sum, far_sum, local_sum, *edge_sums))
    far_back = after(exchange(far_sum, blocks), edge_packed)
    back = call(returned_kernel, shape((rows, 2 * E), bf16))(*read(own_sum, local_sum), far_back, wanted)
    for bit in nbr_bits[:-1]:
        back = add_low(back, swap(back, "nbr", bit))
    kept = fetched(
        counts, after(node_cot, back), normed2, edge_w1, ffn_w2, hidden_slope, ffn_w1, normed1, msg_w3, first_low, hidden, total_act,
        msg_w1, msg_w2, nodes, far_nodes
    )
    *kept, ready_w1, ready_w2, ready_nodes, ready_far = kept
    back_a, back_b = back, swap(back, "nbr", nbr_bits[-1])

    wide, narrow = FF // parts, D // parts
    node_rows = up_to(D + wide + narrow, 16 * blocks)
    mixed_grad, up, node_bias, node_packed = call(
        functools.partial(node_backward_kernel, parts),
        (
            shape((rows, D), f32),
            shape((rows, D), f32),
            shape((16, D), f32),
            shape((node_rows, D), bf16),
        ),
        in_specs=[smem] + [vmem] * 19,
    )(
        nbr_place, back_a, back_b, *kept, mask_row, inv1, inv2, norm1_gain, norm2_gain,
    )
    bits = bits_of("res")
    order_a, order_b = bits, bits[1:2] + bits[:1] + bits[2:]
    rows_ab = node_rows // 2
    part_a = halve([(node_packed, 0)], rows_ab, "res", order_a[0])
    part_b = halve([(node_packed, rows_ab)], rows_ab, "res", order_b[0])
    edge_packed = after(edge_packed, up)
    edge_part = scattered_sum(edge_packed.reshape(parts * edge_rows, D), "nbr", nbr_bits)

    msg_rows = first_rows + narrow + 16
    share_rows = up_to(msg_rows + edge_rows, max(64, 8 * blocks))
    edges_grad, own_sum, far_sum, local_sum, msg_kept, msg_given = call(
        functools.partial(message_backward_kernel, parts),
        (
            shape((kn, rows, E), f32),
            shape((rows, D), bf16),
            shape((n_far, D), bf16),
            shape((rows, D), bf16),
            shape((parts // 2, msg_rows, D), bf16),
            shape((parts // 2, msg_rows, D), bf16),
        ),
        scratch=[
            pltpu.VMEM((width, D), f32),
            pltpu.VMEM((E, D), f32),
            pltpu.VMEM((D, D), f32),
            pltpu.VMEM((16, D), f32),
            pltpu.VMEM((rows, D), f32),
            pltpu.VMEM((3 * D + E, D), bf16),
        ],
        grid=grid,
        in_specs=[
            smem,
            fixed(SLOT, rows),
            edge_tile,
            flat,
            flat,
            flat,
            fixed(rows, D),
            flat_edge,
            fixed(rows, D),
            fixed(n_far, D),
            fixed(2 * D + E, D),
            fixed(D, D),
            fixed(16, D),
        ],
        out_specs=(edge_tile, fixed(rows, D), fixed(n_far, D), fixed(rows, D))
        + (fixed(parts // 2, msg_rows, D),) * 2,
        cost=pl.CostEstimate(flops=16 * total * D * D, bytes_accessed=total * D * 10, transcendentals=0),
    )(nbr_place & 1, *read(place_row, edges, act1, d1, d2), up, *read(base), ready_nodes, ready_far, ready_w1, ready_w2, node_bias)

    far_sum, msg_kept, msg_given, part_a, part_b = held_together(far_sum, msg_kept, msg_given, part_a, part_b)
    flat_rows = parts // 2 * msg_rows
    msg_part = add_low(msg_kept, swap(msg_given, "nbr", 1)).reshape(flat_rows, D)
    part_a = halved_sum(total_of(part_a, rows_ab // 2), "res", order_a[1])
    part_b = halved_sum(total_of(part_b, rows_ab // 2), "res", order_b[1])
    middle, last = bits[2:-1], bits[-1]
    part_a = scattered_sum(part_a, "res", middle)
    part_b = scattered_sum(part_b, "res", middle)
    both = after(jnp.stack([part_a, part_b]), msg_part)
    msg_sum = scattered_sum(msg_part, "nbr", nbr_bits[1:])
    both = halved_sum(both, "res", last, 1)
    msg_sum = jnp.concatenate([msg_sum, edge_part, jnp.zeros((share_rows - msg_rows - edge_rows, D), bf16)], axis=0)
    msg_quarter = quarter_sum(msg_sum, "res", bits[:2])
    both = rejoined(after(both, msg_sum), "res", last, 1)
    far_back = exchange(after(far_sum, msg_sum), blocks)
    back = call(returned_last_kernel, shape((rows, D), bf16))(own_sum, local_sum, far_back, wanted, msg_w1)
    for bit in nbr_bits[:-1]:
        back = add_low(back, swap(back, "nbr", bit))
    back_b = swap(back, "nbr", nbr_bits[-1])
    msg_part = scattered_sum(msg_quarter, "res", middle)
    msg_part = add_low(msg_part, swap(msg_part, "res", last))
    part_a, part_b = both[0], both[1]
    part_a = rejoined(gathered_rows(part_a, "res", middle[::-1]), "res", order_a[1])
    part_b = rejoined(gathered_rows(part_b, "res", middle[::-1]), "res", order_b[1])
    part_a, part_b = after(part_a, msg_part), after(part_b, msg_part)
    other_a = swap(part_a, "res", order_a[0])
    other_b = swap(part_b, "res", order_b[0])
    msg_parts = quarters(gathered_rows(msg_part, "res", middle[::-1]), "res", bits[:2])

    def side(bit):
        return (lax.axis_index("res") // bit) & 1

    node_at = jnp.stack([side(order_a[0]), side(order_b[0])]).astype(jnp.int32)
    msg_at = jnp.stack([lax.axis_index("nbr"), 2 * side(bits[0]) + side(bits[1])]).astype(jnp.int32)
    nodes_grad, ffn_w1_grad, ffn_w2_grad, msg_w3_grad = call(
        functools.partial(node_weights_kernel, parts),
        (shape((rows, D), f32), shape((narrow, FF), f32), shape((wide, D), f32), shape((narrow, D), f32)),
        scratch=[pltpu.VMEM((node_rows, D), bf16)],
        in_specs=[smem] + [vmem] * 7,
    )(node_at, part_a, other_a, part_b, other_b, mixed_grad, back, back_b)
    (
        msg_w1_grad, msg_w2_grad, edge_w1_grad, edge_w2_grad, edge_w3_grad,
        edge_b1_grad, edge_b2_grad, edge_b3_grad, norm3_gain_grad, norm3_bias_grad,
        msg_b1_grad, msg_b2_grad, msg_b3_grad, norm1_gain_grad, norm1_bias_grad,
        ffn_b2_grad, norm2_gain_grad, norm2_bias_grad, ffn_b1_grad,
    ) = call(
        functools.partial(edge_message_weights_kernel, parts, edge_rows),
        (
            shape((first_rows, D), f32),
            shape((narrow, D), f32),
            shape((E, first_rows), f32),
            shape((second_rows, E), f32),
            shape((second_rows, E), f32),
        )
        + (shape((second_rows,), f32),) * 5
        + (shape((narrow,), f32),) * 8
        + (shape((wide,), f32),),
        scratch=[pltpu.VMEM((share_rows, D), bf16)],
        in_specs=[smem] + [vmem] * 4,
    )(msg_at, *msg_parts)
    return (
        sent,
        edges_out.transpose(1, 0, 2),
        nodes_grad,
        edges_grad.transpose(1, 0, 2),
        msg_w1_grad,
        msg_b1_grad,
        msg_w2_grad,
        msg_b2_grad,
        msg_w3_grad,
        msg_b3_grad,
        norm1_gain_grad,
        norm1_bias_grad,
        ffn_w1_grad,
        ffn_b1_grad,
        ffn_w2_grad,
        ffn_b2_grad,
        norm2_gain_grad,
        norm2_bias_grad,
        edge_w1_grad.T,
        edge_b1_grad,
        edge_w2_grad,
        edge_b2_grad,
        edge_w3_grad,
        edge_b3_grad,
        norm3_gain_grad,
        norm3_bias_grad,
    )


def solution(mesh):
    every = P()
    in_specs = (
        (P("res", None), P("res", "nbr", None), P("res", "nbr"), P("res"))
        + (every,) * 22
        + (P("res", None), P("res", "nbr", None))
    )
    matrix, vector = P("nbr", None), P("nbr")
    out_specs = (
        (P("res", None), P("res", "nbr", None), P("res", None), P("res", "nbr", None))
        + (matrix, vector) * 3
        + (vector, vector, matrix, vector, matrix, vector, vector, vector)
        + (matrix, vector) * 3
        + (vector, vector)
    )
    return jax.shard_map(on_device, mesh=mesh, in_specs=in_specs, out_specs=out_specs, check_vma=False)
```

```python
import functools

import jax
import jax.numpy as jnp
from jax import lax
from jax.experimental import pallas as pl
from jax.experimental.pallas import tpu as pltpu
from jax.sharding import PartitionSpec as P

D = 512
E = 192
FF = 2048
FAR = 32
SLOT = 16
KT = 5
VMEM = 32 * 1024 * 1024

bf16 = jnp.bfloat16
f32 = jnp.float32


def mm(a, b):
    return jnp.dot(a, b, preferred_element_type=f32)


def mm_tn(a, b):
    return lax.dot_general(a, b, (((0,), (0,)), ((), ())), preferred_element_type=f32)


def mm_nt(a, b):
    return lax.dot_general(a, b, (((1,), (1,)), ((), ())), preferred_element_type=f32)


def gelu_pair(v):
    c0 = 0.7978845608028654
    c1 = 0.044715 * c0
    square = v * v
    t = jnp.tanh(v * (c0 + c1 * square))
    half = 0.5 + 0.5 * t
    act = v * half
    return act, half + act * (1.0 - t) * (c0 + (3.0 * c1) * square)


def gelu(v):
    t = jnp.tanh(v * (0.7978845608028654 + (0.044715 * 0.7978845608028654) * (v * v)))
    half = 0.5 * v
    return half + half * t


def norm_forward(values):
    centred = values - jnp.mean(values, axis=-1, keepdims=True)
    inverse = lax.rsqrt(jnp.mean(centred * centred, axis=-1, keepdims=True) + 1e-05)
    return centred * inverse, inverse


def norm_backward(upstream, normed, inverse, gain):
    scaled = upstream * gain
    first = jnp.mean(scaled, axis=-1, keepdims=True)
    second = jnp.mean(scaled * normed, axis=-1, keepdims=True)
    return inverse * (scaled - first - normed * second)


def row_of(ref):
    return ref[...].astype(f32).reshape(1, ref.shape[0])


def column_sum(values):
    return jnp.sum(values, axis=0, keepdims=True)


def iota(shape, dim):
    return lax.broadcasted_iota(jnp.int32, shape, dim)


def present_column(mask_ref, rows):
    real = jnp.sum(mask_ref[...].astype(f32), axis=1, keepdims=True)
    return (iota((rows, 1), 0).astype(f32) < real).astype(f32)


def pick_matrix(want_ref, rows):
    want = want_ref[...][:, :1].astype(f32)
    return (want == iota((want.shape[0], rows), 1).astype(f32)).astype(bf16)


def one_hot(column, width):
    return (column == iota((column.shape[0], width), 1)).astype(bf16)


def columns_of(col_ref, first, count):
    values = col_ref[...]
    lane = iota(values.shape, 1)
    return [
        jnp.sum(jnp.where(lane == first + j, values, 0.0), axis=1, keepdims=True).astype(jnp.int32)
        for j in range(count)
    ]


def kept_weight(columns):
    return jnp.concatenate([(column >= 0).astype(f32) for column in columns], axis=0)


def spread(rows, values):
    n, c = rows.shape
    return (values.reshape(-1, n, c) + rows[None]).reshape(values.shape)


def gathered(values, n):
    return jnp.sum(values.reshape(-1, n, values.shape[1]), axis=0)


def slot_sums(row_ref, first, count, width, values, acc):
    n = row_ref.shape[1]
    for j in range(count):
        row = row_ref[pl.ds(first + j, 1), :]
        hot = (row == iota((width, n), 0)).astype(bf16)
        acc[...] += mm(hot, values[j * n : (j + 1) * n])


def index_kernel(blocks, me_ref, near_ref, mask_ref, row_ref, col_ref, want_ref):
    kn, rows = near_ref.shape
    me = me_ref[0].astype(f32)
    lanes = max(16, blocks)
    index = near_ref[...].astype(f32)
    block = jnp.floor((index + 0.5) * (1.0 / rows))
    slot = index - block * rows
    local = block == me
    far_block = jnp.where(local, -1.0, block)
    real = jnp.sum(mask_ref[...].astype(f32), axis=1, keepdims=True)
    own_place = iota((kn, rows), 1).astype(f32)
    kept = jnp.logical_and(jnp.logical_or(jnp.logical_not(local), slot < real), own_place < real)
    slot_line = iota((rows, rows), 0).astype(f32)
    block_line = iota((lanes, rows), 0).astype(f32)
    hot_slot = [(slot[k : k + 1] == slot_line).astype(bf16) for k in range(kn)]
    hot_block = [(far_block[k : k + 1] == block_line).astype(bf16) for k in range(kn)]
    named = mm_nt(hot_block[0], hot_slot[0])
    for k in range(1, kn):
        named = named + mm_nt(hot_block[k], hot_slot[k])
    flags = (named > 0.0).astype(f32)
    before = (iota((rows, rows), 0) < iota((rows, rows), 1)).astype(bf16)
    rank = mm(flags.astype(bf16), before)
    key = jnp.where(flags > 0.0, rank, -1.0)[:blocks]
    key = jnp.broadcast_to(key[:, None, :], (blocks, FAR, rows)).reshape(blocks * FAR, rows)
    level = (iota((blocks * FAR, 1), 0) & (FAR - 1)).astype(f32)
    hit = (key == level).astype(f32)
    place_row = iota((blocks * FAR, rows), 1).astype(f32)
    want = jnp.sum(hit * place_row, axis=1, keepdims=True)
    found = jnp.sum(hit, axis=1, keepdims=True)
    want = jnp.where(found > 0.0, want, 255.0)
    want_ref[...] = jnp.broadcast_to(want, want_ref.shape).astype(bf16)
    after = (iota((rows, rows), 0) > iota((rows, rows), 1)).astype(bf16)
    rank_down = mm_nt(after, flags.astype(bf16)).astype(bf16)
    edge_rank = jnp.concatenate(
        [
            jnp.sum(mm(rank_down, hot_block[k]) * hot_slot[k].astype(f32), axis=0, keepdims=True)
            for k in range(kn)
        ],
        axis=0,
    )
    place = jnp.where(local, blocks * FAR + slot, block * FAR + edge_rank)
    place = jnp.where(kept, place, -1.0)
    place = jnp.concatenate([place, jnp.full((SLOT - kn, rows), -1.0, f32)], axis=0)
    row_ref[...] = place.astype(jnp.int32)
    col_ref[...] = place.T


def message_forward_kernel(
    col_ref, edges_ref, nodes_ref, far_ref, w1_ref, w2_ref, b1_ref, b2_ref,
    act1_ref, pre1_ref, pre2_ref, sum_ref, table, own, acc,
):
    step = pl.program_id(0)
    last = pl.num_programs(0) - 1
    kt, rows, _ = edges_ref.shape
    n_far = far_ref.shape[0]
    width = table.shape[0]

    @pl.when(step == 0)
    def _():
        weight = w1_ref[D : 2 * D, :]
        table[:n_far] = mm(far_ref[...], weight).astype(bf16)
        table[n_far:] = mm(nodes_ref[...], weight).astype(bf16)
        own[...] = mm(nodes_ref[...], w1_ref[:D, :]) + row_of(b1_ref)
        acc[...] = jnp.zeros_like(acc)

    each = range(kt)
    places = [pl.ds(j * rows, rows) for j in each]
    columns = columns_of(col_ref, step * kt, kt)
    pre1 = [mm(one_hot(columns[j], width), table[...]) + mm(edges_ref[j], w1_ref[2 * D :, :]) for j in each]
    act1 = []
    for j in each:
        total = pre1[j] + own[...]
        pre1_ref[places[j], :] = total.astype(bf16)
        act1.append(gelu(total).astype(bf16))
        act1_ref[places[j], :] = act1[j]
    pre2 = [mm(act1[j], w2_ref[...]) for j in each]
    for j in each:
        total = jnp.where(columns[j] >= 0, pre2[j] + row_of(b2_ref), -30.0)
        pre2_ref[places[j], :] = total.astype(bf16)
        acc[...] += gelu(total)

    @pl.when(step == last)
    def _():
        sum_ref[:, :D] = acc[...].astype(bf16)
        counts = jnp.sum((col_ref[...] >= 0.0).astype(f32), axis=1, keepdims=True)
        sum_ref[:, D:] = jnp.broadcast_to(counts, (sum_ref.shape[0], 128)).astype(bf16)


def slope_kernel(pre_ref, slope_ref):
    slope_ref[...] = gelu_pair(pre_ref[...].astype(f32))[1].astype(bf16)


def node_forward_kernel(
    sum_a, sum_b, nodes_ref, mask_ref, want_ref, w3_ref, f1_ref, f2_ref,
    b3_ref, gain1_ref, bias1_ref, fb1_ref, fb2_ref, gain2_ref, bias2_ref,
    total_ref, low_ref, normed1_ref, inv1_ref, hid_ref, slope_ref, normed2_ref, inv2_ref, count_ref, sent_ref, send_ref,
):
    rows = nodes_ref.shape[0]
    present = present_column(mask_ref, rows)
    counts = sum_a[:, D:].astype(f32) + sum_b[:, D:].astype(f32)
    count_ref[...] = counts
    count = counts[:, :1]
    total = sum_a[:, :D].astype(f32) + sum_b[:, :D].astype(f32)
    high = total.astype(bf16)
    total_ref[...] = high
    rest = (total - high.astype(f32)).astype(bf16)
    summed = mm(high, w3_ref[...]) + mm(rest, w3_ref[...]) + count * row_of(b3_ref)
    mixed = nodes_ref[...].astype(f32) + summed / jnp.maximum(count, 1.0)
    normed, inverse = norm_forward(mixed)
    normed1_ref[...] = normed
    inv1_ref[...] = inverse
    first = normed * row_of(gain1_ref) + row_of(bias1_ref)
    low = first.astype(bf16)
    low_ref[...] = low
    act, slope = gelu_pair(mm(low, f1_ref[...]) + row_of(fb1_ref))
    act = act.astype(bf16)
    hid_ref[...] = act
    slope_ref[...] = slope.astype(bf16)
    branch = mm(act, f2_ref[...]) + row_of(fb2_ref)
    normed, inverse = norm_forward(first + branch)
    normed2_ref[...] = normed
    inv2_ref[...] = inverse
    sent = (present * (normed * row_of(gain2_ref) + row_of(bias2_ref))).astype(bf16)
    sent_ref[...] = sent
    send_ref[...] = mm(pick_matrix(want_ref, rows), sent).astype(bf16)


def edge_kernel(
    row_ref, col_ref, edges_ref, cot_ref, sent_ref, far_ref, w1_ref, w2_ref, w3_ref, b1_ref, b2_ref, b3_ref, gain_ref, shift_ref,
    out_ref, base_ref, own_ref, far_grad_ref, local_grad_ref, w1_acc, w2_acc, w3_acc, bias_acc,
    table, own, sums, own_acc,
):
    step = pl.program_id(0)
    last = pl.num_programs(0) - 1
    kt, rows, _ = edges_ref.shape
    n_far = far_ref.shape[0]
    width = table.shape[0]

    @pl.when(step == 0)
    def _():
        weight = w1_ref[:, D : 2 * D]
        table[:n_far] = mm_nt(far_ref[...], weight).astype(bf16)
        table[n_far:] = mm_nt(sent_ref[...], weight).astype(bf16)
        own[...] = mm_nt(sent_ref[...], w1_ref[:, :D]) + row_of(b1_ref)
        for acc in (sums, w1_acc, w2_acc, w3_acc, bias_acc, own_acc):
            acc[...] = jnp.zeros_like(acc)

    edge = edges_ref[...].reshape(kt * rows, E)
    cot = cot_ref[...].reshape(kt * rows, E)
    columns = columns_of(col_ref, step * kt, kt)
    hot = jnp.concatenate([one_hot(column, width) for column in columns], axis=0)
    edge_weight = w1_ref[:, 2 * D :]
    pre1 = spread(own[...], mm(hot, table[...]) + mm_nt(edge, edge_weight))
    act, slope1 = gelu_pair(pre1)
    act1 = act.astype(bf16)
    act, slope2 = gelu_pair(mm(act1, w2_ref[...]) + row_of(b2_ref))
    act2 = act.astype(bf16)
    branch = mm(act2, w3_ref[...]) + row_of(b3_ref)
    weight = kept_weight(columns)
    normed, inverse = norm_forward(edge.astype(f32) + branch)
    gain = row_of(gain_ref)
    out = weight * (normed * gain + row_of(shift_ref))
    out_ref[...] = out.astype(bf16).reshape(kt, rows, E)
    up = weight * cot.astype(f32)
    grad = norm_backward(up, normed, inverse, gain)
    low3 = grad.astype(bf16)
    w3_acc[...] += mm_tn(act2, low3)
    low2 = (slope2 * mm_nt(low3, w3_ref[...])).astype(bf16)
    w2_acc[...] += mm_tn(act1, low2)
    low1 = (slope1 * mm_nt(low2, w2_ref[...])).astype(bf16)
    w1_acc[...] += mm_tn(edge, low1)
    slot_sums(row_ref, step * kt, kt, width, low1, sums)
    base_ref[...] = (grad + mm(low1, edge_weight)).astype(bf16)
    own_sum = gathered(low1.astype(f32), rows)
    own_acc[...] += own_sum
    row = iota((16, 1), 0)
    bias_acc[...] += (
        jnp.where(row == 0, column_sum(own_sum), 0.0)
        + jnp.where(row == 1, column_sum(low2.astype(f32)), 0.0)
        + jnp.where(row == 2, column_sum(low3.astype(f32)), 0.0)
        + jnp.where(row == 3, column_sum(up * normed), 0.0)
        + jnp.where(row == 4, column_sum(up), 0.0)
    )

    @pl.when(step == last)
    def _():
        total = sums[...]
        own_ref[...] = own_acc[...].astype(bf16)
        far_grad_ref[...] = total[:n_far].astype(bf16)
        local_grad_ref[...] = total[n_far:].astype(bf16)


def edge_weights_kernel(
    order, sent_ref, far_ref, own_ref, far_grad_ref, local_grad_ref, w1_ref, w2_ref, w3_ref, bias_ref, packed_ref
):
    parts = len(order)
    first, second = (2 * D + E) // parts, E // parts
    sent = sent_ref[...]
    whole = jnp.concatenate(
        [
            mm_tn(sent, own_ref[...]),
            mm_tn(far_ref[...], far_grad_ref[...]) + mm_tn(sent, local_grad_ref[...]),
            w1_ref[...],
        ],
        axis=0,
    ).astype(bf16)
    second_w = w2_ref[...].astype(bf16)
    third_w = w3_ref[...].astype(bf16)
    bias = bias_ref[...].astype(bf16)
    half = packed_ref.shape[1]
    for q, n in enumerate(order):
        rows = jnp.concatenate(
            [
                whole[n * first : (n + 1) * first],
                second_w[n * second : (n + 1) * second],
                third_w[n * second : (n + 1) * second],
                bias,
            ],
            axis=0,
        )
        packed_ref[q, :, :E] = rows[:half]
        packed_ref[q, :, 256 : 256 + E] = rows[half:]
        packed_ref[q, :, E:256] = jnp.zeros((half, 256 - E), bf16)
        packed_ref[q, :, 256 + E :] = jnp.zeros((half, 256 - E), bf16)


def returned_kernel(own_ref, local_ref, back_ref, want_ref, out_ref):
    rows = local_ref.shape[0]
    near = local_ref[...].astype(f32) + mm_tn(pick_matrix(want_ref, rows), back_ref[...])
    out_ref[...] = jnp.concatenate([own_ref[...], near.astype(bf16)], axis=1)


def returned_last_kernel(own_ref, local_ref, back_ref, want_ref, w1_ref, out_ref):
    rows = local_ref.shape[0]
    near = local_ref[...].astype(f32) + mm_tn(pick_matrix(want_ref, rows), back_ref[...])
    grad = mm_nt(own_ref[...], w1_ref[:D, :]) + mm_nt(near.astype(bf16), w1_ref[D : 2 * D, :])
    out_ref[...] = grad.astype(bf16)


def fetch_kernel(*refs):
    *refs, arrivals = refs
    count = len(refs) // 2
    copies = [pltpu.make_async_copy(refs[i], refs[count + i], arrivals.at[i]) for i in range(count)]
    for copy in copies:
        copy.start()
    for copy in copies:
        copy.wait()


def fetched(*values):
    size = sum(value.size * value.dtype.itemsize for value in values)
    return pl.pallas_call(
        fetch_kernel,
        out_shape=tuple(pltpu.VMEM(value.shape, value.dtype) for value in values),
        in_specs=[pl.BlockSpec(memory_space=pltpu.HBM)] * len(values),
        out_specs=tuple(pl.BlockSpec(memory_space=pltpu.VMEM) for _ in values),
        scratch_shapes=[pltpu.SemaphoreType.DMA((len(values),))],
        compiler_params=pltpu.CompilerParams(vmem_limit_bytes=VMEM),
        cost_estimate=pl.CostEstimate(flops=0, bytes_accessed=2 * size, transcendentals=0),
    )(*read(*values))


def node_backward_kernel(
    parts, place_ref, back_a, back_b, count_ref, cot_ref, normed2_ref, ew1_ref, f2_ref, slope_ref, f1_ref,
    normed1_ref, w3_ref, low_ref, hid_ref, total_ref, mask_ref, inv1_ref, inv2_ref, gain1_ref, gain2_ref,
    mixed_ref, up_ref, bias_ref, packed_ref,
):
    rows = cot_ref.shape[0]
    place = place_ref[0]
    present = present_column(mask_ref, rows)
    count = count_ref[...][:, :1]
    back = (back_a[...].astype(f32) + back_b[...].astype(f32)).astype(bf16)
    node_back = mm(back[:, :E], ew1_ref[:, :D]) + mm(back[:, E:], ew1_ref[:, D : 2 * D])
    up = present * (cot_ref[...].astype(f32) + node_back)
    normed2 = normed2_ref[...]
    sum_grad = norm_backward(up, normed2, inv2_ref[...], row_of(gain2_ref))
    branch_grad = sum_grad.astype(bf16)
    hidden_grad = (slope_ref[...].astype(f32) * mm_nt(branch_grad, f2_ref[...])).astype(bf16)
    first_grad = sum_grad + mm_nt(hidden_grad, f1_ref[...])
    normed1 = normed1_ref[...]
    mixed_grad = norm_backward(first_grad, normed1, inv1_ref[...], row_of(gain1_ref))
    mixed_ref[...] = mixed_grad
    message_grad = (mixed_grad / jnp.maximum(count, 1.0)).astype(bf16)
    up_ref[...] = mm_nt(message_grad, w3_ref[...])
    row = iota((16, 1), 0)
    hidden_sum = column_sum(hidden_grad.astype(f32))
    bias = (
        jnp.where(row == 2, column_sum(count * message_grad.astype(f32)), 0.0)
        + jnp.where(row == 3, column_sum(first_grad * normed1), 0.0)
        + jnp.where(row == 4, column_sum(first_grad), 0.0)
        + jnp.where(row == 5, column_sum(branch_grad.astype(f32)), 0.0)
        + jnp.where(row == 6, column_sum(up * normed2), 0.0)
        + jnp.where(row == 7, column_sum(up), 0.0)
    )
    for j in range(FF // D):
        bias = bias + jnp.where(row == 8 + j, hidden_sum[:, j * D : (j + 1) * D], 0.0)
    bias_ref[...] = bias * (1.0 / parts)
    wide, narrow = FF // parts, D // parts
    low = low_ref[:, pl.ds(pl.multiple_of(place * narrow, narrow), narrow)]
    for j in range(FF // D):
        packed_ref[j * narrow : (j + 1) * narrow, :] = mm_tn(low, hidden_grad[:, j * D : (j + 1) * D]).astype(bf16)
    hid = hid_ref[:, pl.ds(pl.multiple_of(place * wide, wide), wide)]
    packed_ref[D : D + wide, :] = mm_tn(hid, branch_grad).astype(bf16)
    total = total_ref[:, pl.ds(pl.multiple_of(place * narrow, narrow), narrow)]
    packed_ref[D + wide : D + wide + narrow, :] = mm_tn(total, message_grad).astype(bf16)
    at = D + wide + narrow
    if packed_ref.shape[0] > at:
        packed_ref[at:, :] = jnp.zeros((packed_ref.shape[0] - at, D), bf16)


def message_backward_kernel(
    parts, core_ref, row_ref, edges_ref, act1_ref, d1_ref, d2_ref, up_ref, base_ref, nodes_ref, far_ref, w1_ref, w2_ref, node_bias_ref,
    out_ref, own_ref, far_grad_ref, local_grad_ref, kept_ref, given_ref,
    sums, w1_acc, w2_acc, bias_acc, own_acc, whole,
):
    step = pl.program_id(0)
    last = pl.num_programs(0) - 1
    kt, rows, _ = edges_ref.shape
    n_far = far_ref.shape[0]
    width = sums.shape[0]

    @pl.when(step == 0)
    def _():
        for acc in (sums, w1_acc, w2_acc, own_acc):
            acc[...] = jnp.zeros_like(acc)
        bias_acc[...] = node_bias_ref[...]

    edge = edges_ref[...].reshape(kt * rows, E)
    slope2 = d2_ref[...].astype(f32).reshape(kt, rows, D)
    grad2 = (slope2 * up_ref[...][None]).reshape(kt * rows, D)
    low2 = grad2.astype(bf16)
    w2_acc[...] += mm_tn(act1_ref[...], low2)
    grad1 = d1_ref[...].astype(f32) * mm_nt(low2, w2_ref[...])
    low1 = grad1.astype(bf16)
    w1_acc[...] += mm_tn(edge, low1)
    slot_sums(row_ref, step * kt, kt, width, low1, sums)
    grad = base_ref[...].astype(f32) + mm_nt(low1, w1_ref[2 * D :, :])
    out_ref[...] = grad.reshape(kt, rows, E)
    own_sum = gathered(grad1, rows)
    own_acc[...] += own_sum
    row = iota((16, 1), 0)
    bias_acc[...] += jnp.where(row == 0, column_sum(own_sum), 0.0) + jnp.where(
        row == 1, column_sum(grad2), 0.0
    )

    @pl.when(step == last)
    def _():
        total = sums[...]
        own_low = own_acc[...].astype(bf16)
        own_ref[...] = own_low
        far_grad_ref[...] = total[:n_far].astype(bf16)
        local_grad_ref[...] = total[n_far:].astype(bf16)
        nodes = nodes_ref[...]
        first = (2 * D + E) // parts
        second = D // parts
        whole[:D, :] = mm_tn(nodes, own_low).astype(bf16)
        whole[D : 2 * D, :] = (
            mm_tn(far_ref[...], total[:n_far].astype(bf16)) + mm_tn(nodes, total[n_far:].astype(bf16))
        ).astype(bf16)
        whole[2 * D : 2 * D + E, :] = w1_acc[...].astype(bf16)
        whole[2 * D + E :, :] = w2_acc[...].astype(bf16)
        bias = bias_acc[...].astype(bf16)
        half = kept_ref.shape[0]
        for ref, side in ((kept_ref, core_ref[0]), (given_ref, 1 - core_ref[0])):
            for q in range(half):
                n = q * 2 + side
                ref[q, :first, :] = whole[pl.ds(pl.multiple_of(n * first, 16), first), :]
                ref[q, first : first + second, :] = whole[
                    pl.ds(pl.multiple_of(2 * D + E + n * second, 16), second), :
                ]
                ref[q, first + second : first + second + 16, :] = bias


def picked_lanes(rows, place, parts):
    wide = rows.shape[1] // parts
    out = jnp.zeros((rows.shape[0], wide), f32)
    for n in range(parts):
        out = out + jnp.where(place == n, rows[:, n * wide : (n + 1) * wide], 0.0)
    return out


def joined(whole, index, piece):
    rows = piece.shape[0]
    whole[pl.ds(pl.multiple_of(index * rows, 16), rows), :] = piece[...]


def node_weights_kernel(
    parts, at_ref, a0, a1, b0, b1, mixed_ref, back_a, back_b, nodes_ref, f1_ref, f2_ref, w3_ref, whole
):
    nodes_ref[...] = mixed_ref[...] + (back_a[...].astype(f32) + back_b[...].astype(f32))
    top = whole.shape[0] // 2
    low, high = whole.at[:top], whole.at[top:]
    joined(low, at_ref[0], a0)
    joined(low, 1 - at_ref[0], a1)
    joined(high, at_ref[1], b0)
    joined(high, 1 - at_ref[1], b1)
    wide, narrow = FF // parts, D // parts
    for j in range(FF // D):
        f1_ref[:, j * D : (j + 1) * D] = whole[j * narrow : (j + 1) * narrow, :].astype(f32)
    f2_ref[...] = whole[D : D + wide, :].astype(f32)
    w3_ref[...] = whole[D + wide : D + wide + narrow, :].astype(f32)


def edge_message_weights_kernel(
    parts, half, at_ref, p0, p1, p2, p3, w1_ref, w2_ref, ew1_ref, ew2_ref, ew3_ref, *refs
):
    *vectors, fb1_ref, whole = refs
    for mask, piece in enumerate((p0, p1, p2, p3)):
        joined(whole, at_ref[1] ^ mask, piece)
    place = at_ref[0]
    first, narrow, second = (2 * D + E) // parts, D // parts, E // parts
    w1_ref[...] = whole[:first, :].astype(f32)
    w2_ref[...] = whole[first : first + narrow, :].astype(f32)
    at = first + narrow
    bias = whole[at : at + 16, :].astype(f32)
    rows = picked_lanes(bias[:8], place, parts)
    for j, ref in enumerate(vectors[5:]):
        ref[...] = rows[j : j + 1].reshape(narrow)
    hidden = jnp.zeros((1, D), f32)
    for n in range(FF // D):
        hidden = hidden + jnp.where(place == n, bias[8 + n : 9 + n], 0.0)
    fb1_ref[...] = hidden.reshape(FF // parts)
    at += 16
    edge = jnp.concatenate([whole[at : at + half, :E], whole[at : at + half, 256 : 256 + E]], axis=0).astype(f32)
    ew1_ref[...] = edge[:first].T
    ew2_ref[...] = edge[first : first + second]
    ew3_ref[...] = edge[first + second : first + 2 * second]
    rows = picked_lanes(edge[first + 2 * second : first + 2 * second + 8], place, parts)
    for j, ref in enumerate(vectors[:5]):
        ref[...] = rows[j : j + 1].reshape(second)


def swap(values, axis, bit):
    return lax.ppermute(values, axis, [(i, i ^ bit) for i in range(lax.axis_size(axis))])


def bits_of(axis):
    size, bit, out = lax.axis_size(axis), 1, []
    while bit < size:
        out.append(bit)
        bit *= 2
    return out


def add_low(a, b):
    return (a.astype(f32) + b.astype(f32)).astype(bf16)


def shared_sum(values, axis):
    bits = bits_of(axis)
    for bit in bits[:-1]:
        values = add_low(values, swap(values, axis, bit))
    return values, swap(values, axis, bits[-1])


def after(values, *earlier):
    return lax.optimization_barrier((values, *earlier))[0]


def halved_sum(values, axis, bit, dim=0):
    half = values.shape[dim] // 2
    side = (lax.axis_index(axis) // bit) & 1
    kept = lax.dynamic_slice_in_dim(values, side * half, half, dim)
    given = lax.dynamic_slice_in_dim(values, (1 - side) * half, half, dim)
    return add_low(kept, swap(given, axis, bit))


def rejoined(values, axis, bit, dim=0):
    other = swap(values, axis, bit)
    side = (lax.axis_index(axis) // bit) & 1
    return jnp.where(
        side == 0, jnp.concatenate([values, other], axis=dim), jnp.concatenate([other, values], axis=dim)
    )


def scattered_sum(values, axis, bits):
    for bit in bits:
        values = halved_sum(values, axis, bit)
    return values


def gathered_rows(values, axis, bits):
    for bit in bits:
        values = rejoined(values, axis, bit)
    return values


def total_of(addends, rows):
    total = 0.0
    for values, start in addends:
        total = total + lax.dynamic_slice_in_dim(values, start, rows, 0).astype(f32)
    return total.astype(bf16)


def halve(addends, rows, axis, bit):
    half = rows // 2
    side = (lax.axis_index(axis) // bit) & 1
    given = total_of([(values, start + (1 - side) * half) for values, start in addends], half)
    return [(values, start + side * half) for values, start in addends] + [(swap(given, axis, bit), 0)]


def quarter_sum(values, axis, bits):
    rows = values.shape[0] // 4
    low, high = ((lax.axis_index(axis) // bit) & 1 for bit in bits)
    mine = 2 * low + high
    total = lax.dynamic_slice_in_dim(values, mine * rows, rows, 0).astype(f32)
    for mask in (1, 2, 3):
        given = lax.dynamic_slice_in_dim(values, (mine ^ mask) * rows, rows, 0)
        total = total + swap(given, axis, (mask >> 1) * bits[0] + (mask & 1) * bits[1]).astype(f32)
    return total.astype(bf16)


def held_together(*lists):
    flat = []
    for item in lists:
        flat += [values for values, _ in item] if isinstance(item, list) else [item]
    flat = iter(lax.optimization_barrier(tuple(flat)))
    return tuple(
        [(next(flat), start) for _, start in item] if isinstance(item, list) else next(flat) for item in lists
    )


def quarters(values, axis, bits):
    return [values] + [swap(values, axis, (mask >> 1) * bits[0] + (mask & 1) * bits[1]) for mask in (1, 2, 3)]


def exchange(values, blocks):
    shaped = values.reshape((blocks, values.shape[0] // blocks) + values.shape[1:])
    return lax.all_to_all(shaped, "res", 0, 0, tiled=True).reshape(values.shape)


def call(kernel, outs, scratch=(), grid=None, in_specs=None, out_specs=None, cost=None):
    extra = {}
    if grid is not None:
        extra = dict(grid=grid, in_specs=in_specs, out_specs=out_specs)
    elif in_specs is not None:
        extra = dict(in_specs=in_specs)
    return pl.pallas_call(
        kernel,
        out_shape=outs,
        scratch_shapes=list(scratch),
        compiler_params=pltpu.CompilerParams(vmem_limit_bytes=VMEM),
        cost_estimate=cost,
        **extra,
    )


def shape(dims, dtype):
    return jax.ShapeDtypeStruct(dims, dtype)


def stored(dims, dtype):
    return pltpu.HBM(dims, dtype)


def read(*values):
    return tuple(pltpu.with_memory_space_constraint(value, pltpu.HBM) for value in values)


def up_to(value, unit):
    return -(-value // unit) * unit


def on_device(
    nodes,
    edges,
    neighbours,
    residue_mask,
    msg_w1,
    msg_b1,
    msg_w2,
    msg_b2,
    msg_w3,
    msg_b3,
    norm1_gain,
    norm1_bias,
    ffn_w1,
    ffn_b1,
    ffn_w2,
    ffn_b2,
    norm2_gain,
    norm2_bias,
    edge_w1,
    edge_b1,
    edge_w2,
    edge_b2,
    edge_w3,
    edge_b3,
    norm3_gain,
    norm3_bias,
    node_cot,
    edge_cot,
):
    rows, kn = neighbours.shape
    blocks, parts = lax.axis_size("res"), lax.axis_size("nbr")
    total = rows * kn
    n_far = blocks * FAR
    width = n_far + rows
    kt = next(t for t in (KT, 3, 1) if kn % t == 0)
    grid = (kn // kt,)
    nbr_bits = bits_of("nbr")
    order = tuple(
        sum(bit for i, bit in enumerate(nbr_bits) if (q >> (len(nbr_bits) - 1 - i)) & 1) for q in range(parts)
    )
    mask_row = residue_mask.reshape(1, rows)
    edges = edges.transpose(1, 0, 2)
    edge_cot = edge_cot.transpose(1, 0, 2)
    edge_w1 = edge_w1.T
    res_place = lax.axis_index("res").astype(jnp.int32).reshape(1)
    nbr_place = lax.axis_index("nbr").astype(jnp.int32).reshape(1)

    smem = pl.BlockSpec(memory_space=pltpu.SMEM)
    vmem = pl.BlockSpec(memory_space=pltpu.VMEM)

    def fixed(*dims):
        return pl.BlockSpec(dims, lambda i: (0,) * len(dims))

    def tiled(*dims):
        return pl.BlockSpec(dims, lambda i: (i,) + (0,) * (len(dims) - 1))

    place_row, place_col, want = call(
        functools.partial(index_kernel, blocks),
        (
            shape((SLOT, rows), jnp.int32),
            shape((rows, SLOT), f32),
            shape((n_far, 128), bf16),
        ),
        in_specs=[smem, vmem, vmem],
    )(res_place, *read(neighbours.T, mask_row))
    together = lax.optimization_barrier
    wanted = exchange(want, blocks)

    picks = (wanted[:, :1].astype(jnp.int32) == iota((n_far, rows), 1)).astype(bf16)
    far_nodes = exchange(mm(picks, nodes).astype(bf16), blocks)

    edge_tile = tiled(kt, rows, E)
    flat = tiled(kt * rows, D)
    flat_edge = tiled(kt * rows, E)
    kf = 3 if kn % 3 == 0 else 1
    act1, pre1, pre2, act_sum = call(
        message_forward_kernel,
        (stored((total, D), bf16),) * 3 + (shape((rows, D + 128), bf16),),
        scratch=[pltpu.VMEM((width, D), bf16), pltpu.VMEM((rows, D), f32), pltpu.VMEM((rows, D), f32)],
        grid=(kn // kf,),
        in_specs=[
            fixed(rows, SLOT),
            tiled(kf, rows, E),
            fixed(rows, D),
            fixed(n_far, D),
            fixed(2 * D + E, D),
            fixed(D, D),
            fixed(D),
            fixed(D),
        ],
        out_specs=(tiled(kf * rows, D),) * 3 + (fixed(rows, D + 128),),
        cost=pl.CostEstimate(flops=16 * total * D * D, bytes_accessed=total * D * 8, transcendentals=2 * total * D),
    )(*read(place_col, edges, nodes), far_nodes, *read(msg_w1, msg_w2, msg_b1, msg_b2))

    def slope_of(pre):
        return call(
            slope_kernel,
            stored((total, D), bf16),
            grid=grid,
            in_specs=[flat],
            out_specs=flat,
            cost=pl.CostEstimate(flops=10 * total * D, bytes_accessed=total * D * 4, transcendentals=total * D),
        )(*read(pre))

    d1 = slope_of(pre1)
    sum_a, sum_b = shared_sum(act_sum, "nbr")
    sum_b = after(sum_b, d1)

    total_act, first_low, normed1, inv1, hidden, hidden_slope, normed2, inv2, counts, sent, send = call(
        node_forward_kernel,
        (
            stored((rows, D), bf16),
            stored((rows, D), bf16),
            stored((rows, D), f32),
            stored((rows, 1), f32),
            stored((rows, FF), bf16),
            stored((rows, FF), bf16),
            stored((rows, D), f32),
            stored((rows, 1), f32),
            stored((rows, 128), f32),
            stored((rows, D), bf16),
            shape((n_far, D), bf16),
        ),
    )(sum_a, sum_b, nodes, mask_row, wanted, msg_w3, ffn_w1, ffn_w2,
      msg_b3, norm1_gain, norm1_bias, ffn_b1, ffn_b2, norm2_gain, norm2_bias)
    d2 = slope_of(after(pre2, send))
    far_sent = after(exchange(send, blocks), d2)

    first_rows, second_rows = (2 * D + E) // parts, E // parts
    edge_rows = up_to(first_rows + 2 * second_rows + 16, 32) // 2
    edges_out, base, own_sum, far_sum, local_sum, *edge_sums = call(
        edge_kernel,
        (
            shape((kn, rows, E), bf16),
            stored((total, E), bf16),
            stored((rows, E), bf16),
            stored((n_far, E), bf16),
            stored((rows, E), bf16),
            stored((E, E), f32),
            stored((E, E), f32),
            stored((E, E), f32),
            stored((16, E), f32),
        ),
        scratch=[
            pltpu.VMEM((width, E), bf16),
            pltpu.VMEM((rows, E), f32),
            pltpu.VMEM((width, E), f32),
            pltpu.VMEM((rows, E), f32),
        ],
        grid=grid,
        in_specs=[
            fixed(SLOT, rows),
            fixed(rows, SLOT),
            edge_tile,
            edge_tile,
            fixed(rows, D),
            fixed(n_far, D),
            fixed(E, 2 * D + E),
            fixed(E, E),
            fixed(E, E),
        ]
        + [fixed(E)] * 5,
        out_specs=(
            edge_tile,
            flat_edge,
            fixed(rows, E),
            fixed(n_far, E),
            fixed(rows, E),
            fixed(E, E),
            fixed(E, E),
            fixed(E, E),
            fixed(16, E),
        ),
        cost=pl.CostEstimate(flops=16 * total * D * D, bytes_accessed=total * E * 12, transcendentals=2 * total * E),
    )(*read(place_row, place_col, edges, edge_cot, sent), far_sent, *read(edge_w1, edge_w2, edge_w3),
      *read(edge_b1, edge_b2, edge_b3, norm3_gain, norm3_bias))

    edge_packed = call(
        functools.partial(edge_weights_kernel, order),
        stored((parts, edge_rows, D), bf16),
        cost=pl.CostEstimate(flops=10**9, bytes_accessed=10**6, transcendentals=0),
    )(*read(sent, far_sent, own_sum, far_sum, local_sum, *edge_sums))
    far_back = after(exchange(far_sum, blocks), edge_packed)
    back = call(returned_kernel, shape((rows, 2 * E), bf16))(*read(own_sum, local_sum), far_back, wanted)
    for bit in nbr_bits[:-1]:
        back = add_low(back, swap(back, "nbr", bit))
    kept = fetched(
        counts, after(node_cot, back), normed2, edge_w1, ffn_w2, hidden_slope, ffn_w1, normed1, msg_w3, first_low, hidden, total_act,
        msg_w1, msg_w2, nodes, far_nodes
    )
    *kept, ready_w1, ready_w2, ready_nodes, ready_far = kept
    back_a, back_b = back, swap(back, "nbr", nbr_bits[-1])

    wide, narrow = FF // parts, D // parts
    node_rows = up_to(D + wide + narrow, 16 * blocks)
    mixed_grad, up, node_bias, node_packed = call(
        functools.partial(node_backward_kernel, parts),
        (
            shape((rows, D), f32),
            shape((rows, D), f32),
            shape((16, D), f32),
            shape((node_rows, D), bf16),
        ),
        in_specs=[smem] + [vmem] * 19,
    )(
        nbr_place, back_a, back_b, *kept, mask_row, inv1, inv2, norm1_gain, norm2_gain,
    )
    bits = bits_of("res")
    order_a, order_b = bits, bits[1:2] + bits[:1] + bits[2:]
    rows_ab = node_rows // 2
    part_a = halve([(node_packed, 0)], rows_ab, "res", order_a[0])
    part_b = halve([(node_packed, rows_ab)], rows_ab, "res", order_b[0])
    edge_packed = after(edge_packed, up)
    edge_part = scattered_sum(edge_packed.reshape(parts * edge_rows, D), "nbr", nbr_bits)

    msg_rows = first_rows + narrow + 16
    share_rows = up_to(msg_rows + edge_rows, max(64, 8 * blocks))
    edges_grad, own_sum, far_sum, local_sum, msg_kept, msg_given = call(
        functools.partial(message_backward_kernel, parts),
        (
            shape((kn, rows, E), f32),
            shape((rows, D), bf16),
            shape((n_far, D), bf16),
            shape((rows, D), bf16),
            shape((parts // 2, msg_rows, D), bf16),
            shape((parts // 2, msg_rows, D), bf16),
        ),
        scratch=[
            pltpu.VMEM((width, D), f32),
            pltpu.VMEM((E, D), f32),
            pltpu.VMEM((D, D), f32),
            pltpu.VMEM((16, D), f32),
            pltpu.VMEM((rows, D), f32),
            pltpu.VMEM((3 * D + E, D), bf16),
        ],
        grid=grid,
        in_specs=[
            smem,
            fixed(SLOT, rows),
            edge_tile,
            flat,
            flat,
            flat,
            fixed(rows, D),
            flat_edge,
            fixed(rows, D),
            fixed(n_far, D),
            fixed(2 * D + E, D),
            fixed(D, D),
            fixed(16, D),
        ],
        out_specs=(edge_tile, fixed(rows, D), fixed(n_far, D), fixed(rows, D))
        + (fixed(parts // 2, msg_rows, D),) * 2,
        cost=pl.CostEstimate(flops=16 * total * D * D, bytes_accessed=total * D * 10, transcendentals=0),
    )(nbr_place & 1, *read(place_row, edges, act1, d1, d2), up, *read(base), ready_nodes, ready_far, ready_w1, ready_w2, node_bias)

    far_sum, msg_kept, msg_given, part_a, part_b = held_together(far_sum, msg_kept, msg_given, part_a, part_b)
    flat_rows = parts // 2 * msg_rows
    msg_part = add_low(msg_kept, swap(msg_given, "nbr", 1)).reshape(flat_rows, D)
    part_a = halved_sum(total_of(part_a, rows_ab // 2), "res", order_a[1])
    part_b = halved_sum(total_of(part_b, rows_ab // 2), "res", order_b[1])
    middle, last = bits[2:-1], bits[-1]
    part_a = scattered_sum(part_a, "res", middle)
    part_b = scattered_sum(part_b, "res", middle)
    both = after(jnp.stack([part_a, part_b]), msg_part)
    msg_sum = scattered_sum(msg_part, "nbr", nbr_bits[1:])
    both = halved_sum(both, "res", last, 1)
    msg_sum = jnp.concatenate([msg_sum, edge_part, jnp.zeros((share_rows - msg_rows - edge_rows, D), bf16)], axis=0)
    msg_quarter = quarter_sum(msg_sum, "res", bits[:2])
    both = rejoined(after(both, msg_sum), "res", last, 1)
    far_back = exchange(after(far_sum, msg_sum), blocks)
    back = call(returned_last_kernel, shape((rows, D), bf16))(own_sum, local_sum, far_back, wanted, msg_w1)
    for bit in nbr_bits[:-1]:
        back = add_low(back, swap(back, "nbr", bit))
    back_b = swap(back, "nbr", nbr_bits[-1])
    msg_part = scattered_sum(msg_quarter, "res", middle)
    msg_part = add_low(msg_part, swap(msg_part, "res", last))
    part_a, part_b = both[0], both[1]
    part_a = rejoined(gathered_rows(part_a, "res", middle[::-1]), "res", order_a[1])
    part_b = rejoined(gathered_rows(part_b, "res", middle[::-1]), "res", order_b[1])
    part_a, part_b = after(part_a, msg_part), after(part_b, msg_part)
    other_a = swap(part_a, "res", order_a[0])
    other_b = swap(part_b, "res", order_b[0])
    msg_parts = quarters(gathered_rows(msg_part, "res", middle[::-1]), "res", bits[:2])

    def side(bit):
        return (lax.axis_index("res") // bit) & 1

    node_at = jnp.stack([side(order_a[0]), side(order_b[0])]).astype(jnp.int32)
    msg_at = jnp.stack([lax.axis_index("nbr"), 2 * side(bits[0]) + side(bits[1])]).astype(jnp.int32)
    nodes_grad, ffn_w1_grad, ffn_w2_grad, msg_w3_grad = call(
        functools.partial(node_weights_kernel, parts),
        (shape((rows, D), f32), shape((narrow, FF), f32), shape((wide, D), f32), shape((narrow, D), f32)),
        scratch=[pltpu.VMEM((node_rows, D), bf16)],
        in_specs=[smem] + [vmem] * 7,
    )(node_at, part_a, other_a, part_b, other_b, mixed_grad, back, back_b)
    (
        msg_w1_grad, msg_w2_grad, edge_w1_grad, edge_w2_grad, edge_w3_grad,
        edge_b1_grad, edge_b2_grad, edge_b3_grad, norm3_gain_grad, norm3_bias_grad,
        msg_b1_grad, msg_b2_grad, msg_b3_grad, norm1_gain_grad, norm1_bias_grad,
        ffn_b2_grad, norm2_gain_grad, norm2_bias_grad, ffn_b1_grad,
    ) = call(
        functools.partial(edge_message_weights_kernel, parts, edge_rows),
        (
            shape((first_rows, D), f32),
            shape((narrow, D), f32),
            shape((E, first_rows), f32),
            shape((second_rows, E), f32),
            shape((second_rows, E), f32),
        )
        + (shape((second_rows,), f32),) * 5
        + (shape((narrow,), f32),) * 8
        + (shape((wide,), f32),),
        scratch=[pltpu.VMEM((share_rows, D), bf16)],
        in_specs=[smem] + [vmem] * 4,
    )(msg_at, *msg_parts)
    return (
        sent,
        edges_out.transpose(1, 0, 2),
        nodes_grad,
        edges_grad.transpose(1, 0, 2),
        msg_w1_grad,
        msg_b1_grad,
        msg_w2_grad,
        msg_b2_grad,
        msg_w3_grad,
        msg_b3_grad,
        norm1_gain_grad,
        norm1_bias_grad,
        ffn_w1_grad,
        ffn_b1_grad,
        ffn_w2_grad,
        ffn_b2_grad,
        norm2_gain_grad,
        norm2_bias_grad,
        edge_w1_grad.T,
        edge_b1_grad,
        edge_w2_grad,
        edge_b2_grad,
        edge_w3_grad,
        edge_b3_grad,
        norm3_gain_grad,
        norm3_bias_grad,
    )


def solution(mesh):
    every = P()
    in_specs = (
        (P("res", None), P("res", "nbr", None), P("res", "nbr"), P("res"))
        + (every,) * 22
        + (P("res", None), P("res", "nbr", None))
    )
    matrix, vector = P("nbr", None), P("nbr")
    out_specs = (
        (P("res", None), P("res", "nbr", None), P("res", None), P("res", "nbr", None))
        + (matrix, vector) * 3
        + (vector, vector, matrix, vector, matrix, vector, vector, vector)
        + (matrix, vector) * 3
        + (vector, vector)
    )
    return jax.shard_map(on_device, mesh=mesh, in_specs=in_specs, out_specs=out_specs, check_vma=False)
```
